32 devices in a mesh: dp: 8 (over z, core), expert: 4 (over y, x).
Axes of the slice: x: 2, y: 2, z: 4, core: 2. Of those that a mesh axis runs over, the one named last changes fastest.
Arguments:
- tokens: bfloat16 [4096, 1536], P(('dp', 'expert')), may hold values from -6 to 6
- cotangent: bfloat16 [4096, 1536], P(('dp', 'expert')), may hold values from -6 to 6
- lengths: int32 [8, 3], P('dp'), may hold values from 1 to 256, 512 in all within a row
- routes: int32 [4096, 6], P(('dp', 'expert')), may hold values from 0 to 15, all different within a row; in each aligned block of 128 rows (0 to 127, 128 to 255, ...) at most 64 rows name the same one
- w_in: float32 [1536, 6448], P(('dp', 'expert')), may hold values from -0.15625 to 0.15625
- w_in_first: float32 [1536, 6448], P(('dp', 'expert'))
- w_in_second: float32 [1536, 6448], P(('dp', 'expert')), as said below
- w_out: float32 [3072, 1536], P(('dp', 'expert')), may hold values from -0.109375 to 0.109375
- w_out_first: float32 [3072, 1536], P(('dp', 'expert'))
- w_out_second: float32 [3072, 1536], P(('dp', 'expert')), as said below
- w_router: float32 [1536, 16], P(('dp', 'expert'))
- w_router_first: float32 [1536, 16], P(('dp', 'expert'))
- w_router_second: float32 [1536, 16], P(('dp', 'expert')), as said below
- w_shared_gu: float32 [1536, 2048], P(('dp', 'expert')), may hold values from -0.15625 to 0.15625
- w_shared_gu_first: float32 [1536, 2048], P(('dp', 'expert'))
- w_shared_gu_second: float32 [1536, 2048], P(('dp', 'expert')), as said below
- w_shared_down: float32 [1024, 1536], P(('dp', 'expert')), may hold values from -0.1875 to 0.1875
- w_shared_down_first: float32 [1024, 1536], P(('dp', 'expert'))
- w_shared_down_second: float32 [1024, 1536], P(('dp', 'expert')), as said below
- w_expert_gu: float32 [16, 1536, 1024], P('expert', 'dp'), may hold values from -0.3125 to 0.3125
- w_expert_gu_first: float32 [16, 1536, 1024], P('expert', 'dp')
- w_expert_gu_second: float32 [16, 1536, 1024], P('expert', 'dp'), as said below
- w_expert_down: float32 [16, 512, 1536], P('expert', 'dp'), may hold values from -0.25 to 0.25
- w_expert_down_first: float32 [16, 512, 1536], P('expert', 'dp')
- w_expert_down_second: float32 [16, 512, 1536], P('expert', 'dp'), as said below
- norm_gains: float32 [2, 1536], replicated, may hold values from 0.5 to 1.5
- norm_gains_first: float32 [2, 1536], replicated
- norm_gains_second: float32 [2, 1536], replicated, as said below
- conv_params: float32 [5, 3328], replicated, may hold values from -0.5 to 0.5
- conv_params_first: float32 [5, 3328], replicated
- conv_params_second: float32 [5, 3328], replicated, as said below
- head_params: float32 [3, 48], replicated, may hold values from -4.5 to 1.5
- head_params_first: float32 [3, 48], replicated
- head_params_second: float32 [3, 48], replicated, as said below
- mixer_gain: float32 [3072], replicated, may hold values from 0.5 to 1.5
- mixer_gain_first: float32 [3072], replicated
- mixer_gain_second: float32 [3072], replicated, as said below
Outputs:
- output: bfloat16 [4096, 1536], P(('dp', 'expert'))
- grad_tokens: bfloat16 [4096, 1536], P(('dp', 'expert'))
- grad_w_in: float32 [1536, 6448], P(('dp', 'expert'))
- new_w_in: float32 [1536, 6448], P(('dp', 'expert'))
- new_w_in_first: float32 [1536, 6448], P(('dp', 'expert'))
- new_w_in_second: float32 [1536, 6448], P(('dp', 'expert'))
- grad_w_out: float32 [3072, 1536], P(('dp', 'expert'))
- new_w_out: float32 [3072, 1536], P(('dp', 'expert'))
- new_w_out_first: float32 [3072, 1536], P(('dp', 'expert'))
- new_w_out_second: float32 [3072, 1536], P(('dp', 'expert'))
- grad_w_router: float32 [1536, 16], P(('dp', 'expert'))
- new_w_router: float32 [1536, 16], P(('dp', 'expert'))
- new_w_router_first: float32 [1536, 16], P(('dp', 'expert'))
- new_w_router_second: float32 [1536, 16], P(('dp', 'expert'))
- grad_w_shared_gu: float32 [1536, 2048], P(('dp', 'expert'))
- new_w_shared_gu: float32 [1536, 2048], P(('dp', 'expert'))
- new_w_shared_gu_first: float32 [1536, 2048], P(('dp', 'expert'))
- new_w_shared_gu_second: float32 [1536, 2048], P(('dp', 'expert'))
- grad_w_shared_down: float32 [1024, 1536], P(('dp', 'expert'))
- new_w_shared_down: float32 [1024, 1536], P(('dp', 'expert'))
- new_w_shared_down_first: float32 [1024, 1536], P(('dp', 'expert'))
- new_w_shared_down_second: float32 [1024, 1536], P(('dp', 'expert'))
- grad_w_expert_gu: float32 [16, 1536, 1024], P('expert', 'dp')
- new_w_expert_gu: float32 [16, 1536, 1024], P('expert', 'dp')
- new_w_expert_gu_first: float32 [16, 1536, 1024], P('expert', 'dp')
- new_w_expert_gu_second: float32 [16, 1536, 1024], P('expert', 'dp')
- grad_w_expert_down: float32 [16, 512, 1536], P('expert', 'dp')
- new_w_expert_down: float32 [16, 512, 1536], P('expert', 'dp')
- new_w_expert_down_first: float32 [16, 512, 1536], P('expert', 'dp')
- new_w_expert_down_second: float32 [16, 512, 1536], P('expert', 'dp')
- grad_norm_gains: float32 [2, 1536], replicated
- change_norm_gains: float32 [2, 1536], replicated
- new_norm_gains_first: float32 [2, 1536], replicated
- new_norm_gains_second: float32 [2, 1536], replicated
- grad_conv_params: float32 [5, 3328], replicated
- change_conv_params: float32 [5, 3328], replicated
- new_conv_params_first: float32 [5, 3328], replicated
- new_conv_params_second: float32 [5, 3328], replicated
- grad_head_params: float32 [3, 48], replicated
- change_head_params: float32 [3, 48], replicated
- new_head_params_first: float32 [3, 48], replicated
- new_head_params_second: float32 [3, 48], replicated
- grad_mixer_gain: float32 [3072], replicated
- change_mixer_gain: float32 [3072], replicated
- new_mixer_gain_first: float32 [3072], replicated
- new_mixer_gain_second: float32 [3072], replicated
The draws below stay inside these ranges and needn't reach their ends.
Inputs may be any that keep to these rules, and one draw needn't show every extreme that they name: `lengths`: each row lists one sequence's documents in order; they cover its 512 tokens. `routes`: the 6 ids of a row differ; among the 128 rows of one device no expert is named more than 64 times. `w_in_second`: positive. `w_out_second`: positive. `w_router_second`: positive. `w_shared_gu_second`: positive. `w_shared_down_second`: positive. `w_expert_gu_second`: positive. `w_expert_down_second`: positive. `norm_gains_second`: positive. `conv_params_second`: positive. `head_params_second`: positive. `mixer_gain_second`: positive.
All inputs are finite; a program needn't handle non-finite values.
Results may differ from the reference program's by a relative error of at most 0.029.
Values may be sent and summed in bfloat16 or wider, within the bound.
A program may use at most 640 MiB of HBM per device.

```python
import math
from functools import partial
import jax
import jax.numpy as jnp
import numpy as np
from jax import lax

D = 1536
HEADS = 48
HEAD_DIM = 64
STATE = 128
CONV = 4
EXPERT_FF = 512
SHARED_FF = 1024
TOPK = 6
TOK_DEV = 128
STEP = 3
INNER = 3072
CONV_DIM = 3328
IN_COLS = 6448
EXPERTS = 16
LEN = 512
SEQS = 8
TOKENS = 4096
DOCS = 3
DOCMAX = 256
CAP = 64
N_EXPERT = 4


def draw_head_params(key, part):
    lower_ends = jnp.array([-3.5, -4.5, 0.5], jnp.float32)[:, None]
    upper_ends = jnp.array([0.7, -3.0, 1.5], jnp.float32)[:, None]
    uniform_draw = jax.random.uniform(jax.random.fold_in(key, 11), (3, HEADS), jnp.float32)
    return lower_ends + (upper_ends - lower_ends) * uniform_draw


def draw_w_router(key, part):
    base_part = jax.random.normal(jax.random.fold_in(key, 21), (D, EXPERTS), jnp.float32)
    column_scale = jnp.exp(jax.random.uniform(jax.random.fold_in(key, 22), (1, EXPERTS), jnp.float32, 0.0, 0.3))
    return base_part * (0.45 / math.sqrt(D)) * column_scale


def first_moment(key, shape, grad_size):
    base_part = jax.random.normal(jax.random.fold_in(key, 31), shape, jnp.float32)
    return base_part * (0.11 * grad_size)


def second_moment(key, shape, grad_size):
    factor = jnp.exp(jax.random.uniform(jax.random.fold_in(key, 41), shape, jnp.float32, 0.0, math.log(4.0)))
    return factor * (0.053 * grad_size * grad_size)


def size_in():
    return math.sqrt(TOKENS)


def size_out():
    return 1.5 * math.sqrt(TOKENS)


def size_router():
    return 0.3 * math.sqrt(D * TOPK * TOKENS / EXPERTS)


def size_shared_gu():
    return 0.7 * math.sqrt(TOKENS)


def size_shared_down():
    return 0.6 * math.sqrt(TOKENS)


def size_expert_gu():
    return 0.25 * math.sqrt(TOPK * TOKENS / EXPERTS)


def size_expert_down():
    return 0.3 * math.sqrt(TOPK * TOKENS / EXPERTS)


def size_small():
    return math.sqrt(TOKENS)


def draw_w_in_first(key, part):
    return first_moment(key, (D, IN_COLS), size_in())


def draw_w_in_second(key, part):
    return second_moment(key, (D, IN_COLS), size_in())


def draw_w_out_first(key, part):
    return first_moment(key, (INNER, D), size_out())


def draw_w_out_second(key, part):
    return second_moment(key, (INNER, D), size_out())


def draw_w_router_first(key, part):
    return first_moment(key, (D, EXPERTS), size_router())


def draw_w_router_second(key, part):
    return second_moment(key, (D, EXPERTS), size_router())


def draw_w_shared_gu_first(key, part):
    return first_moment(key, (D, 2 * SHARED_FF), size_shared_gu())


def draw_w_shared_gu_second(key, part):
    return second_moment(key, (D, 2 * SHARED_FF), size_shared_gu())


def draw_w_shared_down_first(key, part):
    return first_moment(key, (SHARED_FF, D), size_shared_down())


def draw_w_shared_down_second(key, part):
    return second_moment(key, (SHARED_FF, D), size_shared_down())


def draw_w_expert_gu_first(key, part):
    return first_moment(key, (EXPERTS, D, 2 * EXPERT_FF), size_expert_gu())


def draw_w_expert_gu_second(key, part):
    return second_moment(key, (EXPERTS, D, 2 * EXPERT_FF), size_expert_gu())


def draw_w_expert_down_first(key, part):
    return first_moment(key, (EXPERTS, EXPERT_FF, D), size_expert_down())


def draw_w_expert_down_second(key, part):
    return second_moment(key, (EXPERTS, EXPERT_FF, D), size_expert_down())


def draw_norm_gains_first(key, part):
    return first_moment(key, (2, D), size_small())


def draw_norm_gains_second(key, part):
    return second_moment(key, (2, D), size_small())


def draw_conv_params_first(key, part):
    return first_moment(key, (CONV + 1, CONV_DIM), size_small())


def draw_conv_params_second(key, part):
    return second_moment(key, (CONV + 1, CONV_DIM), size_small())


def draw_head_params_first(key, part):
    return first_moment(key, (3, HEADS), size_small())


def draw_head_params_second(key, part):
    return second_moment(key, (3, HEADS), size_small())


def draw_mixer_gain_first(key, part):
    return first_moment(key, (INNER,), size_small())


def draw_mixer_gain_second(key, part):
    return second_moment(key, (INNER,), size_small())


def levels(rng, shape, split, least, top_value):
    loudness, own = 1.0, jax.random.fold_in(rng, 6)
    for position, parts in split:
        heights = jnp.exp(jax.random.uniform(jax.random.fold_in(own, position), (parts,), jnp.float32, least / len(split), top_value / len(split)))
        loudness = loudness * jnp.repeat(heights, shape[position] // parts).reshape([-1 if axis == position else 1 for axis in range(len(shape))])
    return loudness


def split_up(amount, total, reach, slope):
    weights = [(1 << 20) // math.isqrt(rank ** slope) + 1 for rank in range(2, amount + 1)]
    spare, given = total - reach - (amount - 1), [1] * (amount - 1)
    while spare > 0:
        movable = [i for i in range(amount - 1) if given[i] < reach]
        pool, budget = sum([weights[i] for i in movable]), spare
        for i in movable:
            extra = min(reach - given[i], max(1, budget * weights[i] // pool), spare)
            given[i] = given[i] + extra
            spare = spare - extra
    return np.array([reach] + given)


def uneven_parts(own_key, number_of, total, limit, slope):
    if number_of == 2:
        one = jax.random.randint(own_key, (), max(1, total - limit), min(limit, total - 1) + 1)
        return jnp.stack([one, total - one])
    sizes = jnp.asarray(split_up(number_of, total, limit, slope), jnp.int32)
    couples = (number_of - 1) // 2
    donor, receiver = sizes[1:1 + 2 * couples:2], sizes[2:2 + 2 * couples:2]
    slack = jnp.minimum(donor - 1, limit - receiver)
    moved = jax.random.randint(jax.random.fold_in(own_key, 1), (couples,), 0, 1 << 20) % (slack + 1)
    sizes = sizes.at[1:1 + 2 * couples:2].set(donor - moved).at[2:2 + 2 * couples:2].set(receiver + moved)
    return sizes[jax.random.permutation(jax.random.fold_in(own_key, 2), number_of)]


def assign_block(rng, own, number, rows, number_of, top, most, skew):
    ranking = jax.random.permutation(rng, number_of)
    heavy_load, common = load_shares(number_of, rows * top, most, skew, True), load_shares(number_of, rows * top, most, skew, False)
    places = jnp.arange(number_of)

    def named(sizes, rotation):
        used = int((sizes > 0).sum())
        fixed = max(1, used // 4)
        moved = fixed + (places - fixed + rotation * (used - fixed)) % max(1, number_of - fixed)
        return jnp.zeros((number_of,), jnp.int32).at[ranking[jnp.where(places < fixed, places, moved)]].set(jnp.asarray(sizes, jnp.int32))

    sizes = jnp.where(number % 4 == 0, named(heavy_load, number // 4), named(common, number - number // 4 - 1))
    mixed = jax.random.permutation(jax.random.fold_in(own, 3), number_of)
    source_of, taker = mixed[0:number_of // 2 * 2:2], mixed[1:number_of // 2 * 2:2]
    slack = jnp.minimum(sizes[source_of] - 1, most - sizes[taker]) // 2
    slack = jnp.where((source_of == ranking[0]) | (taker == ranking[0]) | (sizes[taker] == 0), 0, jnp.maximum(slack, 0))
    moved = jax.random.randint(jax.random.fold_in(own, 4), (number_of // 2,), 0, 1 << 20) % (slack + 1)
    sizes = sizes.at[source_of].add(-moved).at[taker].add(moved)
    items = jnp.searchsorted(jnp.cumsum(sizes), jnp.arange(rows * top), side="right").astype(jnp.int32)
    grid = items.reshape(top, rows).T
    grid = grid[jax.random.permutation(jax.random.fold_in(own, 1), rows)]
    rotation = jax.random.randint(jax.random.fold_in(own, 2), (rows, 1), 0, top)
    return jnp.take_along_axis(grid, (jnp.arange(top)[None, :] + rotation) % top, axis=1)


def load_shares(amount, total, bound, skew, full):
    portions = [(1 << 20) // math.isqrt(grade ** skew) + 1 for grade in range(1, amount + 1)]
    largest = bound if full else min(bound, max(-(-total // amount), total * portions[0] // sum(portions)))
    least = 1 if total - largest >= amount - 1 else 0
    holding, rest = [largest] + [least] * (amount - 1), total - largest - least * (amount - 1)
    while rest > 0:
        candidates = [i for i in range(1, amount) if holding[i] < largest] or [i for i in range(1, amount) if holding[i] < bound]
        mass, remaining = sum([portions[i] for i in candidates]), rest
        for i in candidates:
            more = min(bound - holding[i], max(1, remaining * portions[i] // mass), rest)
            holding[i] = holding[i] + more
            rest = rest - more
    return np.array(holding)


def noise(own_key, shape, scale, bound, split=(), kind=jnp.bfloat16):
    factor_of = levels(own_key, shape, split, -0.22, 0.18) if split else 1.0
    drawn = jax.random.normal(own_key, shape, jnp.float32) * scale * factor_of
    return jnp.minimum(jnp.maximum(drawn, -bound), bound).astype(kind)


def setup_inputs(seed: int = 0) -> dict:
    seeds = jax.random.split(jax.random.key(seed), 38)
    tokens = noise(seeds[0], (TOKENS, D), 1.0, 6.0, ((0, 32),))
    cotangent = noise(seeds[1], (TOKENS, D), 1.0, 6.0, ((0, 32),))
    lengths = jax.vmap(lambda own: uneven_parts(own, DOCS, LEN, DOCMAX, 2))(jax.random.split(seeds[2], SEQS)).reshape((SEQS, DOCS)).astype(jnp.int32)
    routes_keys = jax.random.split(jax.random.fold_in(seeds[3], 1), TOKENS // TOK_DEV)
    routes_turns = jax.random.permutation(jax.random.fold_in(seeds[3], 3), TOKENS // TOK_DEV)
    routes = jax.vmap(lambda own, number: assign_block(jax.random.fold_in(seeds[3], 2), own, number, TOK_DEV, EXPERTS, TOPK, CAP, 2))(routes_keys, routes_turns).reshape((TOKENS, TOPK))
    w_in = noise(seeds[4], (D, IN_COLS), D ** -0.5, 0.15625, ((0, 32),), jnp.float32)
    w_in_first = draw_w_in_first(jax.random.fold_in(seeds[37], 71), 0)
    w_in_second = draw_w_in_second(jax.random.fold_in(seeds[37], 71), 0)
    w_out = noise(seeds[7], (INNER, D), INNER ** -0.5, 0.109375, ((0, 32),), jnp.float32)
    w_out_first = draw_w_out_first(jax.random.fold_in(seeds[37], 71), 0)
    w_out_second = draw_w_out_second(jax.random.fold_in(seeds[37], 71), 0)
    w_router = draw_w_router(jax.random.fold_in(seeds[37], 71), 0)
    w_router_first = draw_w_router_first(jax.random.fold_in(seeds[37], 71), 0)
    w_router_second = draw_w_router_second(jax.random.fold_in(seeds[37], 71), 0)
    w_shared_gu = noise(seeds[13], (D, 2 * SHARED_FF), D ** -0.5, 0.15625, ((0, 32),), jnp.float32)
    w_shared_gu_first = draw_w_shared_gu_first(jax.random.fold_in(seeds[37], 71), 0)
    w_shared_gu_second = draw_w_shared_gu_second(jax.random.fold_in(seeds[37], 71), 0)
    w_shared_down = noise(seeds[16], (SHARED_FF, D), SHARED_FF ** -0.5, 0.1875, ((0, 32),), jnp.float32)
    w_shared_down_first = draw_w_shared_down_first(jax.random.fold_in(seeds[37], 71), 0)
    w_shared_down_second = draw_w_shared_down_second(jax.random.fold_in(seeds[37], 71), 0)
    w_expert_gu = noise(seeds[19], (EXPERTS, D, 2 * EXPERT_FF), (D // 4) ** -0.5, 0.3125, ((0, 4), (1, 8)), jnp.float32)
    w_expert_gu_first = draw_w_expert_gu_first(jax.random.fold_in(seeds[37], 71), 0)
    w_expert_gu_second = draw_w_expert_gu_second(jax.random.fold_in(seeds[37], 71), 0)
    w_expert_down = noise(seeds[22], (EXPERTS, EXPERT_FF, D), EXPERT_FF ** -0.5, 0.25, ((0, 4), (1, 8)), jnp.float32)
    w_expert_down_first = draw_w_expert_down_first(jax.random.fold_in(seeds[37], 71), 0)
    w_expert_down_second = draw_w_expert_down_second(jax.random.fold_in(seeds[37], 71), 0)
    norm_gains = jnp.clip(1.0 + 0.1 * jax.random.normal(seeds[25], (2, D), jnp.float32), 0.5, 1.5)
    norm_gains_first = draw_norm_gains_first(jax.random.fold_in(seeds[37], 71), 0)
    norm_gains_second = draw_norm_gains_second(jax.random.fold_in(seeds[37], 71), 0)
    conv_params = jnp.clip(jax.random.uniform(seeds[28], (CONV + 1, CONV_DIM), jnp.float32, -0.5, 0.5), -0.5, 0.5)
    conv_params_first = draw_conv_params_first(jax.random.fold_in(seeds[37], 71), 0)
    conv_params_second = draw_conv_params_second(jax.random.fold_in(seeds[37], 71), 0)
    head_params = draw_head_params(jax.random.fold_in(seeds[37], 71), 0)
    head_params_first = draw_head_params_first(jax.random.fold_in(seeds[37], 71), 0)
    head_params_second = draw_head_params_second(jax.random.fold_in(seeds[37], 71), 0)
    mixer_gain = jnp.clip(1.0 + 0.1 * jax.random.normal(seeds[34], (INNER,), jnp.float32), 0.5, 1.5)
    mixer_gain_first = draw_mixer_gain_first(jax.random.fold_in(seeds[37], 71), 0)
    mixer_gain_second = draw_mixer_gain_second(jax.random.fold_in(seeds[37], 71), 0)
    return dict(tokens=tokens, cotangent=cotangent, lengths=lengths, routes=routes, w_in=w_in, w_in_first=w_in_first, w_in_second=w_in_second, w_out=w_out, w_out_first=w_out_first, w_out_second=w_out_second, w_router=w_router, w_router_first=w_router_first, w_router_second=w_router_second, w_shared_gu=w_shared_gu, w_shared_gu_first=w_shared_gu_first, w_shared_gu_second=w_shared_gu_second, w_shared_down=w_shared_down, w_shared_down_first=w_shared_down_first, w_shared_down_second=w_shared_down_second, w_expert_gu=w_expert_gu, w_expert_gu_first=w_expert_gu_first, w_expert_gu_second=w_expert_gu_second, w_expert_down=w_expert_down, w_expert_down_first=w_expert_down_first, w_expert_down_second=w_expert_down_second, norm_gains=norm_gains, norm_gains_first=norm_gains_first, norm_gains_second=norm_gains_second, conv_params=conv_params, conv_params_first=conv_params_first, conv_params_second=conv_params_second, head_params=head_params, head_params_first=head_params_first, head_params_second=head_params_second, mixer_gain=mixer_gain, mixer_gain_first=mixer_gain_first, mixer_gain_second=mixer_gain_second)


@jax.custom_vjp
def low(v):
    return lax.optimization_barrier(v.astype(jnp.bfloat16)).astype(jnp.float32)

@jax.custom_vjp
def low_back(v):
    return v

def low_keep(v):
    return (low(v), None)

def low_pass(kept, grad):
    return (grad,)

def back_keep(v):
    return (v, None)

def back_low(kept, grad):
    return (low(grad),)
low.defvjp(low_keep, low_pass)
low_back.defvjp(back_keep, back_low)
norm_eps = 1e-05
beta_one = 0.9
beta_two = 0.95
adam_eps = 1e-08
learn_rate = 0.02
decay_rate = 0.1
highest = lax.Precision.HIGHEST

def matmul(left, right):
    return jnp.dot(left, right, precision=highest, preferred_element_type=jnp.float32)

def rms_scale(values):
    return lax.rsqrt(lax.optimization_barrier(jnp.mean(values * values, axis=-1, keepdims=True)) + norm_eps)

def doc_ids(lengths_row, positions):
    starts = (jnp.cumsum(lengths_row) - lengths_row).astype(jnp.int32)
    return (lax.optimization_barrier(jnp.sum((starts[None, :] <= positions[:, None]).astype(jnp.int32), axis=1)) - 1).astype(jnp.int32)

def causal_conv(extended, conv_params, doc_ext, doc_index):
    length = doc_index.shape[0]
    summed = jnp.zeros_like(extended[CONV - 1:]) + conv_params[CONV]
    for offset in range(CONV):
        start_row = CONV - 1 - offset
        usable = (doc_ext[start_row:start_row + length] == doc_index).astype(extended.dtype)
        summed = summed + conv_params[offset] * extended[start_row:start_row + length] * usable[:, None]
    return summed

def ssd_state(values, b_rows, dt_step, log_decay, doc_index):
    cumulated = jnp.cumsum(log_decay, axis=0)
    tail_weight = jnp.exp(cumulated[-1][None, :] - cumulated) * (doc_index == doc_index[-1]).astype(cumulated.dtype)[:, None]
    scaled = values * (dt_step * tail_weight)[:, :, None]
    return jnp.einsum('shp,sn->hpn', scaled, b_rows, precision=highest)

def ssd_carry(log_decay, doc_index, prior_doc):
    cumulated = jnp.cumsum(log_decay, axis=0)
    return jnp.exp(cumulated[-1]) * (doc_index[-1] == prior_doc).astype(cumulated.dtype)

def ssd_output(values, b_rows, c_rows, dt_step, log_decay, doc_index, prior_doc, state_in):
    length = values.shape[0]
    cumulated = jnp.cumsum(log_decay, axis=0)
    places = jnp.arange(length, dtype=jnp.int32)
    usable = (doc_index[:, None] == doc_index[None, :]) & (places[:, None] >= places[None, :])
    spread = cumulated.T[:, :, None] - cumulated.T[:, None, :]
    masked = jnp.exp(jnp.where(usable[None], spread, 0.0)) * usable[None].astype(cumulated.dtype)
    scores = jnp.dot(c_rows, b_rows.T, precision=highest)
    within = jnp.einsum('hts,shp->thp', masked * scores[None], values * dt_step[:, :, None], precision=highest)
    inflow = jnp.exp(cumulated) * (doc_index == prior_doc).astype(cumulated.dtype)[:, None]
    carried = jnp.einsum('hpn,tn->thp', state_in, c_rows, precision=highest)
    return within + inflow[:, :, None] * carried

def route_slots(routes_blk, experts, capacity):
    flat_ids = routes_blk.reshape(-1)
    route_count = flat_ids.shape[0]
    onehot = (flat_ids[:, None] == jnp.arange(experts, dtype=jnp.int32)[None, :]).astype(jnp.int32)
    earlier = (jnp.cumsum(onehot, axis=0) - onehot).astype(jnp.int32)
    slot_ids = lax.optimization_barrier(jnp.sum(earlier * onehot, axis=1)).astype(jnp.int32)
    route_index = (flat_ids * capacity + slot_ids).astype(jnp.int32)
    slot_table = jnp.full((experts * capacity,), route_count, jnp.int32).at[route_index].set(jnp.arange(route_count, dtype=jnp.int32))
    return (route_index, slot_table)

def adam_step(weight, moment_one, moment_two, gradient):
    moment_one = beta_one * moment_one + (1.0 - beta_one) * gradient
    moment_two = beta_two * moment_two + (1.0 - beta_two) * gradient * gradient
    fixed_one = 1.0 - beta_one ** STEP
    fixed_two = 1.0 - beta_two ** STEP
    change = moment_one / fixed_one / (jnp.sqrt(moment_two / fixed_two) + adam_eps) + decay_rate * weight
    moved = -learn_rate * change
    return (gradient, weight + moved, moment_one, moment_two, moved)

def expert_block(w_expert_gu, w_expert_down, piece):
    rows_blk, weights_blk, routes_blk = piece
    route_index, slot_table = route_slots(routes_blk, EXPERTS, CAP)
    tok_index = slot_table // TOPK
    padded = jnp.concatenate([rows_blk, jnp.zeros((1, D), rows_blk.dtype)], axis=0)
    slot_in = low_back(padded[tok_index]).reshape(EXPERTS, CAP, D)
    gate_up = low_back(jnp.einsum('ecd,edf->ecf', slot_in, w_expert_gu, precision=highest))
    middle = low(jax.nn.silu(gate_up[..., :EXPERT_FF]) * gate_up[..., EXPERT_FF:])
    slot_out = low_back(low(jnp.einsum('ecf,efd->ecd', middle, w_expert_down, precision=highest))).reshape(EXPERTS * CAP, D)
    chosen = slot_out[route_index].reshape(TOK_DEV, TOPK, D)
    return jnp.einsum('tk,tkd->td', weights_blk, chosen, precision=highest)

def sequence_layer(params, piece):
    w_in, w_out, w_router, w_shared_gu, w_shared_down, w_expert_gu, w_expert_down, norm_gains, conv_params, head_params, mixer_gain = params
    x_seq, lengths_row, routes_seq = piece
    length = x_seq.shape[0]

    def to_blocks(array):
        return array.reshape((N_EXPERT, TOK_DEV) + array.shape[1:])
    doc_index = doc_ids(lengths_row, jnp.arange(length, dtype=jnp.int32))
    normed = low(x_seq * rms_scale(x_seq) * norm_gains[0])
    projected = matmul(normed, w_in)
    split_at = 2 * INNER + 2 * STATE
    packed = low_back(low(projected[:, :split_at]))
    dt_raw = low_back(projected[:, split_at:])
    gate_z = packed[:, :INNER]
    conv_in = packed[:, INNER:]
    extended = jnp.concatenate([jnp.zeros((CONV - 1, CONV_DIM), conv_in.dtype), conv_in], axis=0)
    doc_ext = jnp.concatenate([jnp.full((CONV - 1,), -1, jnp.int32), doc_index])
    mixed_in = jax.nn.silu(causal_conv(extended, conv_params, doc_ext, doc_index))
    values = mixed_in[:, :INNER].reshape(length, HEADS, HEAD_DIM)
    b_rows = mixed_in[:, INNER:INNER + STATE]
    c_rows = mixed_in[:, INNER + STATE:]
    dt_step = jax.nn.softplus(dt_raw + head_params[1])
    log_decay = -jnp.exp(head_params[0]) * dt_step
    prior_all = jnp.concatenate([jnp.full((1,), -1, jnp.int32), doc_index[:-1]])

    def ssd_block(state_in, blocks):
        vals_blk, b_blk, c_blk, step_blk, decay_blk, doc_blk, prior_doc = blocks
        result = ssd_output(vals_blk, b_blk, c_blk, step_blk, decay_blk, doc_blk, prior_doc, state_in)
        state_next = ssd_carry(decay_blk, doc_blk, prior_doc)[:, None, None] * state_in + ssd_state(vals_blk, b_blk, step_blk, decay_blk, doc_blk)
        return (state_next, result)
    blocks_in = (to_blocks(values), to_blocks(b_rows), to_blocks(c_rows), to_blocks(dt_step), to_blocks(log_decay), to_blocks(doc_index), to_blocks(prior_all)[:, 0])
    state_zero = jnp.zeros((HEADS, HEAD_DIM, STATE), values.dtype)
    unused_state, ssd_out = lax.scan(jax.checkpoint(ssd_block), state_zero, blocks_in)
    ssd_out = ssd_out.reshape(length, HEADS, HEAD_DIM)
    full_y = (ssd_out + head_params[2][None, :, None] * values).reshape(length, INNER)
    gated_y = full_y * jax.nn.silu(gate_z)
    mixer_act = low(gated_y * rms_scale(gated_y) * mixer_gain)
    mixer_res = low_back(matmul(mixer_act, w_out))
    hidden = x_seq + mixer_res
    normed_two = low(hidden * rms_scale(hidden) * norm_gains[1])
    logits = low_back(matmul(normed_two, w_router))
    picked = jnp.take_along_axis(logits, routes_seq, axis=1)
    weights = jax.nn.softmax(picked, axis=-1)
    shared_gu = low_back(matmul(normed_two, w_shared_gu))
    shared_mid = low(jax.nn.silu(shared_gu[:, :SHARED_FF]) * shared_gu[:, SHARED_FF:])
    shared_out = matmul(shared_mid, w_shared_down)
    expert_out = lax.map(jax.checkpoint(partial(expert_block, w_expert_gu, w_expert_down)), (to_blocks(normed_two), to_blocks(weights), to_blocks(routes_seq)))
    return hidden + shared_out + expert_out.reshape(length, D)

def reference(tokens, cotangent, lengths, routes, w_in, w_in_first, w_in_second, w_out, w_out_first, w_out_second, w_router, w_router_first, w_router_second, w_shared_gu, w_shared_gu_first, w_shared_gu_second, w_shared_down, w_shared_down_first, w_shared_down_second, w_expert_gu, w_expert_gu_first, w_expert_gu_second, w_expert_down, w_expert_down_first, w_expert_down_second, norm_gains, norm_gains_first, norm_gains_second, conv_params, conv_params_first, conv_params_second, head_params, head_params_first, head_params_second, mixer_gain, mixer_gain_first, mixer_gain_second):
    masters = (w_in, w_out, w_router, w_shared_gu, w_shared_down, w_expert_gu, w_expert_down, norm_gains, conv_params, head_params, mixer_gain)
    firsts = (w_in_first, w_out_first, w_router_first, w_shared_gu_first, w_shared_down_first, w_expert_gu_first, w_expert_down_first, norm_gains_first, conv_params_first, head_params_first, mixer_gain_first)
    seconds = (w_in_second, w_out_second, w_router_second, w_shared_gu_second, w_shared_down_second, w_expert_gu_second, w_expert_down_second, norm_gains_second, conv_params_second, head_params_second, mixer_gain_second)

    def forward(inputs, params):
        rounded = tuple((low(master) for master in params[:7])) + tuple(params[7:])
        pieces = (inputs.reshape(SEQS, LEN, D), lengths, routes.reshape(SEQS, LEN, TOPK))
        outputs = lax.map(jax.checkpoint(partial(sequence_layer, rounded)), pieces)
        return outputs.reshape(TOKENS, D)
    result, pullback = jax.vjp(forward, tokens.astype(jnp.float32), masters)
    grad_in, grads = pullback(cotangent.astype(jnp.float32))
    updated = [adam_step(master, moment_one, moment_two, gradient) for master, moment_one, moment_two, gradient in zip(masters, firsts, seconds, grads)]
    return (result.astype(jnp.bfloat16), grad_in.astype(jnp.bfloat16), updated[0][0], updated[0][1], updated[0][2], updated[0][3], updated[1][0], updated[1][1], updated[1][2], updated[1][3], updated[2][0], updated[2][1], updated[2][2], updated[2][3], updated[3][0], updated[3][1], updated[3][2], updated[3][3], updated[4][0], updated[4][1], updated[4][2], updated[4][3], updated[5][0], updated[5][1], updated[5][2], updated[5][3], updated[6][0], updated[6][1], updated[6][2], updated[6][3], updated[7][0], updated[7][4], updated[7][2], updated[7][3], updated[8][0], updated[8][4], updated[8][2], updated[8][3], updated[9][0], updated[9][4], updated[9][2], updated[9][3], updated[10][0], updated[10][4], updated[10][2], updated[10][3])
```

```python
import jax
import jax.numpy as jnp
from jax import lax
from jax.sharding import PartitionSpec as P

D = 1536
HEADS = 48
HEAD_DIM = 64
STATE = 128
CONV = 4
EXPERT_FF = 512
SHARED_FF = 1024
STEP = 3
INNER = 3072
CONV_DIM = 3328
LANES = 128

norm_eps = 1e-05
beta_one = 0.9
beta_two = 0.95
adam_eps = 1e-08
learn_rate = 0.02
decay_rate = 0.1
highest = lax.Precision.HIGHEST
bf16 = jnp.bfloat16
f32 = jnp.float32


def dot(left, right):
    return jnp.dot(left, right, preferred_element_type=f32)


def dot_nt(left, right):
    return lax.dot_general(left, right, (((1,), (1,)), ((), ())), preferred_element_type=f32)


def dot_tn(left, right):
    return lax.dot_general(left, right, (((0,), (0,)), ((), ())), preferred_element_type=f32)


def swap(pieces, axis):
    return lax.all_to_all(pieces, axis, split_axis=0, concat_axis=0, tiled=True)


def spread(block, axis):
    count = lax.axis_size(axis)
    return swap(jnp.broadcast_to(block[None], (count,) + block.shape), axis)


def rms_scale(values):
    return lax.rsqrt(jnp.mean(values * values, axis=-1, keepdims=True) + norm_eps)


def silu_slope(values):
    sigmoid_value = jax.nn.sigmoid(values)
    return sigmoid_value * (1.0 + values * (1.0 - sigmoid_value))


def norm_back(grad_norm, unit_rows, scale_rows, gain):
    scaled = grad_norm * gain
    return scale_rows * (scaled - unit_rows * jnp.mean(scaled * unit_rows, axis=-1, keepdims=True))


def adam_step(weight, moment_one, moment_two, gradient):
    moment_one = beta_one * moment_one + (1.0 - beta_one) * gradient
    moment_two = beta_two * moment_two + (1.0 - beta_two) * gradient * gradient
    fixed_one = 1.0 - beta_one**STEP
    fixed_two = 1.0 - beta_two**STEP
    change = (
        moment_one / fixed_one / (jnp.sqrt(moment_two / fixed_two) + adam_eps) + decay_rate * weight
    )
    moved = -learn_rate * change
    return (gradient, weight + moved, moment_one, moment_two, moved)


def split_words(value):
    high = value.astype(bf16)
    rest = value - high.astype(f32)
    mid = rest.astype(bf16)
    low = (rest - mid.astype(f32)).astype(bf16)
    return high, mid, low


def join_words(words):
    return words[0].astype(f32) + words[1].astype(f32) + words[2].astype(f32)


def conv_taps(same_doc, length):
    return [same_doc[:, offset][:, None] for offset in range(CONV)]


def shifted(array, offset):
    if offset == 0:
        return array
    if offset > 0:
        return jnp.pad(array[:-offset], ((offset, 0), (0, 0)))
    return jnp.pad(array[-offset:], ((0, -offset), (0, 0)))


def ssd_forward(values, b_rows, c_rows, dt_step, cum, usable):
    heads = dt_step.shape[1]
    scores = dot_nt(c_rows.astype(bf16), b_rows.astype(bf16))
    diff = cum.T[:, :, None] - cum.T[:, None, :]
    decay = jnp.exp(jnp.where(usable[None], diff, -1e30))
    mixed = (decay * scores[None]).astype(bf16)
    scaled = (values.reshape(-1, heads, HEAD_DIM) * dt_step[:, :, None]).astype(bf16)
    out = jnp.einsum("hts,shp->thp", mixed, scaled, preferred_element_type=f32)
    return out.reshape(values.shape)


def ssd_backward(grad_y, values, b_rows, c_rows, dt_step, cum, usable):
    heads = dt_step.shape[1]
    b_low, c_low = b_rows.astype(bf16), c_rows.astype(bf16)
    scores = dot_nt(c_low, b_low)
    diff = cum.T[:, :, None] - cum.T[:, None, :]
    decay = jnp.exp(jnp.where(usable[None], diff, -1e30))
    mixed = decay * scores[None]
    vals = values.reshape(-1, heads, HEAD_DIM)
    scaled = (vals * dt_step[:, :, None]).astype(bf16)
    gy = grad_y.reshape(-1, heads, HEAD_DIM).astype(bf16)
    grad_scaled = jnp.einsum("hts,thp->shp", mixed.astype(bf16), gy, preferred_element_type=f32)
    grad_mixed = jnp.einsum("thp,shp->hts", gy, scaled, preferred_element_type=f32)
    grad_scores = jnp.sum(grad_mixed * decay, axis=0).astype(bf16)
    product = grad_mixed * mixed
    grad_cum = (jnp.sum(product, axis=2) - jnp.sum(product, axis=1)).T
    grad_c = dot(grad_scores, b_low)
    grad_b = dot_tn(grad_scores, c_low)
    grad_vals = grad_scaled * dt_step[:, :, None]
    grad_step = jnp.sum(grad_scaled * vals, axis=2)
    return grad_vals.reshape(values.shape), grad_b, grad_c, grad_step, grad_cum


def on_device(
    tokens, cotangent, lengths, routes,
    w_in, w_in_first, w_in_second,
    w_out, w_out_first, w_out_second,
    w_router, w_router_first, w_router_second,
    w_shared_gu, w_shared_gu_first, w_shared_gu_second,
    w_shared_down, w_shared_down_first, w_shared_down_second,
    w_expert_gu, w_expert_gu_first, w_expert_gu_second,
    w_expert_down, w_expert_down_first, w_expert_down_second,
    norm_gains, norm_gains_first, norm_gains_second,
    conv_params, conv_params_first, conv_params_second,
    head_params, head_params_first, head_params_second,
    mixer_gain, mixer_gain_first, mixer_gain_second,
):
    groups = lax.axis_size("expert")
    copies = lax.axis_size("dp")
    place = lax.axis_index("expert")
    tok = tokens.shape[0]
    length = tok * groups
    top = routes.shape[1]
    experts = w_router.shape[1]
    own_experts = w_expert_gu.shape[0]
    capacity = (4 * tok * top + 3 * experts - 1) // (3 * experts)
    inner = INNER // groups
    heads = HEADS // groups
    rows_in = w_in.shape[0]
    rows_out = w_out.shape[0]
    rows_sd = w_shared_down.shape[0]
    own_ff = SHARED_FF // groups
    per_pair = copies // groups
    conv_cols = inner + 2 * STATE
    body = 2 * inner + 2 * STATE

    w_in_low = w_in.astype(bf16)
    z_cols = w_in_low[:, :INNER].reshape(rows_in, groups, inner)
    x_cols = w_in_low[:, INNER : 2 * INNER].reshape(rows_in, groups, inner)
    bc_cols = jnp.broadcast_to(
        w_in_low[:, None, 2 * INNER : 2 * INNER + 2 * STATE], (rows_in, groups, 2 * STATE)
    )
    dt_cols = w_in_low[:, 2 * INNER + 2 * STATE :].reshape(rows_in, groups, heads)
    router_cols = jnp.broadcast_to(
        w_router.astype(bf16)[:, None], (rows_in, groups, experts)
    )
    fill = jnp.zeros((rows_in, groups, LANES - heads - experts), bf16)
    win_pieces = jnp.concatenate(
        [z_cols, x_cols, bc_cols, dt_cols, router_cols, fill], axis=2
    ).transpose(1, 0, 2)
    win_rows = swap(win_pieces, "expert").reshape(groups * rows_in, -1)
    win = lax.all_gather(win_rows, "dp", axis=0, tiled=True)
    router = win[:, body + heads : body + heads + experts]
    x_all = spread(tokens, "expert").reshape(length, D)
    cot_all = spread(cotangent, "expert").reshape(length, D)
    routes_all = spread(routes, "expert").reshape(length, top)

    wout_shards = lax.all_gather(w_out.astype(bf16), "dp", axis=0, tiled=False)
    wout = (
        swap(wout_shards.reshape(groups, per_pair * rows_out, D), "expert")
        .reshape(groups, per_pair, rows_out, D)
        .transpose(1, 0, 2, 3)
        .reshape(inner, D)
    )
    sgu_pieces = (
        w_shared_gu.astype(bf16)
        .reshape(rows_in, 2, copies, groups, rows_sd)
        .transpose(3, 0, 1, 2, 4)
        .reshape(groups, rows_in, 2 * own_ff)
    )
    sgu = lax.all_gather(
        swap(sgu_pieces, "expert").reshape(groups * rows_in, 2 * own_ff), "dp", axis=0, tiled=True
    )
    sd = lax.all_gather(w_shared_down.astype(bf16), "dp", axis=0, tiled=True)
    egu = lax.all_gather(w_expert_gu.astype(bf16), "dp", axis=1, tiled=True)
    ed = lax.all_gather(w_expert_down.astype(bf16), "dp", axis=1, tiled=True)

    positions = jnp.arange(length, dtype=jnp.int32)
    starts = jnp.cumsum(lengths[0]) - lengths[0]
    doc_index = jnp.sum((starts[None, :] <= positions[:, None]).astype(jnp.int32), axis=1) - 1
    usable = (doc_index[:, None] == doc_index[None, :]) & (
        positions[:, None] >= positions[None, :]
    )
    usable_low = usable.astype(f32)
    earlier_doc = [
        jnp.concatenate([jnp.full((offset,), -1, jnp.int32), doc_index[: length - offset]])
        for offset in range(CONV)
    ]
    taps = [(earlier == doc_index).astype(f32)[:, None] for earlier in earlier_doc]

    own_x = place * inner
    conv_own = jnp.concatenate(
        [
            lax.dynamic_slice_in_dim(conv_params, own_x, inner, axis=1),
            conv_params[:, INNER:],
        ],
        axis=1,
    )
    head_own = lax.dynamic_slice_in_dim(head_params, place * heads, heads, axis=1)
    gain_own = lax.dynamic_slice_in_dim(mixer_gain, own_x, inner, axis=0)

    inputs = x_all.astype(f32)
    scale_one = rms_scale(inputs)
    normed_one = inputs * scale_one
    normed = (normed_one * norm_gains[0]).astype(bf16)
    projected = dot(normed, win)
    packed = projected[:, :body].astype(bf16)
    dt_raw = projected[:, body : body + heads]
    gate_z = packed[:, :inner].astype(f32)
    conv_in = packed[:, inner:].astype(f32)
    conv_out = conv_own[CONV]
    for offset in range(CONV):
        conv_out = conv_out + conv_own[offset] * shifted(conv_in, offset) * taps[offset]
    mixed_in = jax.nn.silu(conv_out)
    values = mixed_in[:, :inner]
    b_rows = mixed_in[:, inner : inner + STATE]
    c_rows = mixed_in[:, inner + STATE :]
    pre_step = dt_raw + head_own[1]
    dt_step = jax.nn.softplus(pre_step)
    rate_abs = jnp.exp(head_own[0])
    log_decay = -rate_abs * dt_step
    cum = jnp.dot(usable_low, log_decay, precision=highest)
    ssd_out = ssd_forward(values, b_rows, c_rows, dt_step, cum, usable)
    skip_cols = jnp.repeat(head_own[2], HEAD_DIM)
    full_y = ssd_out + skip_cols * values
    gate_act = jax.nn.silu(gate_z)
    gated_y = full_y * gate_act
    square_sum = jnp.sum(gated_y * gated_y, axis=1)
    partial_res = dot((gated_y * gain_own).astype(bf16), wout).astype(bf16)
    side = jnp.pad(jnp.stack(split_words(square_sum), axis=1), ((0, 0), (0, LANES - 3)))
    got = swap(jnp.concatenate([partial_res, side], axis=1).reshape(groups, tok, -1), "expert")
    squares = jnp.sum(
        got[:, :, D].astype(f32) + got[:, :, D + 1].astype(f32) + got[:, :, D + 2].astype(f32),
        axis=0,
    )[:, None]
    scale_mix = lax.rsqrt(squares / INNER + norm_eps)
    mixer_res = jnp.sum(got[:, :, :D].astype(f32), axis=0) * scale_mix
    hidden = tokens.astype(f32) + mixer_res
    scale_two = rms_scale(hidden)
    two_unit = hidden * scale_two
    normed_two_own = (two_unit * norm_gains[1]).astype(bf16)
    side = jnp.pad(jnp.concatenate(split_words(scale_mix), axis=1), ((0, 0), (0, LANES - 3)))
    got = spread(jnp.concatenate([normed_two_own, side], axis=1), "expert").reshape(length, -1)
    normed_two = got[:, :D]
    scale_mix_all = join_words([got[:, D + i : D + i + 1] for i in range(3)])

    logits = dot(normed_two, router)
    expert_ids = jnp.arange(experts, dtype=jnp.int32)
    named = jnp.any(routes_all[:, :, None] == expert_ids[None, None, :], axis=1)
    top_logit = jnp.max(jnp.where(named, logits, -jnp.inf), axis=1, keepdims=True)
    raised = jnp.where(named, jnp.exp(logits - top_logit), 0.0)
    weights = raised / jnp.sum(raised, axis=1, keepdims=True)

    shared_gu = dot(normed_two, sgu)
    shared_gate = shared_gu[:, :own_ff]
    shared_up = shared_gu[:, own_ff:]
    shared_silu = jax.nn.silu(shared_gate)
    shared_mid = (shared_silu * shared_up).astype(bf16)
    grad_shared_mid = dot_nt(cot_all, sd)
    grad_sgu_act = jnp.concatenate(
        [grad_shared_mid * shared_up * silu_slope(shared_gate), grad_shared_mid * shared_silu],
        axis=-1,
    ).astype(bf16)

    own_cols = place * own_experts
    named_own = lax.dynamic_slice_in_dim(named, own_cols, own_experts, axis=1)
    weights_own = lax.dynamic_slice_in_dim(weights, own_cols, own_experts, axis=1)
    named_blk = named_own.reshape(groups, tok, own_experts).astype(f32)
    before = jnp.tril(jnp.ones((tok, tok), f32), -1)
    slot_of = jnp.einsum("ts,gse->gte", before, named_blk)
    slots = jnp.arange(capacity, dtype=f32)
    pick = (
        (slot_of.transpose(0, 2, 1)[:, :, None, :] == slots[None, None, :, None])
        & (named_blk.transpose(0, 2, 1)[:, :, None, :] > 0)
    ).astype(bf16)
    pick_rows = pick.reshape(groups, own_experts * capacity, tok)
    two_blk = normed_two.reshape(groups, tok, D)
    cot_blk = cot_all.reshape(groups, tok, D)
    slot_in = jnp.einsum("gst,gtd->gsd", pick_rows, two_blk, preferred_element_type=f32)
    slot_in = slot_in.astype(bf16).reshape(groups, own_experts, capacity, D)
    slot_cot = jnp.einsum("gst,gtd->gsd", pick_rows, cot_blk, preferred_element_type=f32).reshape(
        groups, own_experts, capacity, D
    )
    slot_weight = jnp.sum(
        pick.astype(f32)
        * weights_own.reshape(groups, tok, own_experts).transpose(0, 2, 1)[:, :, None, :],
        axis=3,
    )
    slot_grad = (slot_cot * slot_weight[..., None]).astype(bf16)
    gate_up = jnp.einsum("gecd,edf->gecf", slot_in, egu, preferred_element_type=f32)
    gate_part = gate_up[..., :EXPERT_FF]
    up_part = gate_up[..., EXPERT_FF:]
    gate_silu = jax.nn.silu(gate_part)
    middle = (gate_silu * up_part).astype(bf16)
    slot_out = jnp.einsum("gecf,efd->gecd", middle, ed, preferred_element_type=f32)
    grad_mid = jnp.einsum("gecd,efd->gecf", slot_grad, ed, preferred_element_type=f32)
    grad_gu = jnp.concatenate(
        [grad_mid * up_part * silu_slope(gate_part), grad_mid * gate_silu], axis=-1
    ).astype(bf16)
    slot_back = jnp.einsum("gecf,edf->gecd", grad_gu, egu, preferred_element_type=f32).astype(bf16)
    grad_ed = jnp.einsum("gecf,gecd->efd", middle, slot_grad, preferred_element_type=f32)
    grad_egu = jnp.einsum("gecd,gecf->edf", slot_in, grad_gu, preferred_element_type=f32)
    slot_q = jnp.sum(slot_cot * slot_out, axis=3)
    token_q = jnp.sum(pick.astype(f32) * slot_q[..., None], axis=2)
    token_q = token_q.transpose(0, 2, 1).reshape(length, own_experts)

    def back_to_tokens(rows):
        rows = rows.reshape(groups, own_experts * capacity, D)
        return jnp.einsum("gst,gsd->gtd", pick_rows, rows, preferred_element_type=f32).reshape(
            length, D
        )

    expert_mix = back_to_tokens((slot_out * slot_weight[..., None]).astype(bf16))
    out_part = (dot(shared_mid, sd) + expert_mix).astype(bf16)
    back_part = (dot_nt(grad_sgu_act, sgu) + back_to_tokens(slot_back)).astype(bf16)
    side = jnp.pad(
        jnp.concatenate(split_words(token_q), axis=1), ((0, 0), (0, LANES - 3 * own_experts))
    )
    got = swap(jnp.concatenate([back_part, side], axis=1).reshape(groups, tok, -1), "expert")
    got_out = swap(out_part.reshape(groups, tok, D), "expert")
    output = (hidden + jnp.sum(got_out.astype(f32), axis=0)).astype(bf16)
    words = [
        got[:, :, D + i * own_experts : D + (i + 1) * own_experts].astype(f32) for i in range(3)
    ]
    q_own = (words[0] + words[1] + words[2]).transpose(1, 0, 2).reshape(tok, experts)
    weights_tok = lax.dynamic_slice_in_dim(weights, place * tok, tok, axis=0)
    grad_logits = (
        weights_tok * (q_own - jnp.sum(weights_tok * q_own, axis=1, keepdims=True))
    ).astype(bf16)
    grad_router = dot_tn(normed_two_own, grad_logits)
    grad_norm_two = jnp.sum(got[:, :, :D].astype(f32), axis=0) + dot_nt(grad_logits, router)
    grad_gain_two = jnp.sum(grad_norm_two * two_unit, axis=0)
    grad_hidden = cotangent.astype(f32) + norm_back(
        grad_norm_two, two_unit, scale_two, norm_gains[1]
    )
    hidden_low = grad_hidden.astype(bf16)
    row_mean = jnp.sum(hidden_low.astype(f32) * mixer_res, axis=1, keepdims=True) / INNER
    side = jnp.pad(jnp.concatenate(split_words(row_mean), axis=1), ((0, 0), (0, LANES - 3)))
    got = spread(jnp.concatenate([hidden_low, side], axis=1), "expert").reshape(length, -1)
    hidden_all = got[:, :D]
    row_mean_all = join_words([got[:, D + i : D + i + 1] for i in range(3)])

    grad_sgu = dot_tn(normed_two, grad_sgu_act).astype(bf16)
    grad_sd = dot_tn(shared_mid, cot_all).astype(bf16)
    sum_egu = lax.psum_scatter(
        grad_egu.astype(bf16), "dp", scatter_dimension=1, tiled=True
    ).astype(f32)
    sum_ed = lax.psum_scatter(grad_ed.astype(bf16), "dp", scatter_dimension=1, tiled=True).astype(
        f32
    )
    sgu_mine = lax.psum_scatter(grad_sgu, "dp", scatter_dimension=0, tiled=True)
    sum_sgu = (
        swap(sgu_mine.reshape(groups, rows_in, 2 * own_ff), "expert")
        .reshape(groups, rows_in, 2, copies, rows_sd)
        .transpose(1, 2, 3, 0, 4)
        .reshape(rows_in, 2 * SHARED_FF)
        .astype(f32)
    )
    sum_sd = lax.psum_scatter(grad_sd, "dp", scatter_dimension=0, tiled=True).astype(f32)

    normed_mix = gated_y * scale_mix_all
    mixer_act = (normed_mix * gain_own).astype(bf16)
    grad_wout = dot_tn(mixer_act, hidden_all).astype(bf16)
    wout_send = (
        grad_wout.reshape(per_pair, groups, rows_out, D)
        .transpose(1, 0, 2, 3)
        .reshape(groups, per_pair * rows_out, D)
    )
    wout_got = swap(wout_send, "expert").reshape(copies * rows_out, D)
    sum_out = lax.psum_scatter(wout_got, "dp", scatter_dimension=0, tiled=True).astype(f32)
    grad_mix_act = dot_nt(hidden_all, wout)
    grad_gain_mix = jnp.sum(grad_mix_act * normed_mix, axis=0)
    grad_gated = scale_mix_all * (grad_mix_act * gain_own - normed_mix * row_mean_all)
    grad_full_y = grad_gated * gate_act
    grad_gate_z = grad_gated * full_y * silu_slope(gate_z)
    grad_skip = jnp.sum(jnp.sum(grad_full_y * values, axis=0).reshape(heads, HEAD_DIM), axis=1)
    grad_vals, grad_b, grad_c, grad_step, grad_cum = ssd_backward(
        grad_full_y, values, b_rows, c_rows, dt_step, cum, usable
    )
    grad_vals = grad_vals + grad_full_y * skip_cols
    grad_decay = lax.dot_general(
        usable_low, grad_cum, (((0,), (0,)), ((), ())), precision=highest
    )
    grad_step = grad_step - grad_decay * rate_abs
    grad_log_rate = jnp.sum(grad_decay * log_decay, axis=0)
    grad_pre = grad_step * jax.nn.sigmoid(pre_step)
    grad_bias = jnp.sum(grad_pre, axis=0)
    grad_mixed = jnp.concatenate([grad_vals, grad_b, grad_c], axis=1)
    grad_conv = grad_mixed * silu_slope(conv_out)
    conv_grads = []
    grad_conv_in = jnp.zeros_like(grad_conv)
    for offset in range(CONV):
        masked = grad_conv * taps[offset]
        conv_grads.append(jnp.sum(masked * shifted(conv_in, offset), axis=0))
        grad_conv_in = grad_conv_in + shifted(conv_own[offset] * masked, -offset)
    conv_grads.append(jnp.sum(grad_conv, axis=0))
    conv_grads = jnp.stack(conv_grads)
    grad_proj = jnp.concatenate(
        [
            grad_gate_z.astype(bf16),
            grad_conv_in.astype(bf16),
            grad_pre.astype(bf16),
            jnp.zeros((length, LANES - heads), bf16),
        ],
        axis=1,
    )
    grad_win = dot_tn(normed, grad_proj)
    grad_win = jnp.concatenate(
        [
            grad_win[:, : body + heads],
            grad_router,
            jnp.zeros((D, LANES - heads - experts), f32),
        ],
        axis=1,
    ).astype(bf16)
    one_part = dot_nt(grad_proj, win)
    grad_gain_one = jnp.sum(one_part * normed_one, axis=0)
    got = swap(one_part.astype(bf16).reshape(groups, tok, D), "expert")
    grad_norm_one = jnp.sum(got.astype(f32), axis=0)
    own_in = tokens.astype(f32)
    own_scale = rms_scale(own_in)
    grad_tokens = (
        grad_hidden + norm_back(grad_norm_one, own_in * own_scale, own_scale, norm_gains[0])
    ).astype(bf16)

    pieces = [
        conv_grads[:, :inner].reshape(-1),
        grad_gain_mix,
        grad_log_rate,
        grad_bias,
        grad_skip,
        conv_grads[:, inner:].reshape(-1),
        grad_gain_one,
        grad_gain_two,
    ]
    sizes = [piece.size for piece in pieces]
    total = sum(sizes)
    unit = copies * LANES
    small = jnp.pad(jnp.concatenate(pieces), (0, -total % unit)).reshape(copies, -1)
    small = jnp.sum(swap(small, "dp"), axis=0)
    small = lax.all_gather(small, ("expert", "dp"), axis=0, tiled=True).reshape(groups, -1)
    parts = []
    start = 0
    for size in sizes:
        parts.append(small[:, start : start + size])
        start += size
    sum_conv = jnp.concatenate(
        [
            parts[0].reshape(groups, CONV + 1, inner).transpose(1, 0, 2).reshape(CONV + 1, INNER),
            jnp.sum(parts[5], axis=0).reshape(CONV + 1, 2 * STATE),
        ],
        axis=1,
    )
    sum_mixer = parts[1].reshape(INNER)
    sum_head = jnp.stack([parts[2].reshape(HEADS), parts[3].reshape(HEADS), parts[4].reshape(HEADS)])
    sum_gains = jnp.stack([jnp.sum(parts[6], axis=0), jnp.sum(parts[7], axis=0)])

    win_mine = lax.psum_scatter(grad_win, "dp", scatter_dimension=0, tiled=True)
    win_got = swap(win_mine.reshape(groups, rows_in, -1), "expert").astype(f32)

    def laid(start, size):
        return win_got[:, :, start : start + size].transpose(1, 0, 2).reshape(rows_in, -1)

    sum_in = jnp.concatenate(
        [
            laid(0, inner),
            laid(inner, inner),
            jnp.sum(win_got[:, :, 2 * inner : body], axis=0),
            laid(body, heads),
        ],
        axis=1,
    )
    sum_router = jnp.sum(win_got[:, :, body + heads : body + heads + experts], axis=0)

    up_in = adam_step(w_in, w_in_first, w_in_second, sum_in)
    up_out = adam_step(w_out, w_out_first, w_out_second, sum_out)
    up_router = adam_step(w_router, w_router_first, w_router_second, sum_router)
    up_sgu = adam_step(w_shared_gu, w_shared_gu_first, w_shared_gu_second, sum_sgu)
    up_sd = adam_step(w_shared_down, w_shared_down_first, w_shared_down_second, sum_sd)
    up_egu = adam_step(w_expert_gu, w_expert_gu_first, w_expert_gu_second, sum_egu)
    up_ed = adam_step(w_expert_down, w_expert_down_first, w_expert_down_second, sum_ed)
    up_gains = adam_step(norm_gains, norm_gains_first, norm_gains_second, sum_gains)
    up_conv = adam_step(conv_params, conv_params_first, conv_params_second, sum_conv)
    up_head = adam_step(head_params, head_params_first, head_params_second, sum_head)
    up_mixer = adam_step(mixer_gain, mixer_gain_first, mixer_gain_second, sum_mixer)
    large = (up_in, up_out, up_router, up_sgu, up_sd, up_egu, up_ed)
    little = (up_gains, up_conv, up_head, up_mixer)
    return (
        (output, grad_tokens)
        + tuple(part for one in large for part in one[:4])
        + tuple(part for one in little for part in (one[0], one[4], one[2], one[3]))
    )


def solution(mesh):
    rows = P(("dp", "expert"), None)
    expert_rows = P("expert", "dp", None)
    whole = P()
    return jax.shard_map(
        on_device,
        mesh=mesh,
        in_specs=(rows, rows, P("dp", None), rows)
        + (rows,) * 15
        + (expert_rows,) * 6
        + (whole,) * 12,
        out_specs=(rows, rows) + (rows,) * 20 + (expert_rows,) * 8 + (whole,) * 16,
        check_vma=False,
    )
```

```python
import functools
import math

import jax
import jax.numpy as jnp
from jax import lax
from jax.experimental import pallas as pl
from jax.experimental.pallas import tpu as pltpu
from jax.sharding import Mesh
from jax.sharding import PartitionSpec as P

D = 1536
HEADS = 48
HEAD_DIM = 64
STATE = 128
CONV = 4
EXPERT_FF = 512
SHARED_FF = 1024
STEP = 3
INNER = 3072
CONV_DIM = 3328
LANES = 128

DP = ("zhi", "zlo", "core")
MATES = ("zlo", "core")
ALL = DP + ("expert",)

norm_eps = 1e-05
beta_one = 0.9
beta_two = 0.95
adam_eps = 1e-08
learn_rate = 0.02
decay_rate = 0.1
highest = lax.Precision.HIGHEST
bf16 = jnp.bfloat16
f32 = jnp.float32


def dot(left, right):
    return jnp.dot(left, right, preferred_element_type=f32)


def dot_nt(left, right):
    return lax.dot_general(left, right, (((1,), (1,)), ((), ())), preferred_element_type=f32)


def dot_tn(left, right):
    return lax.dot_general(left, right, (((0,), (0,)), ((), ())), preferred_element_type=f32)


def swap(pieces, axis):
    return lax.all_to_all(pieces, axis, split_axis=0, concat_axis=0, tiled=True)


def spread(block, axis):
    axes = (axis,) if isinstance(axis, str) else axis
    count = math.prod(lax.axis_size(one) for one in axes)
    return swap(jnp.broadcast_to(block[None], (count,) + block.shape), axis)


def to_partner(value):
    return lax.ppermute(value, "zhi", [(0, 1), (1, 0)])


def rms_scale(values):
    return lax.rsqrt(jnp.mean(values * values, axis=-1, keepdims=True) + norm_eps)


def silu_slope(values):
    sigmoid_value = jax.nn.sigmoid(values)
    return sigmoid_value * (1.0 + values * (1.0 - sigmoid_value))


def norm_back(grad_norm, unit_rows, scale_rows, gain):
    scaled = grad_norm * gain
    return scale_rows * (scaled - unit_rows * jnp.mean(scaled * unit_rows, axis=-1, keepdims=True))


def adam_step(weight, moment_one, moment_two, gradient):
    moment_one = beta_one * moment_one + (1.0 - beta_one) * gradient
    moment_two = beta_two * moment_two + (1.0 - beta_two) * gradient * gradient
    fixed_one = 1.0 - beta_one**STEP
    fixed_two = 1.0 - beta_two**STEP
    change = (
        moment_one / fixed_one / (jnp.sqrt(moment_two / fixed_two) + adam_eps) + decay_rate * weight
    )
    moved = -learn_rate * change
    return (gradient, weight + moved, moment_one, moment_two, moved)


def split_words(value):
    high = value.astype(bf16)
    rest = value - high.astype(f32)
    mid = rest.astype(bf16)
    low = (rest - mid.astype(f32)).astype(bf16)
    return high, mid, low


def join_words(words):
    return words[0].astype(f32) + words[1].astype(f32) + words[2].astype(f32)


def conv_rows(block, masks, params):
    total = params[CONV : CONV + 1] + params[0:1] * block
    for offset in range(1, CONV):
        total = total + params[offset : offset + 1] * (
            pltpu.roll(block, offset, 0) * masks[:, offset : offset + 1]
        )
    return total


def conv_rows_back(grad, block, masks, params):
    length = block.shape[0]
    taps = [jnp.sum(grad * block, axis=0, keepdims=True)]
    rows = params[0:1] * grad
    for offset in range(1, CONV):
        masked = grad * masks[:, offset : offset + 1]
        taps.append(jnp.sum(masked * pltpu.roll(block, offset, 0), axis=0, keepdims=True))
        rows = rows + pltpu.roll(params[offset : offset + 1] * masked, length - offset, 0)
    taps.append(jnp.sum(grad, axis=0, keepdims=True))
    return rows, taps


def dot_words(exact, value, contract):
    total = None
    for word in split_words(value):
        part = lax.dot_general(exact, word, (contract, ((), ())), preferred_element_type=f32)
        total = part if total is None else total + part
    return total


def dot_words_left(value, exact):
    total = None
    for word in split_words(value):
        part = jnp.dot(word, exact, preferred_element_type=f32)
        total = part if total is None else total + part
    return total


def softplus(value):
    return jnp.maximum(value, 0.0) + jnp.log1p(jnp.exp(-jnp.abs(value)))


def head_lanes(pair, transposed=False):
    rows = lax.broadcasted_iota(jnp.int32, (LANES, LANES), 0)
    lanes = lax.broadcasted_iota(jnp.int32, (LANES, LANES), 1)
    if transposed:
        rows, lanes = lanes, rows
    return (rows == 2 * pair + lanes // HEAD_DIM).astype(f32).astype(bf16)


def lane_of(matrix, lane):
    lanes = lax.broadcasted_iota(jnp.int32, matrix.shape, 1)
    return jnp.sum(jnp.where(lanes == lane, matrix, 0.0), axis=1, keepdims=True)


def scan_setup(dt_ref, packed_ref, conv_ref, masks, head_ref, doc_col, doc_row, inner,
               neg_ref, scores_ref, cum_ref, cum_t_ref):
    length = dt_ref.shape[0]
    pre_step = dt_ref[...] + head_ref[1:2]
    dt_step = softplus(pre_step)
    log_decay = -head_ref[0:1] * dt_step
    at = lax.broadcasted_iota(jnp.int32, (length, length), 0)
    to = lax.broadcasted_iota(jnp.int32, (length, length), 1)
    usable = (doc_col == doc_row) & (at >= to)
    neg_ref[...] = jnp.where(usable, 0.0, -1e30)
    exact = usable.astype(f32).astype(bf16)
    cum_ref[...] = dot_words(exact, log_decay, ((1,), (0,)))
    cum_t_ref[...] = cum_ref[...].T
    start = 2 * inner
    b_in = packed_ref[:, start : start + STATE].astype(f32)
    c_in = packed_ref[:, start + STATE : start + 2 * STATE].astype(f32)
    b_out = conv_rows(b_in, masks, conv_ref[:, inner : inner + STATE])
    c_out = conv_rows(c_in, masks, conv_ref[:, inner + STATE : inner + 2 * STATE])
    b_low = jax.nn.silu(b_out).astype(bf16)
    c_low = jax.nn.silu(c_out).astype(bf16)
    scores_ref[...] = dot_nt(c_low, b_low)
    return pre_step, dt_step, log_decay, exact, b_out, c_out, b_low, c_low


def pair_slices(pair, inner):
    at = pl.ds(pl.multiple_of(pair * LANES, LANES), LANES)
    x_at = pl.ds(pl.multiple_of(inner + pair * LANES, LANES), LANES)
    return at, x_at


def forward_kernel(x_ref, win_ref, gain_ref, conv_ref, masks_ref, head_ref, cols_ref, doc_col_ref,
                   doc_row_ref, wout_ref, packed_ref, dt_ref, y_ref, out_ref,
                   normed_ref, neg_ref, scores_ref, cum_ref, cum_t_ref, act_ref, square_ref):
    length = x_ref.shape[0]
    inner = wout_ref.shape[0]
    body = packed_ref.shape[1]
    step = 2 * LANES

    @pl.loop(0, length // LANES)
    def _(part):
        rows = pl.ds(pl.multiple_of(part * LANES, LANES), LANES)
        block = x_ref[rows, :].astype(f32)
        scale = lax.rsqrt(jnp.mean(block * block, axis=1, keepdims=True) + norm_eps)
        normed_ref[rows, :] = (block * scale * gain_ref[0:1]).astype(bf16)

    @pl.loop(0, body // step)
    def _(part):
        at = pl.ds(pl.multiple_of(part * step, step), step)
        packed_ref[:, at] = dot(normed_ref[...], win_ref[:, at]).astype(bf16)

    dt_ref[...] = dot(normed_ref[...], win_ref[:, body:])
    masks = masks_ref[...]
    _, dt_step, *_ = scan_setup(
        dt_ref, packed_ref, conv_ref, masks, head_ref, doc_col_ref[...], doc_row_ref[...], inner,
        neg_ref, scores_ref, cum_ref, cum_t_ref,
    )
    square_ref[...] = jnp.zeros_like(square_ref)
    lanes = lax.broadcasted_iota(jnp.int32, (LANES, LANES), 1)

    @pl.loop(0, inner // LANES)
    def _(pair):
        at, x_at = pair_slices(pair, inner)
        values = jax.nn.silu(conv_rows(packed_ref[:, x_at].astype(f32), masks, conv_ref[:, at]))
        dt_wide = dot_words_left(dt_step, head_lanes(pair))
        scaled = (values * dt_wide).astype(bf16)
        cum_cols = [lane_of(cum_ref[...], 2 * pair + k) for k in range(2)]
        cum_rows = [cum_t_ref[pl.ds(2 * pair + k, 1), :] for k in range(2)]
        outs = []
        for part in range(length // LANES):
            rows = slice(part * LANES, (part + 1) * LANES)
            wide = (part + 1) * LANES
            pieces = []
            for k in range(2):
                decay = jnp.exp(cum_cols[k][rows] - cum_rows[k][:, :wide] + neg_ref[rows, :wide])
                mixed = (decay * scores_ref[rows, :wide]).astype(bf16)
                pieces.append(dot(mixed, scaled[:wide]))
            outs.append(jnp.where(lanes < HEAD_DIM, pieces[0], pieces[1]))
        full_y = jnp.concatenate(outs, axis=0) + cols_ref[1:2, at] * values
        y_ref[:, at] = full_y.astype(bf16)
        gated = full_y * jax.nn.silu(packed_ref[:, at].astype(f32))
        square_ref[...] += gated * gated
        act_ref[:, at] = (gated * cols_ref[0:1, at]).astype(bf16)

    @pl.loop(0, D // step)
    def _(part):
        at = pl.ds(pl.multiple_of(part * step, step), step)
        out_ref[:, at] = dot(act_ref[...], wout_ref[:, at]).astype(bf16)

    squares = jnp.sum(square_ref[...], axis=1, keepdims=True)
    out_ref[:, D:] = word_lanes(squares)


def word_lanes(column):
    lanes = lax.broadcasted_iota(jnp.int32, (column.shape[0], LANES), 1)
    words = [word.astype(f32) for word in split_words(column)]
    row = jnp.where(lanes == 0, words[0], jnp.where(lanes == 1, words[1], words[2]))
    return jnp.where(lanes < 3, row, 0.0).astype(bf16)


def word_sum(words):
    return words[:, 0:1].astype(f32) + words[:, 1:2].astype(f32) + words[:, 2:3].astype(f32)


def backward_kernel(hid_ref, scale_ref, wout_ref, conv_ref, masks_ref, head_ref, cols_ref,
                    doc_col_ref, doc_row_ref, packed_ref, dt_ref, y_ref,
                    proj_ref, conv_grad_ref, cols_grad_ref, head_grad_ref,
                    neg_ref, scores_ref, cum_ref, cum_t_ref, grad_scores_ref, row_ref, col_ref,
                    step_ref, scaled_ref, low_ref):
    length = dt_ref.shape[0]
    inner = wout_ref.shape[0]
    body = packed_ref.shape[1]
    masks = masks_ref[...]
    pre_step, dt_step, log_decay, exact, b_out, c_out, b_low, c_low = scan_setup(
        dt_ref, packed_ref, conv_ref, masks, head_ref, doc_col_ref[...], doc_row_ref[...], inner,
        neg_ref, scores_ref, cum_ref, cum_t_ref,
    )
    grad_scores_ref[...] = jnp.zeros_like(grad_scores_ref)
    row_ref[...] = jnp.zeros_like(row_ref)
    col_ref[...] = jnp.zeros_like(col_ref)
    step_ref[...] = jnp.zeros_like(step_ref)
    conv_grad_ref[...] = jnp.zeros_like(conv_grad_ref)
    cols_grad_ref[...] = jnp.zeros_like(cols_grad_ref)
    head_grad_ref[...] = jnp.zeros_like(head_grad_ref)
    scale_mix = word_sum(scale_ref[...])
    row_mean = word_sum(hid_ref[:, D:])
    lanes_all = lax.broadcasted_iota(jnp.int32, (length, LANES), 1)
    lanes = lax.broadcasted_iota(jnp.int32, (LANES, LANES), 1)

    @pl.loop(0, inner // LANES)
    def _(pair):
        at, x_at = pair_slices(pair, inner)
        grad_act = dot_nt(hid_ref[:, :D], wout_ref[at, :])
        conv_in = packed_ref[:, x_at].astype(f32)
        conv_out = conv_rows(conv_in, masks, conv_ref[:, at])
        values = jax.nn.silu(conv_out)
        gate_z = packed_ref[:, at].astype(f32)
        gate_act = jax.nn.silu(gate_z)
        full_y = y_ref[:, at].astype(f32)
        normed_mix = full_y * gate_act * scale_mix
        gain = cols_ref[0:1, at]
        skip = cols_ref[1:2, at]
        cols_grad_ref[0:1, at] = jnp.sum(grad_act * normed_mix, axis=0, keepdims=True)
        grad_gated = scale_mix * (grad_act * gain - normed_mix * row_mean)
        grad_y = grad_gated * gate_act
        proj_ref[:, at] = (grad_gated * full_y * silu_slope(gate_z)).astype(bf16)
        cols_grad_ref[1:2, at] = jnp.sum(grad_y * values, axis=0, keepdims=True)
        dt_wide = dot_words_left(dt_step, head_lanes(pair))
        scaled_low = (values * dt_wide).astype(bf16)
        low_ref[...] = grad_y.astype(bf16)
        scaled_ref[...] = jnp.zeros_like(scaled_ref)
        for k in range(2):
            head = 2 * pair + k
            cum_col = lane_of(cum_ref[...], head)
            cum_row = cum_t_ref[pl.ds(head, 1), :]
            for part in range(length // LANES):
                rows = slice(part * LANES, (part + 1) * LANES)
                wide = (part + 1) * LANES
                decay = jnp.exp(cum_col[rows] - cum_row[:, :wide] + neg_ref[rows, :wide])
                mixed = decay * scores_ref[rows, :wide]
                mine = jnp.where(lanes // HEAD_DIM == k, low_ref[rows, :].astype(f32), 0.0)
                mine = mine.astype(bf16)
                grad_mixed = dot_nt(mine, scaled_low[:wide])
                grad_scores_ref[rows, :wide] += grad_mixed * decay
                product = grad_mixed * mixed
                row_ref[rows, :] += jnp.where(
                    lanes == head, jnp.sum(product, axis=1, keepdims=True), 0.0
                )
                sums = jnp.sum(product, axis=0, keepdims=True)
                if part < length // LANES - 1:
                    sums = jnp.concatenate(
                        [sums, jnp.zeros((1, length - wide), f32)], axis=1
                    )
                col_sums = sums if part == 0 else col_sums + sums
                scaled_ref[:wide, :] += dot_tn(mixed.astype(bf16), mine)
            col_ref[pl.ds(head, 1), :] = col_sums
        grad_scaled = scaled_ref[...]
        step_ref[...] += dot_words_left(grad_scaled * values, head_lanes(pair, True))
        grad_values = grad_scaled * dt_wide + grad_y * skip
        grad_rows, taps = conv_rows_back(
            grad_values * silu_slope(conv_out), conv_in, masks, conv_ref[:, at]
        )
        proj_ref[:, x_at] = grad_rows.astype(bf16)
        for k in range(CONV + 1):
            conv_grad_ref[k : k + 1, at] = taps[k]

    grad_scores = grad_scores_ref[...].astype(bf16)
    for number, (grad, before) in enumerate(
        ((dot_tn(grad_scores, c_low), b_out), (dot(grad_scores, b_low), c_out))
    ):
        start = inner + number * STATE
        conv_in = packed_ref[:, inner + start : inner + start + STATE].astype(f32)
        grad_rows, taps = conv_rows_back(
            grad * silu_slope(before), conv_in, masks, conv_ref[:, start : start + STATE]
        )
        proj_ref[:, inner + start : inner + start + STATE] = grad_rows.astype(bf16)
        for k in range(CONV + 1):
            conv_grad_ref[k : k + 1, start : start + STATE] = taps[k]
    grad_cum = row_ref[...] - col_ref[...].T
    grad_decay = dot_words(exact, grad_cum, ((0,), (0,)))
    rate_abs = head_ref[0:1]
    grad_pre = (step_ref[...] - grad_decay * rate_abs) * jax.nn.sigmoid(pre_step)
    head_grad_ref[0:1] = jnp.sum(grad_decay * log_decay, axis=0, keepdims=True)
    head_grad_ref[1:2] = jnp.sum(grad_pre, axis=0, keepdims=True)
    proj_ref[:, body:] = grad_pre.astype(bf16)


def route_kernel(two_ref, cot_ref, routes_ref, router_ref, ids_ref,
                 in_ref, top_ref, grad_ref, weights_ref, pick_ref):
    tok = two_ref.shape[0]
    held, capacity, _ = in_ref.shape
    rows = two_ref[:, :D]
    logits = dot(rows, router_ref[...])
    lanes = lax.broadcasted_iota(jnp.int32, (tok, LANES), 1)
    named = lanes < 0
    for k in range(routes_ref.shape[1]):
        named = named | (lanes == routes_ref[:, k : k + 1])
    top_logit = jnp.max(jnp.where(named, logits, -1e30), axis=1, keepdims=True)
    raised = jnp.where(named, jnp.exp(jnp.where(named, logits - top_logit, 0.0)), 0.0)
    weights = raised / jnp.sum(raised, axis=1, keepdims=True)
    weights_ref[...] = weights
    at = lax.broadcasted_iota(jnp.int32, (tok, tok), 0)
    to = lax.broadcasted_iota(jnp.int32, (tok, tok), 1)
    named_f = named.astype(f32)
    slot = dot((at > to).astype(f32).astype(bf16), named_f.astype(bf16))
    slots = lax.broadcasted_iota(jnp.int32, (tok, capacity), 1).astype(f32)
    picks = []
    for expert in range(held):
        lane = ids_ref[0] + expert
        mine = (lane_of(slot, lane) == slots) & (lane_of(named_f, lane) > 0.0)
        pick = mine.astype(f32).astype(bf16)
        picks.append(pick)
        in_ref[expert] = dot_tn(pick, rows).astype(bf16)
        top = dot_tn(pick, cot_ref[...])
        top_ref[expert] = top.astype(bf16)
        words = word_lanes(lane_of(weights, lane))
        slot_weight = jnp.sum(dot_tn(pick, words), axis=1, keepdims=True)
        grad_ref[expert] = (top * slot_weight).astype(bf16)
    pick_ref[0] = jnp.concatenate(picks, axis=1)


def shared_kernel(two_ref, cot_ref, sgu_ref, sd_ref, out_ref, back_ref, grad_gu_ref, grad_down_ref,
                  mid_ref, act_ref):
    width = sd_ref.shape[0]
    gate = dot(two_ref[:, :D], sgu_ref[:, :width])
    up = dot(two_ref[:, :D], sgu_ref[:, width:])
    silu = jax.nn.silu(gate)
    mid_ref[...] = (silu * up).astype(bf16)
    grad_mid = dot_nt(cot_ref[...], sd_ref[...])
    act_ref[:, :width] = (grad_mid * up * silu_slope(gate)).astype(bf16)
    act_ref[:, width:] = (grad_mid * silu).astype(bf16)

    @pl.loop(0, D // 256)
    def _(part):
        at = pl.ds(pl.multiple_of(part * 256, 256), 256)
        out_ref[:, at] = dot(mid_ref[...], sd_ref[:, at]).astype(bf16)
        back_ref[:, at] = dot_nt(act_ref[...], sgu_ref[at, :]).astype(bf16)
        grad_gu_ref[at, :] = dot_tn(two_ref[:, at], act_ref[...]).astype(bf16)
        grad_down_ref[:, at] = dot_tn(mid_ref[...], cot_ref[:, at]).astype(bf16)


def expert_kernel(in_ref, top_ref, grad_ref, gu_ref, down_ref, out_ref, back_ref, q_ref, sums_ref,
                  mid_ref, act_ref):
    mates, _, halves, rows_gu, _ = gu_ref.shape
    rows_down = down_ref.shape[3]
    shards = [(h, m) for h in range(halves) for m in range(mates)]

    def gu(at, which=shards):
        return jnp.concatenate([gu_ref[m, 0, h, :, at] for h, m in which], axis=0)

    def down(at):
        return jnp.concatenate([down_ref[m, 0, h, :, at] for h, m in shards], axis=0)

    for part in range(EXPERT_FF // 256):
        at = slice(part * 256, (part + 1) * 256)
        up_at = slice(EXPERT_FF + part * 256, EXPERT_FF + (part + 1) * 256)
        gate = dot(in_ref[0], gu(at))
        up = dot(in_ref[0], gu(up_at))
        silu = jax.nn.silu(gate)
        mid_ref[:, at] = (silu * up).astype(bf16)
        each = 256 // rows_down
        rows = jnp.concatenate(
            [down_ref[m, 0, h, :, :] for h, m in shards[part * each : (part + 1) * each]], axis=0
        )
        grad_mid = dot_nt(grad_ref[0], rows)
        act_ref[:, at] = (grad_mid * up * silu_slope(gate)).astype(bf16)
        act_ref[:, up_at] = (grad_mid * silu).astype(bf16)
    step = 384
    each = step // rows_gu
    q = jnp.zeros((in_ref.shape[1], 1), f32)
    for part in range(D // step):
        at = slice(part * step, (part + 1) * step)
        rows = dot(mid_ref[...], down(at))
        out_ref[0, :, at] = rows.astype(bf16)
        q = q + jnp.sum(rows * top_ref[0, :, at].astype(f32), axis=1, keepdims=True)
        chosen = shards[part * each : (part + 1) * each]
        back_ref[0, :, at] = dot_nt(act_ref[...], gu(slice(None), chosen)).astype(bf16)
        for number in range(2):
            half_at = slice(number * EXPERT_FF, (number + 1) * EXPERT_FF)
            total = dot_tn(in_ref[0, :, at], act_ref[:, half_at]).astype(bf16)
            for k, (h, m) in enumerate(chosen):
                sums_ref[m, h, 0, number * rows_gu : (number + 1) * rows_gu, :] = total[
                    k * rows_gu : (k + 1) * rows_gu
                ]
    q_ref[0] = jnp.broadcast_to(q, q_ref.shape[1:])
    for part in range(D // EXPERT_FF):
        total = dot_tn(mid_ref[...], grad_ref[0, :, part * EXPERT_FF : (part + 1) * EXPERT_FF])
        total = total.astype(bf16)
        start = 2 * rows_gu + part * rows_down
        for k, (h, m) in enumerate(shards):
            sums_ref[m, h, 0, start : start + rows_down, :] = total[
                k * rows_down : (k + 1) * rows_down
            ]


def combine_kernel(pick_ref, weights_ref, ids_ref, out_ref, back_ref, q_ref, own_out_ref,
                   own_back_ref, mix_ref, rows_ref):
    held = out_ref.shape[0]
    capacity = out_ref.shape[1]
    block = pl.program_id(0)
    own = (block < pl.num_programs(0) // 2).astype(f32)
    picks = [pick_ref[0, :, e * capacity : (e + 1) * capacity] for e in range(held)]
    mix = own_out_ref[...].astype(f32) * own
    back = own_back_ref[...].astype(f32) * own
    lanes = lax.broadcasted_iota(jnp.int32, (pick_ref.shape[1], LANES), 1)
    words = jnp.zeros((pick_ref.shape[1], LANES), f32)
    for expert in range(held):
        weight = lane_of(weights_ref[...], ids_ref[0] + expert)
        mix = mix + weight * dot(picks[expert], out_ref[expert])
        back = back + dot(picks[expert], back_ref[expert])
        token_q = jnp.sum(dot(picks[expert], word_lanes(q_ref[expert, :, :1])), axis=1,
                          keepdims=True)
        for k, word in enumerate(split_words(token_q)):
            words = jnp.where(lanes == k * held + expert, word.astype(f32), words)
    mix_ref[...] = mix.astype(bf16)
    rows_ref[:, :D] = back.astype(bf16)
    rows_ref[:, D:] = words.astype(bf16)


def peers():
    count = lax.axis_size("expert")
    me = lax.axis_index("expert")
    return count, me, [lax.rem(me + step, count) for step in range(1, count)]


def greet(with_partner):
    count, me, others = peers()
    barrier = pltpu.get_barrier_semaphore()
    for other in others:
        pl.semaphore_signal(
            barrier, inc=1, device_id={"expert": other}, device_id_type=pl.DeviceIdType.MESH
        )
    if with_partner:
        pl.semaphore_signal(
            barrier, inc=1, device_id={"zhi": 1 - lax.axis_index("zhi")},
            device_id_type=pl.DeviceIdType.MESH,
        )
    pl.semaphore_wait(barrier, count - 1 + (1 if with_partner else 0))


def remote(src, dst, sems, number, target):
    return pltpu.make_async_remote_copy(
        src_ref=src, dst_ref=dst, send_sem=sems[0].at[number], recv_sem=sems[1].at[number],
        device_id=target, device_id_type=pl.DeviceIdType.MESH,
    )


def spread_copies(src, dst, sems, base):
    _, me, others = peers()
    return [
        remote(src, dst.at[me], sems, base + number, {"expert": other})
        for number, other in enumerate(others)
    ]


def reduce_copies(src, dst, sems, base, rows, start):
    _, _, others = peers()
    return [
        remote(
            src.at[pl.ds(pl.multiple_of(start + other * rows, rows), rows)],
            dst.at[number], sems, base + number, {"expert": other},
        )
        for number, other in enumerate(others)
    ]


def reduced(src, dst, rows, start, columns):
    _, me, others = peers()
    total = src[pl.ds(pl.multiple_of(start + me * rows, rows), rows), columns].astype(f32)
    for number in range(len(others)):
        total = total + dst[number, :, columns].astype(f32)
    return total


def hidden_kernel(part_ref, tokens_ref, gain_ref, hidden_ref, res_ref, two_ref,
                  got_ref, send_sems, recv_sems):
    tok = tokens_ref.shape[0]
    sems = (send_sems, recv_sems)
    greet(False)
    copies = reduce_copies(part_ref, got_ref, sems, 0, tok, 0)
    for copy in copies:
        copy.start()
    for copy in copies:
        copy.wait()
    squares = word_sum(reduced(part_ref, got_ref, tok, 0, slice(D, D + LANES)))
    scale_mix = lax.rsqrt(squares / INNER + norm_eps)
    res = reduced(part_ref, got_ref, tok, 0, slice(0, D)) * scale_mix
    res_ref[...] = res
    hidden = tokens_ref[...].astype(f32) + res
    hidden_ref[...] = hidden
    scale = lax.rsqrt(jnp.mean(hidden * hidden, axis=1, keepdims=True) + norm_eps)
    two_ref[:, :D] = (hidden * scale * gain_ref[1:2]).astype(bf16)
    two_ref[:, D:] = word_lanes(scale_mix)


def share_kernel(two_ref, own_ref, other_ref, came_ref, send_sems, recv_sems, local_sems):
    count, me, _ = peers()
    sems = (send_sems, recv_sems)
    greet(True)
    over = remote(two_ref, came_ref, sems, 0, {"zhi": 1 - lax.axis_index("zhi")})
    over.start()
    first = spread_copies(two_ref, own_ref, sems, 1)
    for copy in first:
        copy.start()
    mine = pltpu.make_async_copy(two_ref, own_ref.at[me], local_sems.at[0])
    mine.start()
    over.wait()
    second = spread_copies(came_ref, other_ref, sems, count)
    for copy in second:
        copy.start()
    theirs = pltpu.make_async_copy(came_ref, other_ref.at[me], local_sems.at[1])
    theirs.start()
    for copy in first + second:
        copy.wait()
    mine.wait()
    theirs.wait()


def q_lanes(sources, held, own_experts, half):
    lanes = lax.broadcasted_iota(jnp.int32, sources[0][1].shape, 1)
    total = jnp.zeros(lanes.shape, f32)
    for place, words in sources:
        for expert in range(held):
            value = sum(
                words[:, k * held + expert : k * held + expert + 1].astype(f32) for k in range(3)
            )
            lane = place * own_experts + half * held + expert
            total = jnp.where(lanes == lane, value, total)
    return total


def back_kernel(back_ref, hidden_ref, res_ref, cot_ref, weights_ref, router_ref, gain_ref,
                all_ref, grad_hidden_ref, grad_logits_ref, gain_grad_ref,
                got_other_ref, got_own_ref, send_ref, came_ref, low_ref, send_sems, recv_sems,
                local_sem, *, own_experts):
    tok = cot_ref.shape[0]
    length = back_ref.shape[0] // 2
    held = own_experts // 2
    count, me, others = peers()
    half = lax.axis_index("zhi")
    sems = (send_sems, recv_sems)
    words_at = slice(D, D + LANES)
    greet(True)
    first = reduce_copies(back_ref, got_other_ref, sems, 0, tok, length)
    second = reduce_copies(back_ref, got_own_ref, sems, count - 1, tok, 0)
    for copy in first + second:
        copy.start()

    def q_of(start, slots):
        mine = back_ref[pl.ds(pl.multiple_of(start + me * tok, tok), tok), words_at]
        sources = [(me, mine)]
        for number in range(count - 1):
            sources.append((lax.rem(me + count - 1 - number, count), slots[number, :, words_at]))
        return q_lanes(sources, held, own_experts, half)

    for copy in first:
        copy.wait()
    send_ref[:, :D] = reduced(back_ref, got_other_ref, tok, length, slice(0, D)).astype(bf16)
    lanes = lax.broadcasted_iota(jnp.int32, (tok, LANES), 1)
    words = jnp.zeros((tok, LANES), f32)
    shift = LANES // 4
    for k, word in enumerate(split_words(q_of(length, got_other_ref))):
        placed = word.astype(f32) if k == 0 else pltpu.roll(word.astype(f32), k * shift, 1)
        words = words + placed
    send_ref[:, D:] = words.astype(bf16)
    over = remote(send_ref, came_ref, sems, 2 * (count - 1), {"zhi": 1 - half})
    over.start()
    for copy in second:
        copy.wait()
    q_own = q_of(0, got_own_ref)
    total = reduced(back_ref, got_own_ref, tok, 0, slice(0, D))
    over.wait()
    came = came_ref[:, D:].astype(f32)
    came = came + pltpu.roll(came, LANES - shift, 1) + pltpu.roll(came, LANES - 2 * shift, 1)
    q = q_own + jnp.where(lanes < shift, came, 0.0)
    weights = weights_ref[...]
    grad_logits = weights * (q - jnp.sum(weights * q, axis=1, keepdims=True))
    grad_logits_ref[...] = grad_logits.astype(bf16)
    total = total + came_ref[:, :D].astype(f32) + dot_nt(grad_logits_ref[...], router_ref[...])
    hidden = hidden_ref[...]
    scale = lax.rsqrt(jnp.mean(hidden * hidden, axis=1, keepdims=True) + norm_eps)
    unit = hidden * scale
    gain_grad_ref[...] = jnp.broadcast_to(
        jnp.sum(total * unit, axis=0, keepdims=True), gain_grad_ref.shape
    )
    grad_hidden = cot_ref[...].astype(f32) + norm_back(total, unit, scale, gain_ref[1:2])
    grad_hidden_ref[...] = grad_hidden
    low_ref[:, :D] = grad_hidden.astype(bf16)
    row_mean = jnp.sum(low_ref[:, :D].astype(f32) * res_ref[...], axis=1, keepdims=True) / INNER
    low_ref[:, D:] = word_lanes(row_mean)
    third = spread_copies(low_ref, all_ref, sems, 2 * count - 1)
    for copy in third:
        copy.start()
    mine = pltpu.make_async_copy(low_ref, all_ref.at[me], local_sem)
    mine.start()
    for copy in third:
        copy.wait()
    mine.wait()


def remote_call(kernel, number, out_shapes, scratch, sems, *operands):
    spec = pl.BlockSpec(memory_space=pltpu.VMEM)
    return pl.pallas_call(
        kernel,
        out_shape=out_shapes,
        in_specs=[spec] * len(operands),
        out_specs=[spec] * len(out_shapes),
        scratch_shapes=[pltpu.VMEM(shape, dtype) for shape, dtype in scratch] + sems,
        compiler_params=pltpu.CompilerParams(
            collective_id=number, has_side_effects=True, vmem_limit_bytes=48 * 1024 * 1024
        ),
    )(*operands)


def vmem_call(kernel, out_shapes, scratch, *operands):
    spec = pl.BlockSpec(memory_space=pltpu.VMEM)
    return pl.pallas_call(
        kernel,
        out_shape=out_shapes,
        in_specs=[spec] * len(operands),
        out_specs=[spec] * len(out_shapes),
        scratch_shapes=[pltpu.VMEM(shape, dtype) for shape, dtype in scratch],
        compiler_params=pltpu.CompilerParams(vmem_limit_bytes=56 * 1024 * 1024),
    )(*operands)


def grid_call(kernel, steps, in_specs, out_specs, out_shapes, scratch, *operands):
    return pl.pallas_call(
        kernel,
        grid=(steps,),
        out_shape=out_shapes,
        in_specs=in_specs,
        out_specs=out_specs,
        scratch_shapes=[pltpu.VMEM(shape, dtype) for shape, dtype in scratch],
        compiler_params=pltpu.CompilerParams(vmem_limit_bytes=56 * 1024 * 1024),
    )(*operands)


def sgu_rows(grad):
    copies = lax.axis_size("zhi") * lax.axis_size("zlo") * lax.axis_size("core")
    wide = D // grad.shape[1]
    pieces = grad.reshape(copies, wide, -1, grad.shape[1])
    return jnp.concatenate([pieces[:, k] for k in range(wide)], axis=2)


def on_device(
    tokens, cotangent, lengths, routes,
    w_in, w_in_first, w_in_second,
    w_out, w_out_first, w_out_second,
    w_router, w_router_first, w_router_second,
    w_shared_gu, w_shared_gu_first, w_shared_gu_second,
    w_shared_down, w_shared_down_first, w_shared_down_second,
    w_expert_gu, w_expert_gu_first, w_expert_gu_second,
    w_expert_down, w_expert_down_first, w_expert_down_second,
    norm_gains, norm_gains_first, norm_gains_second,
    conv_params, conv_params_first, conv_params_second,
    head_params, head_params_first, head_params_second,
    mixer_gain, mixer_gain_first, mixer_gain_second,
):
    groups = lax.axis_size("expert")
    copies = (lax.axis_size("zhi") * lax.axis_size("zlo") * lax.axis_size("core"))
    place = lax.axis_index("expert")
    tok = tokens.shape[0]
    length = tok * groups
    top = routes.shape[1]
    experts = w_router.shape[1]
    own_experts = w_expert_gu.shape[0]
    capacity = (4 * tok * top + 3 * experts - 1) // (3 * experts)
    inner = INNER // groups
    heads = HEADS // groups
    rows_in = w_in.shape[0]
    rows_out = w_out.shape[0]
    rows_sd = w_shared_down.shape[0]
    own_ff = SHARED_FF // groups
    per_pair = copies // groups
    conv_cols = inner + 2 * STATE
    body = 2 * inner + 2 * STATE

    w_in_low = w_in.astype(bf16)
    z_cols = w_in_low[:, :INNER].reshape(rows_in, groups, inner)
    x_cols = w_in_low[:, INNER : 2 * INNER].reshape(rows_in, groups, inner)
    bc_cols = jnp.broadcast_to(
        w_in_low[:, None, 2 * INNER : 2 * INNER + 2 * STATE], (rows_in, groups, 2 * STATE)
    )
    dt_cols = w_in_low[:, 2 * INNER + 2 * STATE :].reshape(rows_in, groups, heads)
    router_cols = jnp.broadcast_to(
        w_router.astype(bf16)[:, None], (rows_in, groups, experts)
    )
    fill = jnp.zeros((rows_in, groups, LANES - heads - experts), bf16)
    win_pieces = jnp.concatenate(
        [z_cols, x_cols, bc_cols, dt_cols, router_cols, fill], axis=2
    ).transpose(1, 0, 2)
    win_rows = swap(win_pieces, "expert").reshape(groups * rows_in, -1)
    down_own = jnp.concatenate([w_out.astype(bf16), w_shared_down.astype(bf16)], axis=0)
    win = lax.all_gather(win_rows, DP, axis=0, tiled=True)
    router = win[:, body + heads : body + heads + experts]
    both_all = spread(jnp.stack([tokens, cotangent]), "expert").transpose(1, 0, 2, 3)
    x_all = both_all[0].reshape(length, D)
    cot_all = both_all[1].reshape(length, D)
    routes_two = spread(jnp.stack([routes, to_partner(routes)]), "expert")
    routes_two = routes_two.transpose(1, 0, 2, 3).reshape(2 * length, top)

    rows_two = rows_out + rows_sd
    down_rows = lax.all_gather(down_own, DP, axis=0, tiled=False)
    sd = down_rows[:, rows_out:].reshape(own_ff, D)
    wout = (
        swap(down_rows[:, :rows_out].reshape(groups, per_pair * rows_out, D), "expert")
        .reshape(groups, per_pair, rows_out, D)
        .transpose(1, 0, 2, 3)
        .reshape(inner, D)
    )
    sgu_pieces = (
        w_shared_gu.astype(bf16)
        .reshape(rows_in, 2, copies, groups, rows_sd)
        .transpose(3, 0, 1, 2, 4)
        .reshape(groups, rows_in, 2 * own_ff)
    )
    sgu = lax.all_gather(
        swap(sgu_pieces, "expert").reshape(groups * rows_in, 2 * own_ff), DP, axis=0, tiled=True
    )

    half = lax.axis_index("zhi")
    held = own_experts // 2
    rows_egu, rows_ed = w_expert_gu.shape[1], w_expert_down.shape[1]

    def halves(shard):
        kept = lax.dynamic_slice_in_dim(shard, half * held, held, axis=0)
        sent = lax.dynamic_slice_in_dim(shard, (1 - half) * held, held, axis=0)
        return kept, sent

    def gathered(kept, came):
        both = jnp.where(half == 0, jnp.stack([kept, came], 1), jnp.stack([came, kept], 1))
        return lax.all_gather(both, MATES, axis=0, tiled=False)

    egu_own, ed_own = w_expert_gu.astype(bf16), w_expert_down.astype(bf16)
    win, wout, routes_two, x_all, egu_own, ed_own, cot_own = lax.optimization_barrier(
        (win, wout, routes_two, x_all, egu_own, ed_own, cotangent)
    )
    cot_other = to_partner(cot_own)
    egu_kept, egu_sent = halves(egu_own)
    ed_kept, ed_sent = halves(ed_own)
    egu_came = to_partner(egu_sent)
    ed_came = to_partner(ed_sent)

    positions = jnp.arange(length, dtype=jnp.int32)
    starts = jnp.cumsum(lengths[0]) - lengths[0]
    doc_index = jnp.sum((starts[None, :] <= positions[:, None]).astype(jnp.int32), axis=1) - 1
    earlier_doc = [
        jnp.concatenate([jnp.full((offset,), -1, jnp.int32), doc_index[: length - offset]])
        for offset in range(CONV)
    ]
    masks = jnp.stack([(earlier == doc_index).astype(f32) for earlier in earlier_doc], axis=1)
    masks = jnp.pad(masks, ((0, 0), (0, LANES - CONV)))
    doc_col, doc_row = doc_index[:, None], doc_index[None, :]

    own_x = place * inner
    conv_own = jnp.concatenate(
        [
            lax.dynamic_slice_in_dim(conv_params, own_x, inner, axis=1),
            conv_params[:, INNER:],
        ],
        axis=1,
    )
    head_own = lax.dynamic_slice_in_dim(head_params, place * heads, heads, axis=1)
    gain_own = lax.dynamic_slice_in_dim(mixer_gain, own_x, inner, axis=0)

    conv_pad = jnp.pad(conv_own, ((0, 3), (0, 0)))
    rate_abs = jnp.exp(head_own[0])
    head_rows = jnp.pad(jnp.stack([rate_abs, head_own[1]]), ((0, 6), (0, LANES - heads)))
    col_rows = jnp.pad(
        jnp.stack([gain_own, jnp.repeat(head_own[2], HEAD_DIM)]), ((0, 6), (0, 0))
    )
    gain_rows = jnp.pad(norm_gains, ((0, 6), (0, 0)))

    square = ((length, length), f32)
    lane_rows = ((length, LANES), f32)
    lane_cols = ((LANES, length), f32)
    packed, dt_raw, full_y, res_part = vmem_call(
        forward_kernel,
        [
            jax.ShapeDtypeStruct((length, body), bf16),
            jax.ShapeDtypeStruct((length, LANES), f32),
            jax.ShapeDtypeStruct((length, inner), bf16),
            jax.ShapeDtypeStruct((length, D + LANES), bf16),
        ],
        [((length, D), bf16), square, square, lane_rows, lane_cols, ((length, inner), bf16),
         lane_rows],
        x_all, win, gain_rows, conv_pad, masks, head_rows, col_rows, doc_col, doc_row, wout,
    )
    pairs = pltpu.SemaphoreType.DMA
    payload = ((tok, D + LANES), bf16)
    hidden, mixer_res, two_own = remote_call(
        hidden_kernel, 0,
        [
            jax.ShapeDtypeStruct((tok, D), f32),
            jax.ShapeDtypeStruct((tok, D), f32),
            jax.ShapeDtypeStruct((tok, D + LANES), bf16),
        ],
        [((groups - 1, tok, D + LANES), bf16)],
        [pairs((groups - 1,)), pairs((groups - 1,))],
        res_part, tokens, gain_rows,
    )
    egu_came, ed_came, cot_other, two_own = lax.optimization_barrier(
        (egu_came, ed_came, cot_other, two_own)
    )
    egu = gathered(egu_kept, egu_came)
    ed = gathered(ed_kept, ed_came)
    gathered_shape = jax.ShapeDtypeStruct((groups, tok, D + LANES), bf16)
    got, other_two = remote_call(
        share_kernel, 1, [gathered_shape] * 2, [payload],
        [pairs((2 * groups - 1,)), pairs((2 * groups - 1,)), pairs((2,))],
        two_own,
    )
    got = got.reshape(length, -1)
    other_two = other_two.reshape(length, -1)
    scale_words = got[:, D:]
    cot_other = spread(cot_other, "expert").reshape(length, D)

    blocks = 2 * groups
    expert_at = (place * own_experts + half * held).reshape(1)
    two_rows = jnp.concatenate([got, other_two], axis=0)
    cot_two = jnp.concatenate([cot_all, cot_other], axis=0)
    router_lanes = jnp.pad(router, ((0, 0), (0, LANES - experts)))
    slot_rows = blocks * capacity

    def by_block(*shape):
        return pl.BlockSpec(shape, lambda b: (b,) + (0,) * (len(shape) - 1))

    def fixed(*shape):
        return pl.BlockSpec(shape, lambda b: (0,) * len(shape))

    slot_spec = pl.BlockSpec((held, capacity, D), lambda b: (0, b, 0))
    in_smem = pl.BlockSpec(memory_space=pltpu.SMEM)
    slot_shape = jax.ShapeDtypeStruct((held, slot_rows, D), bf16)
    slot_in, slot_top, slot_grad, weights, pick = grid_call(
        route_kernel, blocks,
        [by_block(tok, D + LANES), by_block(tok, D), by_block(tok, top), fixed(D, LANES), in_smem],
        [slot_spec] * 3 + [by_block(tok, LANES), by_block(1, tok, held * capacity)],
        [slot_shape] * 3
        + [
            jax.ShapeDtypeStruct((2 * length, LANES), f32),
            jax.ShapeDtypeStruct((blocks, tok, held * capacity), bf16),
        ],
        [],
        two_rows, cot_two, routes_two, router_lanes, expert_at,
    )
    shared_out, shared_back, grad_sgu, grad_sd = vmem_call(
        shared_kernel,
        [
            jax.ShapeDtypeStruct((length, D), bf16),
            jax.ShapeDtypeStruct((length, D), bf16),
            jax.ShapeDtypeStruct((D, 2 * own_ff), bf16),
            jax.ShapeDtypeStruct((own_ff, D), bf16),
        ],
        [((length, own_ff), bf16), ((length, 2 * own_ff), bf16)],
        got, cot_all, sgu, sd,
    )

    mates = copies // 2
    packed_rows = 2 * rows_egu + rows_ed * D // EXPERT_FF

    def by_expert(*shape):
        return pl.BlockSpec((1,) + shape, lambda e: (e,) + (0,) * len(shape))

    def weight_spec(rows, columns):
        return pl.BlockSpec((mates, 1, 2, rows, columns), lambda e: (0, e, 0, 0, 0))

    slot_out, slot_back, slot_q, expert_grads = grid_call(
        expert_kernel, held,
        [by_expert(slot_rows, D)] * 3
        + [weight_spec(rows_egu, 2 * EXPERT_FF), weight_spec(rows_ed, D)],
        [by_expert(slot_rows, D)] * 2
        + [
            by_expert(slot_rows, LANES),
            pl.BlockSpec((mates, 2, 1, packed_rows, EXPERT_FF), lambda e: (0, 0, e, 0, 0)),
        ],
        [slot_shape] * 2
        + [
            jax.ShapeDtypeStruct((held, slot_rows, LANES), f32),
            jax.ShapeDtypeStruct((mates, 2, held, packed_rows, EXPERT_FF), bf16),
        ],
        [((slot_rows, EXPERT_FF), bf16), ((slot_rows, 2 * EXPERT_FF), bf16)],
        slot_in, slot_top, slot_grad, egu, ed,
    )
    own_spec = pl.BlockSpec((tok, D), lambda b: (jnp.minimum(b, groups - 1), 0))
    out_parts, back_parts = grid_call(
        combine_kernel, blocks,
        [
            by_block(1, tok, held * capacity), by_block(tok, LANES), in_smem, slot_spec, slot_spec,
            pl.BlockSpec((held, capacity, LANES), lambda b: (0, b, 0)), own_spec, own_spec,
        ],
        [by_block(tok, D), by_block(tok, D + LANES)],
        [
            jax.ShapeDtypeStruct((2 * length, D), bf16),
            jax.ShapeDtypeStruct((2 * length, D + LANES), bf16),
        ],
        [],
        pick, weights, expert_at, slot_out, slot_back, slot_q, shared_out, shared_back,
    )

    weights_tok = lax.dynamic_slice_in_dim(weights, place * tok, tok, axis=0)
    hidden_all, grad_hidden, grad_logits, gain_two = remote_call(
        functools.partial(back_kernel, own_experts=own_experts), 2,
        [
            gathered_shape,
            jax.ShapeDtypeStruct((tok, D), f32),
            jax.ShapeDtypeStruct((tok, LANES), bf16),
            jax.ShapeDtypeStruct((8, D), f32),
        ],
        [((groups - 1, tok, D + LANES), bf16)] * 2 + [payload] * 3,
        [pairs((3 * groups - 2,)), pairs((3 * groups - 2,)), pairs(())],
        back_parts, hidden, mixer_res, cotangent, weights_tok, router_lanes, gain_rows,
    )
    hidden_all = hidden_all.reshape(length, -1)
    grad_gain_two = gain_two[0]
    grad_router = dot_tn(two_own[:, :D], grad_logits[:, :experts])

    out_parts, hidden_all = lax.optimization_barrier((out_parts, hidden_all))
    out_own, out_other = out_parts[:length], out_parts[length:]
    other_out = swap(out_other.reshape(groups, tok, D), "expert")
    other_out = to_partner(jnp.sum(other_out.astype(f32), axis=0).astype(bf16))
    own_out = swap(out_own.reshape(groups, tok, D), "expert")

    expert_mine = lax.psum_scatter(
        expert_grads.reshape(-1, EXPERT_FF), MATES, scatter_dimension=0, tiled=True
    ).reshape(expert_grads.shape[1:])

    gate_z = packed[:, :inner].astype(f32)
    mixer_act = (
        full_y.astype(f32) * jax.nn.silu(gate_z) * word_sum(scale_words) * gain_own
    ).astype(bf16)
    grad_wout = dot_tn(mixer_act, hidden_all[:, :D]).astype(bf16)
    wout_send = (
        grad_wout.reshape(per_pair, groups, rows_out, D)
        .transpose(1, 0, 2, 3)
        .reshape(groups, per_pair * rows_out, D)
    )
    wout_got = swap(wout_send, "expert").reshape(copies, rows_out, D)
    grad_proj, conv_grads, col_grads, head_grads = vmem_call(
        backward_kernel,
        [
            jax.ShapeDtypeStruct((length, body + LANES), bf16),
            jax.ShapeDtypeStruct((8, conv_cols), f32),
            jax.ShapeDtypeStruct((8, inner), f32),
            jax.ShapeDtypeStruct((8, LANES), f32),
        ],
        [square, square, lane_rows, lane_cols, square, lane_rows, lane_cols, lane_rows, lane_rows,
         ((length, LANES), bf16)],
        hidden_all, scale_words, wout, conv_pad, masks, head_rows, col_rows, doc_col, doc_row,
        packed, dt_raw, full_y,
    )
    conv_grads = conv_grads[: CONV + 1]
    grad_gain_mix = col_grads[0]
    grad_skip = jnp.sum(col_grads[1].reshape(heads, HEAD_DIM), axis=1)
    grad_log_rate = head_grads[0, :heads]
    grad_bias = head_grads[1, :heads]
    grad_proj, expert_mine = lax.optimization_barrier((grad_proj, expert_mine))
    inputs = x_all.astype(f32)
    normed_one = inputs * rms_scale(inputs)
    normed = (normed_one * norm_gains[0]).astype(bf16)
    grad_win = (
        dot_tn(normed, grad_proj)
        + jnp.pad(grad_router, ((0, 0), (body + heads, LANES - heads - experts)))
    ).astype(bf16)
    rows_sgu = groups * rows_in * 2 * own_ff // D
    second = jnp.concatenate(
        [wout_got, grad_sd.reshape(copies, rows_sd, D), sgu_rows(grad_sgu)], axis=1
    )
    second = jnp.pad(second, ((0, 0), (0, groups * rows_in - second.shape[1]), (0, 0)))
    dense = jnp.concatenate(
        [grad_win.reshape(copies, groups * rows_in, -1), second], axis=2
    )
    dense_mine = lax.psum_scatter(dense, DP, scatter_dimension=0, tiled=True)[0]
    one_part = dot_nt(grad_proj, win)
    grad_gain_one = jnp.sum(one_part * normed_one, axis=0)
    one_low = one_part.astype(bf16)
    one_low, expert_mine, own_out, other_out = lax.optimization_barrier(
        (one_low, expert_mine, own_out, other_out)
    )
    got = swap(one_low.reshape(groups, tok, D), "expert")
    output = (
        hidden + jnp.sum(own_out.astype(f32), axis=0) + other_out.astype(f32)
    ).astype(bf16)
    kept = lax.dynamic_index_in_dim(expert_mine, half, 0, False)
    came = to_partner(lax.dynamic_index_in_dim(expert_mine, 1 - half, 0, False))
    expert_sum = jnp.where(
        half == 0, jnp.concatenate([kept, came], 0), jnp.concatenate([came, kept], 0)
    )
    sum_egu = jnp.concatenate(
        [expert_sum[:, :rows_egu], expert_sum[:, rows_egu : 2 * rows_egu]], axis=2
    ).astype(f32)
    sum_ed = jnp.concatenate(
        [
            expert_sum[:, 2 * rows_egu + k * rows_ed : 2 * rows_egu + (k + 1) * rows_ed]
            for k in range(D // EXPERT_FF)
        ],
        axis=2,
    ).astype(f32)

    grad_norm_one = jnp.sum(got.astype(f32), axis=0)
    own_in = tokens.astype(f32)
    own_scale = rms_scale(own_in)
    grad_tokens = (
        grad_hidden + norm_back(grad_norm_one, own_in * own_scale, own_scale, norm_gains[0])
    ).astype(bf16)

    pieces = [
        conv_grads[:, :inner].reshape(-1),
        grad_gain_mix,
        grad_log_rate,
        grad_bias,
        grad_skip,
        conv_grads[:, inner:].reshape(-1),
        grad_gain_one,
        grad_gain_two,
    ]
    sizes = [piece.size for piece in pieces]
    total = sum(sizes)
    unit = copies * LANES
    small = jnp.pad(jnp.concatenate(pieces), (0, -total % unit)).reshape(copies, -1)
    small = jnp.sum(swap(small, DP), axis=0)
    small = spread(small, ("expert",) + DP).reshape(groups, -1)
    parts = []
    start = 0
    for size in sizes:
        parts.append(small[:, start : start + size])
        start += size
    sum_conv = jnp.concatenate(
        [
            parts[0].reshape(groups, CONV + 1, inner).transpose(1, 0, 2).reshape(CONV + 1, INNER),
            jnp.sum(parts[5], axis=0).reshape(CONV + 1, 2 * STATE),
        ],
        axis=1,
    )
    sum_mixer = parts[1].reshape(INNER)
    sum_head = jnp.stack([parts[2].reshape(HEADS), parts[3].reshape(HEADS), parts[4].reshape(HEADS)])
    sum_gains = jnp.stack([jnp.sum(parts[6], axis=0), jnp.sum(parts[7], axis=0)])

    win_mine = dense_mine[:, : body + LANES]
    second_mine = dense_mine[:, body + LANES :]
    sum_out = second_mine[:rows_out].astype(f32)
    sum_sd = second_mine[rows_out:rows_two].astype(f32)
    sgu_mine = jnp.concatenate(
        [
            second_mine[rows_two : rows_two + rows_sgu, k * 2 * own_ff : (k + 1) * 2 * own_ff]
            for k in range(D // (2 * own_ff))
        ],
        axis=0,
    )
    sum_sgu = (
        swap(sgu_mine.reshape(groups, rows_in, 2 * own_ff), "expert")
        .reshape(groups, rows_in, 2, copies, rows_sd)
        .transpose(1, 2, 3, 0, 4)
        .reshape(rows_in, 2 * SHARED_FF)
        .astype(f32)
    )
    win_got = swap(win_mine.reshape(groups, rows_in, -1), "expert").astype(f32)

    def laid(start, size):
        return win_got[:, :, start : start + size].transpose(1, 0, 2).reshape(rows_in, -1)

    sum_in = jnp.concatenate(
        [
            laid(0, inner),
            laid(inner, inner),
            jnp.sum(win_got[:, :, 2 * inner : body], axis=0),
            laid(body, heads),
        ],
        axis=1,
    )
    sum_router = jnp.sum(win_got[:, :, body + heads : body + heads + experts], axis=0)

    up_in = adam_step(w_in, w_in_first, w_in_second, sum_in)
    up_out = adam_step(w_out, w_out_first, w_out_second, sum_out)
    up_router = adam_step(w_router, w_router_first, w_router_second, sum_router)
    up_sgu = adam_step(w_shared_gu, w_shared_gu_first, w_shared_gu_second, sum_sgu)
    up_sd = adam_step(w_shared_down, w_shared_down_first, w_shared_down_second, sum_sd)
    up_egu = adam_step(w_expert_gu, w_expert_gu_first, w_expert_gu_second, sum_egu)
    up_ed = adam_step(w_expert_down, w_expert_down_first, w_expert_down_second, sum_ed)
    up_gains = adam_step(norm_gains, norm_gains_first, norm_gains_second, sum_gains)
    up_conv = adam_step(conv_params, conv_params_first, conv_params_second, sum_conv)
    up_head = adam_step(head_params, head_params_first, head_params_second, sum_head)
    up_mixer = adam_step(mixer_gain, mixer_gain_first, mixer_gain_second, sum_mixer)
    large = (up_in, up_out, up_router, up_sgu, up_sd, up_egu, up_ed)
    little = (up_gains, up_conv, up_head, up_mixer)
    return (
        (output, grad_tokens)
        + tuple(part for one in large for part in one[:4])
        + tuple(part for one in little for part in (one[0], one[4], one[2], one[3]))
    )


def solution(mesh):
    copies, groups = mesh.devices.shape
    split = Mesh(mesh.devices.reshape(2, copies // 4, 2, groups), ALL)
    rows = P(ALL, None)
    expert_rows = P("expert", DP, None)
    whole = P()
    return jax.shard_map(
        on_device,
        mesh=split,
        in_specs=(rows, rows, P(DP, None), rows)
        + (rows,) * 15
        + (expert_rows,) * 6
        + (whole,) * 12,
        out_specs=(rows, rows) + (rows,) * 20 + (expert_rows,) * 8 + (whole,) * 16,
        check_vma=False,
    )
```

```python
import functools
import math

import jax
import jax.numpy as jnp
from jax import lax
from jax.experimental import pallas as pl
from jax.experimental.pallas import tpu as pltpu
from jax.sharding import Mesh
from jax.sharding import PartitionSpec as P

D = 1536
HEADS = 48
HEAD_DIM = 64
STATE = 128
CONV = 4
EXPERT_FF = 512
SHARED_FF = 1024
STEP = 3
INNER = 3072
CONV_DIM = 3328
LANES = 128
CHUNK = 384

DP = ("zhi", "zlo", "core")
MATES = ("zlo", "core")
ALL = DP + ("expert",)

norm_eps = 1e-05
beta_one = 0.9
beta_two = 0.95
adam_eps = 1e-08
learn_rate = 0.02
decay_rate = 0.1
highest = lax.Precision.HIGHEST
bf16 = jnp.bfloat16
f32 = jnp.float32


def dot(left, right):
    return jnp.dot(left, right, preferred_element_type=f32)


def dot_nt(left, right):
    return lax.dot_general(left, right, (((1,), (1,)), ((), ())), preferred_element_type=f32)


def dot_tn(left, right):
    return lax.dot_general(left, right, (((0,), (0,)), ((), ())), preferred_element_type=f32)


def swap(pieces, axis):
    return lax.all_to_all(pieces, axis, split_axis=0, concat_axis=0, tiled=True)


def spread(block, axis):
    axes = (axis,) if isinstance(axis, str) else axis
    count = math.prod(lax.axis_size(one) for one in axes)
    return swap(jnp.broadcast_to(block[None], (count,) + block.shape), axis)


def to_partner(value):
    return lax.ppermute(value, "zhi", [(0, 1), (1, 0)])


def rms_scale(values):
    return lax.rsqrt(jnp.mean(values * values, axis=-1, keepdims=True) + norm_eps)


def silu_slope(values):
    sigmoid_value = jax.nn.sigmoid(values)
    return sigmoid_value * (1.0 + values * (1.0 - sigmoid_value))


def norm_back(grad_norm, unit_rows, scale_rows, gain):
    scaled = grad_norm * gain
    return scale_rows * (scaled - unit_rows * jnp.mean(scaled * unit_rows, axis=-1, keepdims=True))


def adam_step(weight, moment_one, moment_two, gradient):
    moment_one = beta_one * moment_one + (1.0 - beta_one) * gradient
    moment_two = beta_two * moment_two + (1.0 - beta_two) * gradient * gradient
    fixed_one = 1.0 - beta_one**STEP
    fixed_two = 1.0 - beta_two**STEP
    change = (
        moment_one / fixed_one / (jnp.sqrt(moment_two / fixed_two) + adam_eps) + decay_rate * weight
    )
    moved = -learn_rate * change
    return (gradient, weight + moved, moment_one, moment_two, moved)


def split_words(value):
    high = value.astype(bf16)
    rest = value - high.astype(f32)
    mid = rest.astype(bf16)
    low = (rest - mid.astype(f32)).astype(bf16)
    return high, mid, low


def join_words(words):
    return words[0].astype(f32) + words[1].astype(f32) + words[2].astype(f32)


def conv_rows(block, masks, params):
    total = params[CONV : CONV + 1] + params[0:1] * block
    for offset in range(1, CONV):
        total = total + params[offset : offset + 1] * (
            pltpu.roll(block, offset, 0) * masks[:, offset : offset + 1]
        )
    return total


def conv_rows_back(grad, block, masks, params):
    length = block.shape[0]
    taps = [jnp.sum(grad * block, axis=0, keepdims=True)]
    rows = params[0:1] * grad
    for offset in range(1, CONV):
        masked = grad * masks[:, offset : offset + 1]
        taps.append(jnp.sum(masked * pltpu.roll(block, offset, 0), axis=0, keepdims=True))
        rows = rows + pltpu.roll(params[offset : offset + 1] * masked, length - offset, 0)
    taps.append(jnp.sum(grad, axis=0, keepdims=True))
    return rows, taps


def dot_words(exact, value, contract):
    total = None
    for word in split_words(value):
        part = lax.dot_general(exact, word, (contract, ((), ())), preferred_element_type=f32)
        total = part if total is None else total + part
    return total


def dot_words_left(value, exact):
    total = None
    for word in split_words(value):
        part = jnp.dot(word, exact, preferred_element_type=f32)
        total = part if total is None else total + part
    return total


def softplus(value):
    return jnp.maximum(value, 0.0) + jnp.log1p(jnp.exp(-jnp.abs(value)))


def head_lanes(pair, transposed=False):
    rows = lax.broadcasted_iota(jnp.int32, (LANES, LANES), 0)
    lanes = lax.broadcasted_iota(jnp.int32, (LANES, LANES), 1)
    if transposed:
        rows, lanes = lanes, rows
    return (rows == 2 * pair + lanes // HEAD_DIM).astype(f32).astype(bf16)


def lane_of(matrix, lane):
    lanes = lax.broadcasted_iota(jnp.int32, matrix.shape, 1)
    return jnp.sum(jnp.where(lanes == lane, matrix, 0.0), axis=1, keepdims=True)


def scan_setup(dt_ref, packed_ref, conv_ref, masks, head_ref, doc_col, doc_row, inner,
               neg_ref, scores_ref, cum_ref, cum_t_ref):
    length = dt_ref.shape[0]
    pre_step = dt_ref[...] + head_ref[1:2]
    dt_step = softplus(pre_step)
    log_decay = -head_ref[0:1] * dt_step
    at = lax.broadcasted_iota(jnp.int32, (length, length), 0)
    to = lax.broadcasted_iota(jnp.int32, (length, length), 1)
    usable = (doc_col == doc_row) & (at >= to)
    neg_ref[...] = jnp.where(usable, 0.0, -1e30)
    exact = usable.astype(f32).astype(bf16)
    cum_ref[...] = dot_words(exact, log_decay, ((1,), (0,)))
    cum_t_ref[...] = cum_ref[...].T
    start = 2 * inner
    b_in = packed_ref[:, start : start + STATE].astype(f32)
    c_in = packed_ref[:, start + STATE : start + 2 * STATE].astype(f32)
    b_out = conv_rows(b_in, masks, conv_ref[:, inner : inner + STATE])
    c_out = conv_rows(c_in, masks, conv_ref[:, inner + STATE : inner + 2 * STATE])
    b_low = jax.nn.silu(b_out).astype(bf16)
    c_low = jax.nn.silu(c_out).astype(bf16)
    scores_ref[...] = dot_nt(c_low, b_low)
    return pre_step, dt_step, log_decay, exact, b_out, c_out, b_low, c_low


def pair_slices(pair, inner):
    at = pl.ds(pl.multiple_of(pair * LANES, LANES), LANES)
    x_at = pl.ds(pl.multiple_of(inner + pair * LANES, LANES), LANES)
    return at, x_at


def forward_kernel(x_ref, win_ref, gain_ref, conv_ref, masks_ref, head_ref, cols_ref, doc_col_ref,
                   doc_row_ref, wout_ref, gu_ref, gu_sent_ref, cot_ref, cot_came_ref,
                   packed_ref, dt_ref, y_ref, out_ref, gu_all_ref, gu_came_ref, cot_two_ref,
                   normed_ref, neg_ref, scores_ref, cum_ref, cum_t_ref, act_ref, square_ref,
                   send_sems, recv_sems, mate_send, mate_recv, mate_local, local_sems):
    greet(group_ids() + near_ids())
    count, me, _ = peers()
    sems = (send_sems, recv_sems)
    over = remote(gu_sent_ref, gu_came_ref, sems, 0, partner_id())
    weights = MateSpread(gu_ref, gu_all_ref, (mate_send, mate_recv), 0, mate_local)
    cots = [
        pltpu.make_async_copy(cot_ref, cot_two_ref.at[0], local_sems.at[0]),
        pltpu.make_async_copy(cot_came_ref, cot_two_ref.at[1, me], local_sems.at[1]),
    ]
    cots += spread_copies(cot_came_ref, cot_two_ref.at[1], sems, 1)
    over.start()
    weights.start()
    for copy in cots:
        copy.start()
    length = x_ref.shape[0]
    inner = wout_ref.shape[0]
    body = packed_ref.shape[1]
    step = 2 * LANES

    @pl.loop(0, length // LANES)
    def _(part):
        rows = pl.ds(pl.multiple_of(part * LANES, LANES), LANES)
        block = x_ref[rows, :].astype(f32)
        scale = lax.rsqrt(jnp.mean(block * block, axis=1, keepdims=True) + norm_eps)
        normed_ref[rows, :] = (block * scale * gain_ref[0:1]).astype(bf16)

    @pl.loop(0, body // step)
    def _(part):
        at = pl.ds(pl.multiple_of(part * step, step), step)
        packed_ref[:, at] = dot(normed_ref[...], win_ref[:, at]).astype(bf16)

    dt_ref[...] = dot(normed_ref[...], win_ref[:, body:])
    masks = masks_ref[...]
    _, dt_step, *_ = scan_setup(
        dt_ref, packed_ref, conv_ref, masks, head_ref, doc_col_ref[...], doc_row_ref[...], inner,
        neg_ref, scores_ref, cum_ref, cum_t_ref,
    )
    square_ref[...] = jnp.zeros_like(square_ref)
    lanes = lax.broadcasted_iota(jnp.int32, (LANES, LANES), 1)

    @pl.loop(0, inner // LANES)
    def _(pair):
        at, x_at = pair_slices(pair, inner)
        values = jax.nn.silu(conv_rows(packed_ref[:, x_at].astype(f32), masks, conv_ref[:, at]))
        dt_wide = dot_words_left(dt_step, head_lanes(pair))
        scaled = (values * dt_wide).astype(bf16)
        cum_cols = [lane_of(cum_ref[...], 2 * pair + k) for k in range(2)]
        cum_rows = [cum_t_ref[pl.ds(2 * pair + k, 1), :] for k in range(2)]
        outs = []
        for part in range(length // LANES):
            rows = slice(part * LANES, (part + 1) * LANES)
            wide = (part + 1) * LANES
            pieces = []
            for k in range(2):
                decay = jnp.exp(cum_cols[k][rows] - cum_rows[k][:, :wide] + neg_ref[rows, :wide])
                mixed = (decay * scores_ref[rows, :wide]).astype(bf16)
                pieces.append(dot(mixed, scaled[:wide]))
            outs.append(jnp.where(lanes < HEAD_DIM, pieces[0], pieces[1]))
        full_y = jnp.concatenate(outs, axis=0) + cols_ref[1:2, at] * values
        y_ref[:, at] = full_y.astype(bf16)
        gated = full_y * jax.nn.silu(packed_ref[:, at].astype(f32))
        square_ref[...] += gated * gated
        act_ref[:, at] = (gated * cols_ref[0:1, at]).astype(bf16)

    @pl.loop(0, D // step)
    def _(part):
        at = pl.ds(pl.multiple_of(part * step, step), step)
        out_ref[:, at] = dot(act_ref[...], wout_ref[:, at]).astype(bf16)

    squares = jnp.sum(square_ref[...], axis=1, keepdims=True)
    out_ref[:, D:] = word_lanes(squares)
    weights.forward()
    for copy in cots:
        copy.wait()
    over.wait()
    weights.finish()


def word_lanes(column):
    lanes = lax.broadcasted_iota(jnp.int32, (column.shape[0], LANES), 1)
    words = [word.astype(f32) for word in split_words(column)]
    row = jnp.where(lanes == 0, words[0], jnp.where(lanes == 1, words[1], words[2]))
    return jnp.where(lanes < 3, row, 0.0).astype(bf16)


def word_sum(words):
    return words[:, 0:1].astype(f32) + words[:, 1:2].astype(f32) + words[:, 2:3].astype(f32)


def backward_kernel(hid_ref, scale_ref, wout_ref, conv_ref, masks_ref, head_ref, cols_ref,
                    doc_col_ref, doc_row_ref, packed_ref, dt_ref, y_ref, sums_ref, came_one_ref, out_ref,
                    proj_ref, conv_grad_ref, cols_grad_ref, head_grad_ref, total_ref, wout_send_ref,
                    out_own_ref, out_send_ref,
                    neg_ref, scores_ref, cum_ref, cum_t_ref, grad_scores_ref, row_ref, col_ref,
                    step_ref, scaled_ref, low_ref, wout_grad_ref, theirs_ref, out_got_ref, out_mine_ref, send_sem, recv_sem, out_send, out_recv,
                    out_local):
    greet(group_ids() + [partner_id()])
    tok = out_own_ref.shape[0]
    count = lax.axis_size("expert")
    out_sems = (out_send, out_recv)
    rows_all = out_ref.shape[0] // 2
    out_copies = reduce_copies(out_ref, out_got_ref.at[0], out_sems, 0, tok, rows_all)
    out_copies += reduce_copies(out_ref, out_got_ref.at[1], out_sems, count - 1, tok, 0)
    mine = pl.ds(pl.multiple_of(lax.axis_index("expert") * tok, tok), tok)
    yours = pl.ds(pl.multiple_of(rows_all + lax.axis_index("expert") * tok, tok), tok)
    out_copies += [
        pltpu.make_async_copy(out_ref.at[yours], out_mine_ref.at[0], out_local.at[0]),
        pltpu.make_async_copy(out_ref.at[mine], out_mine_ref.at[1], out_local.at[1]),
    ]
    for copy in out_copies:
        copy.start()
    half = lax.axis_index("zhi")
    held = sums_ref.shape[0]
    across = pltpu.make_async_remote_copy(
        src_ref=sums_ref.at[1, 1 - half], dst_ref=theirs_ref, send_sem=send_sem,
        recv_sem=recv_sem, device_id=partner_id(), device_id_type=pl.DeviceIdType.MESH,
    )
    across.start()
    length = dt_ref.shape[0]
    inner = wout_ref.shape[0]
    body = packed_ref.shape[1]
    scale_mix = word_sum(scale_ref[...])

    @pl.loop(0, inner // LANES)
    def _(pair):
        at, _ = pair_slices(pair, inner)
        gated = y_ref[:, at].astype(f32) * jax.nn.silu(packed_ref[:, at].astype(f32))
        act = (gated * scale_mix * cols_ref[0:1, at]).astype(bf16)
        wout_grad_ref[at, :] = dot_tn(act, hid_ref[:, :D]).astype(bf16)

    owners, rows_out, _ = wout_send_ref.shape
    real = inner // owners
    for k in range(owners):
        wout_send_ref[k, :real, :] = wout_grad_ref[k * real : (k + 1) * real, :]
        if real < rows_out:
            wout_send_ref[k, real:, :] = jnp.zeros((rows_out - real, D), bf16)
    for e in range(held):
        total_ref[half * held + e] = sums_ref[e, half]
    total_ref[(1 - half) * held] = came_one_ref[...]
    masks = masks_ref[...]
    pre_step, dt_step, log_decay, exact, b_out, c_out, b_low, c_low = scan_setup(
        dt_ref, packed_ref, conv_ref, masks, head_ref, doc_col_ref[...], doc_row_ref[...], inner,
        neg_ref, scores_ref, cum_ref, cum_t_ref,
    )
    grad_scores_ref[...] = jnp.zeros_like(grad_scores_ref)
    row_ref[...] = jnp.zeros_like(row_ref)
    col_ref[...] = jnp.zeros_like(col_ref)
    step_ref[...] = jnp.zeros_like(step_ref)
    conv_grad_ref[...] = jnp.zeros_like(conv_grad_ref)
    cols_grad_ref[...] = jnp.zeros_like(cols_grad_ref)
    head_grad_ref[...] = jnp.zeros_like(head_grad_ref)
    row_mean = word_sum(hid_ref[:, D:])
    lanes_all = lax.broadcasted_iota(jnp.int32, (length, LANES), 1)
    lanes = lax.broadcasted_iota(jnp.int32, (LANES, LANES), 1)

    @pl.loop(0, inner // LANES)
    def _(pair):
        at, x_at = pair_slices(pair, inner)
        grad_act = dot_nt(hid_ref[:, :D], wout_ref[at, :])
        conv_in = packed_ref[:, x_at].astype(f32)
        conv_out = conv_rows(conv_in, masks, conv_ref[:, at])
        values = jax.nn.silu(conv_out)
        gate_z = packed_ref[:, at].astype(f32)
        gate_act = jax.nn.silu(gate_z)
        full_y = y_ref[:, at].astype(f32)
        normed_mix = full_y * gate_act * scale_mix
        gain = cols_ref[0:1, at]
        skip = cols_ref[1:2, at]
        cols_grad_ref[0:1, at] = jnp.sum(grad_act * normed_mix, axis=0, keepdims=True)
        grad_gated = scale_mix * (grad_act * gain - normed_mix * row_mean)
        grad_y = grad_gated * gate_act
        proj_ref[:, at] = (grad_gated * full_y * silu_slope(gate_z)).astype(bf16)
        cols_grad_ref[1:2, at] = jnp.sum(grad_y * values, axis=0, keepdims=True)
        dt_wide = dot_words_left(dt_step, head_lanes(pair))
        scaled_low = (values * dt_wide).astype(bf16)
        low_ref[...] = grad_y.astype(bf16)
        scaled_ref[...] = jnp.zeros_like(scaled_ref)
        for k in range(2):
            head = 2 * pair + k
            cum_col = lane_of(cum_ref[...], head)
            cum_row = cum_t_ref[pl.ds(head, 1), :]
            for part in range(length // LANES):
                rows = slice(part * LANES, (part + 1) * LANES)
                wide = (part + 1) * LANES
                decay = jnp.exp(cum_col[rows] - cum_row[:, :wide] + neg_ref[rows, :wide])
                mixed = decay * scores_ref[rows, :wide]
                mine = jnp.where(lanes // HEAD_DIM == k, low_ref[rows, :].astype(f32), 0.0)
                mine = mine.astype(bf16)
                grad_mixed = dot_nt(mine, scaled_low[:wide])
                grad_scores_ref[rows, :wide] += grad_mixed * decay
                product = grad_mixed * mixed
                row_ref[rows, :] += jnp.where(
                    lanes == head, jnp.sum(product, axis=1, keepdims=True), 0.0
                )
                sums = jnp.sum(product, axis=0, keepdims=True)
                if part < length // LANES - 1:
                    sums = jnp.concatenate(
                        [sums, jnp.zeros((1, length - wide), f32)], axis=1
                    )
                col_sums = sums if part == 0 else col_sums + sums
                scaled_ref[:wide, :] += dot_tn(mixed.astype(bf16), mine)
            col_ref[pl.ds(head, 1), :] = col_sums
        grad_scaled = scaled_ref[...]
        step_ref[...] += dot_words_left(grad_scaled * values, head_lanes(pair, True))
        grad_values = grad_scaled * dt_wide + grad_y * skip
        grad_rows, taps = conv_rows_back(
            grad_values * silu_slope(conv_out), conv_in, masks, conv_ref[:, at]
        )
        proj_ref[:, x_at] = grad_rows.astype(bf16)
        for k in range(CONV + 1):
            conv_grad_ref[k : k + 1, at] = taps[k]

    grad_scores = grad_scores_ref[...].astype(bf16)
    for number, (grad, before) in enumerate(
        ((dot_tn(grad_scores, c_low), b_out), (dot(grad_scores, b_low), c_out))
    ):
        start = inner + number * STATE
        conv_in = packed_ref[:, inner + start : inner + start + STATE].astype(f32)
        grad_rows, taps = conv_rows_back(
            grad * silu_slope(before), conv_in, masks, conv_ref[:, start : start + STATE]
        )
        proj_ref[:, inner + start : inner + start + STATE] = grad_rows.astype(bf16)
        for k in range(CONV + 1):
            conv_grad_ref[k : k + 1, start : start + STATE] = taps[k]
    grad_cum = row_ref[...] - col_ref[...].T
    grad_decay = dot_words(exact, grad_cum, ((0,), (0,)))
    rate_abs = head_ref[0:1]
    grad_pre = (step_ref[...] - grad_decay * rate_abs) * jax.nn.sigmoid(pre_step)
    head_grad_ref[0:1] = jnp.sum(grad_decay * log_decay, axis=0, keepdims=True)
    head_grad_ref[1:2] = jnp.sum(grad_pre, axis=0, keepdims=True)
    proj_ref[:, body:] = grad_pre.astype(bf16)
    for copy in out_copies:
        copy.wait()
    totals = []
    for side in range(2):
        total = out_mine_ref[side].astype(f32)
        for number in range(count - 1):
            total = total + out_got_ref[side, number].astype(f32)
        totals.append(total)
    out_send_ref[...] = totals[0].astype(bf16)
    out_own_ref[...] = totals[1]
    across.wait()
    total_ref[(1 - half) * held + 1] = theirs_ref[...]


def route_kernel(two_ref, cot_ref, routes_ref, router_ref, ids_ref,
                 in_ref, top_ref, grad_ref, weights_ref, pick_ref, *, top_count, heads):
    tok = two_ref.shape[0]
    held, capacity, _ = in_ref.shape
    rows = two_ref[:, :D]
    logits = pltpu.roll(dot(rows, router_ref[...]), LANES - heads, 1)
    lanes = lax.broadcasted_iota(jnp.int32, (tok, LANES), 1)
    named = lanes < 0
    for k in range(top_count):
        named = named | (lanes == routes_ref[:, k : k + 1])
    top_logit = jnp.max(jnp.where(named, logits, -1e30), axis=1, keepdims=True)
    raised = jnp.where(named, jnp.exp(jnp.where(named, logits - top_logit, 0.0)), 0.0)
    weights = raised / jnp.sum(raised, axis=1, keepdims=True)
    weights_ref[...] = weights
    at = lax.broadcasted_iota(jnp.int32, (tok, tok), 0)
    to = lax.broadcasted_iota(jnp.int32, (tok, tok), 1)
    named_f = named.astype(f32)
    slot = dot((at > to).astype(f32).astype(bf16), named_f.astype(bf16))
    slots = lax.broadcasted_iota(jnp.int32, (tok, capacity), 1).astype(f32)
    picks = []
    for expert in range(held):
        lane = ids_ref[0] + expert
        mine = (lane_of(slot, lane) == slots) & (lane_of(named_f, lane) > 0.0)
        pick = mine.astype(f32).astype(bf16)
        picks.append(pick)
        in_ref[expert] = dot_tn(pick, rows).astype(bf16)
        top = dot_tn(pick, cot_ref[...])
        top_ref[expert] = top.astype(bf16)
        words = word_lanes(lane_of(weights, lane))
        slot_weight = jnp.sum(dot_tn(pick, words), axis=1, keepdims=True)
        grad_ref[expert] = (top * slot_weight).astype(bf16)
    pick_ref[0] = jnp.concatenate(picks, axis=1)


def expert_kernel(in_ref, top_ref, grad_ref, half_ref, gu_near_ref, gu_far_ref, down_near_ref,
                  down_far_ref, out_ref, back_ref, q_ref, sums_ref, mid_ref, act_ref):
    mates, _, rows_gu, _ = gu_near_ref.shape
    rows_down = down_near_ref.shape[2]
    shards = [(h, m) for h in range(2) for m in range(mates)]
    half = half_ref[0]
    sides = (
        (half, gu_near_ref, down_near_ref),
        (1 - half, gu_far_ref, down_far_ref),
    )

    def joined(ref, at, which=range(mates)):
        return jnp.concatenate([ref[m, 0, :, at] for m in which], axis=0)

    def block(place, size, offset=0):
        return pl.ds(pl.multiple_of(offset + place * size, LANES), size)

    wide = D // 2
    tall = EXPERT_FF // 2
    for place, _, down in sides:
        at = block(place, tall)
        up_at = block(place, tall, EXPERT_FF)
        gate = sum(
            dot(in_ref[0, :, block(side, wide)], joined(gu, at)) for side, gu, _ in sides
        )
        up = sum(
            dot(in_ref[0, :, block(side, wide)], joined(gu, up_at)) for side, gu, _ in sides
        )
        silu = jax.nn.silu(gate)
        mid_ref[:, at] = (silu * up).astype(bf16)
        grad_mid = dot_nt(grad_ref[0], joined(down, slice(None)))
        act_ref[:, at] = (grad_mid * up * silu_slope(gate)).astype(bf16)
        act_ref[:, up_at] = (grad_mid * silu).astype(bf16)
    step = 384
    each = step // rows_gu
    for side, gu, _ in sides:
        for part in range(wide // step):
            rows = joined(gu, slice(None), range(part * each, (part + 1) * each))
            at = pl.ds(pl.multiple_of(side * wide + part * step, LANES), step)
            back_ref[0, :, at] = dot_nt(act_ref[...], rows).astype(bf16)
    q = jnp.zeros((in_ref.shape[1], 1), f32)
    for part in range(D // step):
        at = slice(part * step, (part + 1) * step)
        rows = sum(dot(mid_ref[:, block(side, tall)], joined(down, at)) for side, _, down in sides)
        out_ref[0, :, at] = rows.astype(bf16)
        q = q + jnp.sum(rows * top_ref[0, :, at].astype(f32), axis=1, keepdims=True)
        chosen = shards[part * each : (part + 1) * each]
        for number in range(2):
            half_at = slice(number * EXPERT_FF, (number + 1) * EXPERT_FF)
            total = dot_tn(in_ref[0, :, at], act_ref[:, half_at]).astype(bf16)
            for k, (h, m) in enumerate(chosen):
                sums_ref[m, 0, h, number * rows_gu : (number + 1) * rows_gu, :] = total[
                    k * rows_gu : (k + 1) * rows_gu
                ]
    q_ref[0] = jnp.broadcast_to(q, q_ref.shape[1:])
    for part in range(D // EXPERT_FF):
        total = dot_tn(mid_ref[...], grad_ref[0, :, part * EXPERT_FF : (part + 1) * EXPERT_FF])
        total = total.astype(bf16)
        start = 2 * rows_gu + part * rows_down
        for k, (h, m) in enumerate(shards):
            sums_ref[m, 0, h, start : start + rows_down, :] = total[
                k * rows_down : (k + 1) * rows_down
            ]


def combine_kernel(pick_ref, weights_ref, ids_ref, out_ref, back_ref, q_ref, own_out_ref,
                   own_back_ref, mix_ref, rows_ref):
    held = out_ref.shape[0]
    capacity = out_ref.shape[1]
    block = pl.program_id(0)
    own = (block < pl.num_programs(0) // 2).astype(f32)
    picks = [pick_ref[0, :, e * capacity : (e + 1) * capacity] for e in range(held)]
    mix = own_out_ref[...].astype(f32) * own
    back = own_back_ref[...].astype(f32) * own
    lanes = lax.broadcasted_iota(jnp.int32, (pick_ref.shape[1], LANES), 1)
    words = jnp.zeros((pick_ref.shape[1], LANES), f32)
    for expert in range(held):
        weight = lane_of(weights_ref[...], ids_ref[0] + expert)
        mix = mix + weight * dot(picks[expert], out_ref[expert])
        back = back + dot(picks[expert], back_ref[expert])
        token_q = jnp.sum(dot(picks[expert], word_lanes(q_ref[expert, :, :1])), axis=1,
                          keepdims=True)
        for k, word in enumerate(split_words(token_q)):
            words = jnp.where(lanes == k * held + expert, word.astype(f32), words)
    mix_ref[...] = mix.astype(bf16)
    rows_ref[:, :D] = back.astype(bf16)
    rows_ref[:, D:] = words.astype(bf16)


def peers():
    count = lax.axis_size("expert")
    me = lax.axis_index("expert")
    return count, me, [lax.rem(me + step, count) for step in range(1, count)]


def group_ids():
    return [{"expert": other} for other in peers()[2]]


def partner_id():
    return {"zhi": 1 - lax.axis_index("zhi")}


def core_id():
    return {"core": 1 - lax.axis_index("core")}


def mate_ids():
    count, me = lax.axis_size("zlo"), lax.axis_index("zlo")
    return [lax.rem(me + step, count) for step in range(1, count)]


def greet(targets):
    barrier = pltpu.get_barrier_semaphore()
    for target in targets:
        pl.semaphore_signal(
            barrier, inc=1, device_id=target, device_id_type=pl.DeviceIdType.MESH
        )
    pl.semaphore_wait(barrier, len(targets))


def remote(src, dst, sems, number, target):
    return pltpu.make_async_remote_copy(
        src_ref=src, dst_ref=dst, send_sem=sems[0].at[number], recv_sem=sems[1].at[number],
        device_id=target, device_id_type=pl.DeviceIdType.MESH,
    )


def spread_copies(src, dst, sems, base):
    _, me, others = peers()
    return [
        remote(src, dst.at[me], sems, base + number, {"expert": other})
        for number, other in enumerate(others)
    ]


def reduce_copies(src, dst, sems, base, rows, start):
    _, _, others = peers()
    return [
        remote(
            src.at[pl.ds(pl.multiple_of(start + other * rows, rows), rows)],
            dst.at[number], sems, base + number, {"expert": other},
        )
        for number, other in enumerate(others)
    ]


def reduced(src, dst, rows, start, columns):
    _, me, others = peers()
    total = src[pl.ds(pl.multiple_of(start + me * rows, rows), rows), columns].astype(f32)
    for number in range(len(others)):
        total = total + dst[number, :, columns].astype(f32)
    return total


class MateSpread:
    def __init__(self, rows, full, sems, base, local_sem):
        planes = mate_ids()
        core, me = lax.axis_index("core"), lax.axis_index("zlo")
        slot = me * 2 + core
        self.over = [
            remote(rows, full.at[slot], sems, base + number, {"zlo": mate})
            for number, mate in enumerate(planes)
        ]
        count = len(planes)
        self.beside = [remote(rows, full.at[slot], sems, base + count, core_id())]
        size = count + 1
        self.onward = [
            remote(
                full.at[lax.rem(me + size - 1 - number, size) * 2 + core],
                full.at[lax.rem(me + size - 1 - number, size) * 2 + core],
                sems, base + count + 1 + number, core_id(),
            )
            for number in range(count)
        ]
        self.own = pltpu.make_async_copy(rows, full.at[slot], local_sem)

    def start(self):
        for copy in self.over + self.beside + [self.own]:
            copy.start()

    def forward(self):
        for copy, onward in zip(self.over, self.onward):
            copy.wait()
            onward.start()

    def finish(self):
        for copy in self.beside + self.onward + [self.own]:
            copy.wait()


def mate_sems(planes):
    return 2 * planes - 1


def near_ids():
    return [partner_id(), core_id()] + [{"zlo": mate} for mate in mate_ids()]


def plane_place():
    planes = lax.axis_size("zlo")
    return lax.axis_index("zhi") * planes + lax.axis_index("zlo"), 2 * planes


def plane_id(plane):
    planes = lax.axis_size("zlo")
    return {"zhi": plane // planes, "zlo": lax.rem(plane, planes)}


def line_sems(count):
    return [
        pltpu.SemaphoreType.DMA((count - 1,)), pltpu.SemaphoreType.DMA((count - 1,)),
        pltpu.SemaphoreType.DMA((count - 1,)), pltpu.SemaphoreType.DMA((count - 1,)),
        pltpu.SemaphoreType.DMA((2 * count - 1,)), pltpu.SemaphoreType.DMA((2 * count - 1,)),
    ]


class LineGather:
    def __init__(self, full, sems):
        self.full = full
        self.up, self.down, self.side = sems[0:2], sems[2:4], sems[4:6]
        self.core = lax.axis_index("core")
        self.at, self.count = plane_place()

    def block(self, plane):
        return self.full.at[plane * 2 + self.core]

    def move(self, plane, sems, number, target):
        return remote(self.block(plane), self.block(plane), sems, number, target)

    def upward(self, step):
        return self.move(self.at - step, self.up, step, plane_id(self.at + 1))

    def downward(self, step):
        return self.move(self.at + step, self.down, step, plane_id(self.at - 1))

    def sends_up(self, step):
        return (self.at < self.count - 1) & (self.at >= step)

    def sends_down(self, step):
        return (self.at > 0) & (self.at + step < self.count)

    def gets_up(self, step):
        return self.at >= step + 1

    def gets_down(self, step):
        return self.at + step + 1 < self.count

    def beside(self, plane, number):
        return self.move(plane, self.side, number, core_id())

    def start(self):
        pl.when(self.sends_up(0))(lambda: self.upward(0).start())
        pl.when(self.sends_down(0))(lambda: self.downward(0).start())
        self.beside(self.at, 0).start()

    def step(self, step):
        def from_below():
            self.move(self.at - step - 1, self.up, step, plane_id(self.at)).wait_recv()
            self.beside(self.at - step - 1, 1 + step).start()

        def from_above():
            self.move(self.at + step + 1, self.down, step, plane_id(self.at)).wait_recv()
            self.beside(self.at + step + 1, self.count + step).start()

        pl.when(self.gets_up(step))(from_below)
        if step + 1 < self.count - 1:
            pl.when(self.sends_up(step + 1))(lambda: self.upward(step + 1).start())
        pl.when(self.gets_down(step))(from_above)
        if step + 1 < self.count - 1:
            pl.when(self.sends_down(step + 1))(lambda: self.downward(step + 1).start())

    def finish(self):
        self.beside(self.at, 0).wait()
        for step in range(self.count - 1):
            pl.when(self.sends_up(step))(lambda step=step: self.upward(step).wait_send())
            pl.when(self.sends_down(step))(lambda step=step: self.downward(step).wait_send())
            pl.when(self.gets_up(step))(
                lambda step=step: self.beside(self.at - step - 1, 1 + step).wait()
            )
            pl.when(self.gets_down(step))(
                lambda step=step: self.beside(self.at + step + 1, self.count + step).wait()
            )


def start_kernel(lengths_ref, x_ref, cot_ref, routes_ref, win_ref, sgu_ref, wout_ref, sd_ref,
                 gu_ref, down_ref,
                 x_all_ref, cot_all_ref, cot_came_ref, routes_two_ref, win_all_ref, sgu_all_ref, wout_own_ref,
                 sd_own_ref, masks_ref, doc_col_ref, doc_row_ref, gu_kept_ref, gu_sent_ref,
                 down_kept_ref, down_sent_ref,
                 wout_all_ref, sd_all_ref, routes_came_ref, send_sems, recv_sems,
                 out_send, out_recv, near_send, near_recv, local_sems, *line):
    count, me, others = peers()
    at, planes = plane_place()
    half = lax.axis_index("zhi")
    sems = (send_sems, recv_sems)
    near = (near_send, near_recv)
    barrier = pltpu.get_barrier_semaphore()

    def tell(target):
        pl.semaphore_signal(
            barrier, inc=1, device_id=target, device_id_type=pl.DeviceIdType.MESH
        )

    for target in group_ids() + [partner_id(), core_id()]:
        tell(target)
    pl.when(at > 0)(lambda: tell(plane_id(at - 1)))
    pl.when(at < planes - 1)(lambda: tell(plane_id(at + 1)))
    ends = (at > 0).astype(jnp.int32) + (at < planes - 1).astype(jnp.int32)
    pl.semaphore_wait(barrier, count + 1 + ends)

    slot = at * 2 + lax.axis_index("core")
    peer_count = len(others)

    def pieces(src, dst, base, local):
        copies = [
            remote(src.at[other], dst.at[slot, me], sems, base + number, {"expert": other})
            for number, other in enumerate(others)
        ]
        return copies + [pltpu.make_async_copy(src.at[me], dst.at[slot, me], local)]

    def shared_rows(src, dst, base, local):
        return spread_copies(src, dst, sems, base) + [
            pltpu.make_async_copy(src, dst.at[me], local)
        ]

    def started(copies):
        for copy in copies:
            copy.start()
        return copies

    def ended(copies):
        for copy in copies:
            copy.wait()

    lines = [
        LineGather(full, line[6 * k : 6 * k + 6])
        for k, full in enumerate((win_all_ref, wout_all_ref, sgu_all_ref, sd_all_ref))
    ]
    win_copies = started(pieces(win_ref, win_all_ref, 0, local_sems.at[0]))
    keep = started([
        pltpu.make_async_copy(wout_ref, wout_all_ref.at[slot], local_sems.at[1]),
        pltpu.make_async_copy(sd_ref, sd_all_ref.at[slot], local_sems.at[2]),
    ])
    ended(keep)
    lines[1].start()
    lines[3].start()
    sgu_copies = started(pieces(sgu_ref, sgu_all_ref, peer_count, local_sems.at[3]))
    routes_over = started([remote(routes_ref, routes_came_ref, near, 1, partner_id())])
    ended(win_copies)
    lines[0].start()
    wide = started(
        shared_rows(x_ref, x_all_ref, 2 * peer_count, local_sems.at[4])
        + shared_rows(routes_ref, routes_two_ref.at[0], 3 * peer_count, local_sems.at[5])
    )
    for step in range(planes - 1):
        lines[1].step(step)
        lines[3].step(step)
    lines[1].finish()
    lines[3].finish()
    rows = wout_own_ref.shape[0]
    out_copies = []
    for j in range(rows):
        for k, (full, own) in enumerate(
            ((wout_all_ref, wout_own_ref), (sd_all_ref, sd_own_ref))
        ):
            base = (2 * j + k) * peer_count
            for number, other in enumerate(others):
                out_copies.append(remote(
                    full.at[other * rows + j], own.at[j, me], (out_send, out_recv),
                    base + number, {"expert": other},
                ))
            out_copies.append(pltpu.make_async_copy(
                full.at[me * rows + j], own.at[j, me], local_sems.at[9 + 2 * j + k]
            ))
    started(out_copies)
    lines[0].step(0)
    ended(sgu_copies)
    lines[2].start()
    cot_over = started([remote(cot_ref, cot_came_ref, near, 0, partner_id())])
    wide += started(shared_rows(cot_ref, cot_all_ref, 4 * peer_count, local_sems.at[6]))

    length = masks_ref.shape[0]
    place = lax.broadcasted_iota(jnp.int32, (length, LANES), 0)
    lane = lax.broadcasted_iota(jnp.int32, (length, LANES), 1)
    across = lax.broadcasted_iota(jnp.int32, (1, length), 1)
    doc, earlier, doc_row = place * 0 - 1, place * 0 - 1, across * 0 - 1
    start = 0
    for k in range(lengths_ref.shape[1]):
        doc = doc + (place >= start).astype(jnp.int32)
        earlier = earlier + (place - lane >= start).astype(jnp.int32)
        doc_row = doc_row + (across >= start).astype(jnp.int32)
        start = start + lengths_ref[0, k]
    masks_ref[...] = (doc == earlier).astype(f32)
    doc_col_ref[...] = doc[:, :1]
    doc_row_ref[...] = doc_row
    held = gu_kept_ref.shape[0]
    for e in range(held):
        gu_kept_ref[e] = gu_ref[half * held + e].astype(bf16)
        gu_sent_ref[e] = gu_ref[(1 - half) * held + e].astype(bf16)
        down_kept_ref[e] = down_ref[half * held + e].astype(bf16)
        down_sent_ref[e] = down_ref[(1 - half) * held + e].astype(bf16)

    ended(routes_over)
    wide += started(
        shared_rows(routes_came_ref, routes_two_ref.at[1], 5 * peer_count, local_sems.at[7])
    )
    for step in range(1, planes - 1):
        lines[0].step(step)
        lines[2].step(step - 1)
    lines[2].step(planes - 2)
    lines[0].finish()
    lines[2].finish()
    ended(wide + out_copies + cot_over)


def hidden_kernel(part_ref, tokens_ref, gain_ref, down_ref, down_sent_ref,
                  hidden_ref, res_ref, two_ref, down_all_ref, down_came_ref,
                  got_ref, send_sems, recv_sems, mate_send, mate_recv, mate_local):
    tok = tokens_ref.shape[0]
    sems = (send_sems, recv_sems)
    greet(group_ids() + near_ids())
    copies = reduce_copies(part_ref, got_ref, sems, 0, tok, 0)
    over = remote(down_sent_ref, down_came_ref, sems, len(copies), partner_id())
    weights = MateSpread(down_ref, down_all_ref, (mate_send, mate_recv), 0, mate_local)
    for copy in copies + [over]:
        copy.start()
    weights.start()
    for copy in copies:
        copy.wait()
    squares = word_sum(reduced(part_ref, got_ref, tok, 0, slice(D, D + LANES)))
    scale_mix = lax.rsqrt(squares / INNER + norm_eps)
    res = reduced(part_ref, got_ref, tok, 0, slice(0, D)) * scale_mix
    res_ref[...] = res
    hidden = tokens_ref[...].astype(f32) + res
    hidden_ref[...] = hidden
    scale = lax.rsqrt(jnp.mean(hidden * hidden, axis=1, keepdims=True) + norm_eps)
    two_ref[:, :D] = (hidden * scale * gain_ref[1:2]).astype(bf16)
    two_ref[:, D:] = word_lanes(scale_mix)
    weights.forward()
    over.wait()
    weights.finish()


def share_kernel(two_ref, gu_ref, down_ref, cot_ref, sgu_ref, sd_ref,
                 two_all_ref, gu_all_ref, down_all_ref, out_ref, back_ref, grad_gu_ref,
                 grad_down_ref, came_ref, rows_ref, mid_ref, act_ref,
                 send_sems, recv_sems, mate_send, mate_recv, local_sems):
    count, me, _ = peers()
    sems = (send_sems, recv_sems)
    mate = (mate_send, mate_recv)
    own_ref, other_ref = two_all_ref.at[0], two_all_ref.at[1]
    greet(group_ids() + near_ids())
    over = remote(two_ref, came_ref, sems, 0, partner_id())
    over.start()
    first = spread_copies(two_ref, own_ref, sems, 1)
    for copy in first:
        copy.start()
    mine = pltpu.make_async_copy(two_ref, own_ref.at[me], local_sems.at[0])
    mine.start()
    step = (mate_send.shape[0]) // 2
    gu_weights = MateSpread(gu_ref, gu_all_ref, mate, 0, local_sems.at[1])
    down_weights = MateSpread(down_ref, down_all_ref, mate, step, local_sems.at[2])
    gu_weights.start()
    down_weights.start()
    over.wait()
    second = spread_copies(came_ref, other_ref, sems, count)
    for copy in second:
        copy.start()
    theirs = pltpu.make_async_copy(came_ref, other_ref.at[me], local_sems.at[3])
    theirs.start()
    for copy in first:
        copy.wait()
    mine.wait()

    length, width = rows_ref.shape[0], sd_ref.shape[0]
    tok = two_ref.shape[0]
    for g in range(count):
        rows_ref[g * tok : (g + 1) * tok, :] = two_all_ref[0, g, :, :D]
    gate = dot(rows_ref[...], sgu_ref[:, :width])
    up = dot(rows_ref[...], sgu_ref[:, width:])
    silu = jax.nn.silu(gate)
    mid_ref[...] = (silu * up).astype(bf16)
    grad_mid = dot_nt(cot_ref[:length, :], sd_ref[...])
    act_ref[:, :width] = (grad_mid * up * silu_slope(gate)).astype(bf16)
    act_ref[:, width:] = (grad_mid * silu).astype(bf16)
    gu_weights.forward()

    @pl.loop(0, D // 256)
    def _(part):
        at = pl.ds(pl.multiple_of(part * 256, 256), 256)
        out_ref[:, at] = dot(mid_ref[...], sd_ref[:, at]).astype(bf16)
        back_ref[:, at] = dot_nt(act_ref[...], sgu_ref[at, :]).astype(bf16)

    owners, rows_down, _ = grad_down_ref.shape
    real = width // owners
    total = dot_tn(mid_ref[...], cot_ref[:length, :]).astype(bf16)
    for k in range(owners):
        grad_down_ref[k, :real, :] = total[k * real : (k + 1) * real]
        if real < rows_down:
            grad_down_ref[k, real:, :] = jnp.zeros((rows_down - real, D), bf16)
    each = D // owners
    wide = max(each, 384)
    for part in range(D // wide):
        total = dot_tn(rows_ref[:, part * wide : (part + 1) * wide], act_ref[...]).astype(bf16)
        for k in range(wide // each):
            owner = part * (wide // each) + k
            grad_gu_ref[owner // 2, owner % 2] = total[k * each : (k + 1) * each]
    for copy in second:
        copy.wait()
    theirs.wait()
    down_weights.forward()
    gu_weights.finish()
    down_weights.finish()


def q_lanes(sources, held, own_experts, half):
    lanes = lax.broadcasted_iota(jnp.int32, sources[0][1].shape, 1)
    total = jnp.zeros(lanes.shape, f32)
    for place, words in sources:
        for expert in range(held):
            value = sum(
                words[:, k * held + expert : k * held + expert + 1].astype(f32) for k in range(3)
            )
            lane = place * own_experts + half * held + expert
            total = jnp.where(lanes == lane, value, total)
    return total


def sum_plane(sums_ref, part_ref, slots_ref, expert):
    me = lax.axis_index("zlo")
    for h in range(sums_ref.shape[1]):
        total = part_ref[me, expert, h].astype(f32)
        for number in range(slots_ref.shape[0]):
            total = total + slots_ref[number, expert, h].astype(f32)
        sums_ref[expert, h] = total.astype(bf16)


def back_kernel(back_ref, hidden_ref, res_ref, cot_ref, weights_ref, router_ref, gain_ref, grads_ref,
                all_ref, grad_hidden_ref, grad_logits_ref, gain_grad_ref, sums_ref, theirs_ref,
                got_other_ref, got_own_ref, send_ref, came_ref, low_ref, slots_ref, core_ref,
                send_sems, recv_sems, plane_send, plane_recv, core_send, core_recv, local_sem,
                *, own_experts, heads):
    tok = cot_ref.shape[0]
    length = back_ref.shape[0] // 2
    held = own_experts // 2
    count, me, others = peers()
    half = lax.axis_index("zhi")
    sems = (send_sems, recv_sems)
    words_at = slice(D, D + LANES)
    mates = mate_ids()
    greet(group_ids() + near_ids())
    core = lax.axis_index("core")
    planes_here = core_ref.shape[0]
    core_copies = [
        [
            remote(
                grads_ref.at[z, 1 - core, expert], core_ref.at[z, expert], (core_send, core_recv),
                expert * planes_here + z, core_id(),
            )
            for z in range(planes_here)
        ]
        for expert in range(held)
    ]
    plane_sems = (plane_send, plane_recv)
    planes = [
        [
            remote(
                core_ref.at[mate, expert], slots_ref.at[number, expert], plane_sems,
                expert * len(mates) + number, {"zlo": mate},
            )
            for number, mate in enumerate(mates)
        ]
        for expert in range(held)
    ]
    first = reduce_copies(back_ref, got_other_ref, sems, 0, tok, length)
    second = reduce_copies(back_ref, got_own_ref, sems, count - 1, tok, 0)
    for copy in first + core_copies[0] + core_copies[1]:
        copy.start()
    for expert in range(held):
        for z, copy in enumerate(core_copies[expert]):
            copy.wait()
            for h in range(2):
                core_ref[z, expert, h] = (
                    core_ref[z, expert, h].astype(f32) + grads_ref[z, core, expert, h].astype(f32)
                ).astype(bf16)
        if expert == 0:
            for copy in planes[0]:
                copy.start()

    def q_of(start, slots):
        mine = back_ref[pl.ds(pl.multiple_of(start + me * tok, tok), tok), words_at]
        sources = [(me, mine)]
        for number in range(count - 1):
            sources.append((lax.rem(me + count - 1 - number, count), slots[number, :, words_at]))
        return q_lanes(sources, held, own_experts, half)

    for copy in first:
        copy.wait()
    send_ref[:, :D] = reduced(back_ref, got_other_ref, tok, length, slice(0, D)).astype(bf16)
    lanes = lax.broadcasted_iota(jnp.int32, (tok, LANES), 1)
    words = jnp.zeros((tok, LANES), f32)
    shift = LANES // 4
    for k, word in enumerate(split_words(q_of(length, got_other_ref))):
        placed = word.astype(f32) if k == 0 else pltpu.roll(word.astype(f32), k * shift, 1)
        words = words + placed
    send_ref[:, D:] = words.astype(bf16)
    over = remote(send_ref, came_ref, sems, 2 * (count - 1), {"zhi": 1 - half})
    over.start()
    for copy in second:
        copy.start()
    for copy in planes[0]:
        copy.wait()
    for copy in planes[1]:
        copy.start()
    sum_plane(sums_ref, core_ref, slots_ref, 0)
    across = remote(
        sums_ref.at[0, 1 - half], theirs_ref, plane_sems, held * len(mates), partner_id()
    )
    for copy in second:
        copy.wait()
    q_own = q_of(0, got_own_ref)
    total = reduced(back_ref, got_own_ref, tok, 0, slice(0, D))
    over.wait()
    across.start()
    came = came_ref[:, D:].astype(f32)
    came = came + pltpu.roll(came, LANES - shift, 1) + pltpu.roll(came, LANES - 2 * shift, 1)
    q = q_own + jnp.where(lanes < shift, came, 0.0)
    weights = weights_ref[...]
    grad_logits = weights * (q - jnp.sum(weights * q, axis=1, keepdims=True))
    grad_logits_ref[...] = grad_logits.astype(bf16)
    placed_logits = pltpu.roll(grad_logits, heads, 1).astype(bf16)
    total = total + came_ref[:, :D].astype(f32) + dot_nt(placed_logits, router_ref[...])
    hidden = hidden_ref[...]
    scale = lax.rsqrt(jnp.mean(hidden * hidden, axis=1, keepdims=True) + norm_eps)
    unit = hidden * scale
    gain_grad_ref[...] = jnp.broadcast_to(
        jnp.sum(total * unit, axis=0, keepdims=True), gain_grad_ref.shape
    )
    grad_hidden = cot_ref[...].astype(f32) + norm_back(total, unit, scale, gain_ref[1:2])
    grad_hidden_ref[...] = grad_hidden
    low_ref[:, :D] = grad_hidden.astype(bf16)
    row_mean = jnp.sum(low_ref[:, :D].astype(f32) * res_ref[...], axis=1, keepdims=True) / INNER
    low_ref[:, D:] = word_lanes(row_mean)
    third = spread_copies(low_ref, all_ref, sems, 2 * count - 1)
    for copy in third:
        copy.start()
    mine = pltpu.make_async_copy(low_ref, all_ref.at[me], local_sem)
    mine.start()
    for copy in planes[1]:
        copy.wait()
    sum_plane(sums_ref, core_ref, slots_ref, 1)
    for copy in third:
        copy.wait()
    mine.wait()
    across.wait()


def dense_kernel(x_ref, tokens_ref, win_ref, gain_ref, proj_ref, two_ref, logits_ref, sgu_ref,
                 wout_ref, down_ref, grad_hidden_ref, out_own_ref, out_send_ref, hidden_ref,
                 conv_ref, cols_ref,
                 head_ref, gain_two_ref,
                 got_ref, own_out_ref, own_down_ref, tokens_grad_ref, output_ref, all_small_ref,
                 normed_ref, first_ref, second_ref, core_ref, slots_ref, plane_ref, came_ref,
                 send_ref, one_ref, one_got_ref, out_came_ref, scale_ref, step_ref, step_came_ref, core_send, core_recv, plane_send,
                 plane_recv, half_send, half_recv, row_send, row_recv, one_send, one_recv, out_send,
                 out_recv, small_send, small_recv, fold_send, fold_recv, local_sems, fold_sems,
                 own_sems, *, shared_chunks, heads):
    length = x_ref.shape[0]
    tok = tokens_ref.shape[0]
    chunks_one = first_ref.shape[0]
    chunks = core_ref.shape[0]
    own_rows = first_ref.shape[3]
    rows_in = send_ref.shape[2]
    core, half, zlo = lax.axis_index("core"), lax.axis_index("zhi"), lax.axis_index("zlo")
    mates = mate_ids()
    count, me, others = peers()
    planes = core_ref.shape[1] // 2
    greet(group_ids() + near_ids())

    def source(chunk):
        if chunk < chunks_one:
            return first_ref.at[chunk]
        start = (chunk - chunks_one) * CHUNK
        return second_ref.at[:, :, :, start : start + CHUNK]

    wide_out = D * wout_ref.shape[1] // own_rows
    wide_down = D * down_ref.shape[1] // own_rows
    start = wide_out + wide_down
    beside = pltpu.make_async_copy(
        sgu_ref, second_ref.at[:, :, :, start : start + sgu_ref.shape[3]], own_sems.at[0]
    )
    beside.start()
    each = wout_ref.shape[0] // count
    fold_copies = []
    number = 0
    local = 0
    for full, width, offset in ((wout_ref, wide_out, 0), (down_ref, wide_down, wide_out)):
        rows = full.shape[1]
        for j in range(each):
            for fold in range(D // width):
                columns = slice(fold * width, (fold + 1) * width)
                place = pl.ds(fold * rows, rows)
                owner = me * each + j
                target = second_ref.at[
                    owner // 2, lax.rem(owner, 2), place, offset : offset + width
                ]
                for other in others:
                    fold_copies.append(remote(
                        full.at[j * count + other, :, columns], target, (fold_send, fold_recv),
                        number, {"expert": other},
                    ))
                    number += 1
                fold_copies.append(pltpu.make_async_copy(
                    full.at[j * count + me, :, columns], target, fold_sems.at[local]
                ))
                local += 1
    for copy in fold_copies:
        copy.start()

    core_copies, plane_copies, half_copies, row_copies = {}, {}, {}, {}

    def send_core(chunk):
        copies = [
            pltpu.make_async_remote_copy(
                src_ref=source(chunk).at[:, 1 - core],
                dst_ref=core_ref.at[chunk], send_sem=core_send.at[chunk],
                recv_sem=core_recv.at[chunk], device_id=core_id(),
                device_id_type=pl.DeviceIdType.MESH,
            )
        ]
        for copy in copies:
            copy.start()
        core_copies[chunk] = copies

    def send_plane(chunk):
        for copy in core_copies[chunk]:
            copy.wait()
        for k in range(2 * planes):
            core_ref[chunk, k] = (
                source(chunk)[k, core].astype(f32) + core_ref[chunk, k].astype(f32)
            ).astype(bf16)
        copies = [
            remote(
                core_ref.at[chunk, pl.ds(h * planes + mate, 1)],
                slots_ref.at[chunk, number, pl.ds(h, 1)],
                (plane_send, plane_recv), (chunk * len(mates) + number) * 2 + h, {"zlo": mate},
            )
            for number, mate in enumerate(mates)
            for h in range(2)
        ]
        for copy in copies:
            copy.start()
        plane_copies[chunk] = copies

    def send_half(chunk):
        for copy in plane_copies[chunk]:
            copy.wait()
        for h in range(2):
            total = core_ref[chunk, h * planes + zlo].astype(f32)
            for number in range(len(mates)):
                total = total + slots_ref[chunk, number, h].astype(f32)
            plane_ref[chunk, h] = total.astype(bf16)
        copy = remote(
            plane_ref.at[chunk, 1 - half], came_ref.at[chunk], (half_send, half_recv), chunk,
            partner_id(),
        )
        copy.start()
        half_copies[chunk] = copy

    def send_rows(chunk):
        half_copies[chunk].wait()
        total = plane_ref[chunk, half].astype(f32) + came_ref[chunk].astype(f32)
        for block in range(CHUNK // LANES):
            at = (chunk - chunks_one) * CHUNK + block * LANES
            columns = total[:, block * LANES : (block + 1) * LANES]
            if 0 <= at < wide_out:
                put(own_out_ref, columns, wide_out, at)
            elif wide_out <= at < wide_out + wide_down:
                put(own_down_ref, columns, wide_down, at - wide_out)
        if chunk not in shared_chunks:
            return
        spot = shared_chunks.index(chunk)
        columns = slice(spot * CHUNK, (spot + 1) * CHUNK)
        low = total.astype(bf16)
        for place in range(count):
            send_ref[spot, place] = low[place * rows_in : (place + 1) * rows_in]
        copies = [
            remote(
                send_ref.at[spot, other], got_ref.at[me, :, columns], (row_send, row_recv),
                chunk * (count - 1) + number, {"expert": other},
            )
            for number, other in enumerate(others)
        ]
        mine = pltpu.make_async_copy(
            send_ref.at[spot, me], got_ref.at[me, :, columns], local_sems.at[chunk]
        )
        for copy in copies + [mine]:
            copy.start()
        row_copies[chunk] = copies + [mine]

    def put(ref, columns, width, at):
        rows = ref.shape[0]
        for fold in range(D // width):
            ref[:, fold * width + at : fold * width + at + LANES] = columns[
                fold * rows : (fold + 1) * rows
            ]

    alone = [chunk for chunk in range(chunks_one, chunks)
             if (chunk - chunks_one) * CHUNK >= wide_out + wide_down]
    mixed = [chunk for chunk in range(chunks_one, chunks) if chunk not in alone]
    order = alone + list(range(chunks_one)) + mixed
    ready = set()

    @pl.loop(0, length // LANES)
    def _(part):
        rows = pl.ds(pl.multiple_of(part * LANES, LANES), LANES)
        block = x_ref[rows, :].astype(f32)
        scale = lax.rsqrt(jnp.mean(block * block, axis=1, keepdims=True) + norm_eps)
        normed_ref[rows, :] = (block * scale * gain_ref[0:1]).astype(bf16)
        scale_ref[rows, :] = scale

    out_over = remote(out_send_ref, out_came_ref, (out_send, out_recv), 0, partner_id())

    def produce(chunk):
        if chunk in ready:
            return
        ready.add(chunk)
        if chunk in alone:
            beside.wait()
        elif chunk in mixed:
            if not any(one in ready for one in mixed if one != chunk):
                for copy in fold_copies:
                    copy.wait()
                if not alone:
                    beside.wait()
            for one in mixed:
                ready.add(one)
                send_core(one)
            return
        else:
            at = slice(chunk * CHUNK, (chunk + 1) * CHUNK)
            total = dot_tn(normed_ref[...], proj_ref[:, at])
            if chunk == chunks_one - 1:
                logits = pltpu.roll(logits_ref[...].astype(f32), heads, 1).astype(bf16)
                router = dot_tn(two_ref[:, :D], logits)
                total = total + jnp.concatenate(
                    [jnp.zeros((D, CHUNK - LANES), f32), router], axis=1
                )
            low = total.astype(bf16)
            for k in range(D // own_rows):
                first_ref[chunk, k // 2, k % 2] = low[k * own_rows : (k + 1) * own_rows]
        send_core(chunk)

    begin = conv_ref.shape[1]
    step_ref[0, :, :begin] = conv_ref[...]
    step_ref[0, :, begin : begin + cols_ref.shape[1]] = cols_ref[...]
    begin += cols_ref.shape[1]
    step_ref[0, :, begin : begin + LANES] = head_ref[...]
    begin += LANES
    step_ref[0, :, begin : begin + D] = gain_two_ref[...]
    begin += D

    def input_part(part):
        at = slice(part * CHUNK, (part + 1) * CHUNK)
        one = dot_nt(proj_ref[...], win_ref[at, :])
        gains = jnp.sum(one * (x_ref[:, at].astype(f32) * scale_ref[...]), axis=0, keepdims=True)
        step_ref[0, :, begin + part * CHUNK : begin + (part + 1) * CHUNK] = jnp.broadcast_to(
            gains, (8, CHUNK)
        )
        one_ref[:, at] = one.astype(bf16)

    one_copies = reduce_copies(one_ref, one_got_ref, (one_send, one_recv), 0, tok, 0)

    small_sems = (small_send, small_recv)
    rounds = [[core_id()], [{"zlo": mate} for mate in mates], [partner_id()]]
    bases = [sum(len(targets) for targets in rounds[:level]) for level in range(4)]
    small_copies = [
        [
            remote(
                step_ref.at[level], step_came_ref.at[bases[level] + k], small_sems,
                bases[level] + k, target,
            )
            for k, target in enumerate(targets)
        ]
        for level, targets in enumerate(rounds)
    ]
    small_copies.append([
        remote(
            step_ref.at[3], all_small_ref.at[me], small_sems, bases[3] + number, {"expert": other}
        )
        for number, other in enumerate(others)
    ])
    small_copies[3].append(
        pltpu.make_async_copy(step_ref.at[3], all_small_ref.at[me], own_sems.at[1])
    )

    def small_start(level):
        for copy in small_copies[level]:
            copy.start()

    def small_sum(level):
        total = step_ref[level]
        for k, copy in enumerate(small_copies[level]):
            copy.wait()
            total = total + step_came_ref[bases[level] + k]
        step_ref[level + 1] = total

    amount = len(order)
    parts = D // CHUNK
    produce(order[0])
    for tick in range(amount + 4):
        if tick + 1 < amount:
            produce(order[tick + 1])
        if tick < amount:
            send_plane(order[tick])
        if tick == 2:
            out_over.start()
        if 2 <= tick < amount + 2:
            send_half(order[tick - 2])
        if 4 <= tick:
            send_rows(order[tick - 4])
        if amount - parts <= tick < amount:
            input_part(tick - (amount - parts))
        if tick == amount - 1:
            for copy in one_copies:
                copy.start()
            small_start(0)
        if amount <= tick < amount + 3:
            small_sum(tick - amount)
            small_start(tick - amount + 1)
    for copy in one_copies:
        copy.wait()
    total = reduced(one_ref, one_got_ref, tok, 0, slice(0, D))
    block = tokens_ref[...].astype(f32)
    scale = lax.rsqrt(jnp.mean(block * block, axis=1, keepdims=True) + norm_eps)
    tokens_grad_ref[...] = (
        grad_hidden_ref[...] + norm_back(total, block * scale, scale, gain_ref[0:1])
    ).astype(bf16)
    out_over.wait()
    output_ref[...] = (
        hidden_ref[...] + out_own_ref[...] + out_came_ref[...].astype(f32)
    ).astype(bf16)
    for copy in small_copies[3]:
        copy.wait()
    for copies in row_copies.values():
        for copy in copies:
            copy.wait()


def kernel_room(shapes):
    total = 0
    for shape, dtype in shapes:
        size = jnp.dtype(dtype).itemsize
        rows = shape[-2] if len(shape) > 1 else 1
        padded = -(-rows // 16) * 16 * -(-shape[-1] // LANES) * LANES
        total += math.prod(shape[:-2]) * padded * size
    rows = max([0] + [shape[0] for shape, _ in shapes if len(shape) == 2 and shape[0] == shape[1]])
    total += 20 * rows * rows + 5 * 1024 * 1024
    return min(max(total, 54 * 1024 * 1024), 62 * 1024 * 1024)


def remote_call(kernel, number, out_shapes, scratch, sems, *operands, outside=()):
    spec = pl.BlockSpec(memory_space=pltpu.VMEM)
    scalars = pl.BlockSpec(memory_space=pltpu.SMEM)
    anywhere = pl.BlockSpec(memory_space=pl.ANY)
    inside = [one for k, one in enumerate(operands) if k not in outside]
    return pl.pallas_call(
        kernel,
        out_shape=out_shapes,
        in_specs=[
            anywhere if k in outside
            else scalars if one.dtype == jnp.int32 and one.size < LANES else spec
            for k, one in enumerate(operands)
        ],
        out_specs=[spec] * len(out_shapes),
        scratch_shapes=[pltpu.VMEM(shape, dtype) for shape, dtype in scratch] + sems,
        compiler_params=pltpu.CompilerParams(
            collective_id=number, has_side_effects=True,
            vmem_limit_bytes=kernel_room(
                [(one.shape, one.dtype) for one in inside + out_shapes] + scratch
            ),
        ),
    )(*operands)


def vmem_call(kernel, out_shapes, scratch, *operands):
    spec = pl.BlockSpec(memory_space=pltpu.VMEM)
    return pl.pallas_call(
        kernel,
        out_shape=out_shapes,
        in_specs=[spec] * len(operands),
        out_specs=[spec] * len(out_shapes),
        scratch_shapes=[pltpu.VMEM(shape, dtype) for shape, dtype in scratch],
        compiler_params=pltpu.CompilerParams(vmem_limit_bytes=56 * 1024 * 1024),
    )(*operands)


def grid_call(kernel, steps, in_specs, out_specs, out_shapes, scratch, *operands):
    return pl.pallas_call(
        kernel,
        grid=(steps,),
        out_shape=out_shapes,
        in_specs=in_specs,
        out_specs=out_specs,
        scratch_shapes=[pltpu.VMEM(shape, dtype) for shape, dtype in scratch],
        compiler_params=pltpu.CompilerParams(vmem_limit_bytes=56 * 1024 * 1024),
    )(*operands)


def on_device(
    tokens, cotangent, lengths, routes,
    w_in, w_in_first, w_in_second,
    w_out, w_out_first, w_out_second,
    w_router, w_router_first, w_router_second,
    w_shared_gu, w_shared_gu_first, w_shared_gu_second,
    w_shared_down, w_shared_down_first, w_shared_down_second,
    w_expert_gu, w_expert_gu_first, w_expert_gu_second,
    w_expert_down, w_expert_down_first, w_expert_down_second,
    norm_gains, norm_gains_first, norm_gains_second,
    conv_params, conv_params_first, conv_params_second,
    head_params, head_params_first, head_params_second,
    mixer_gain, mixer_gain_first, mixer_gain_second,
):
    groups = lax.axis_size("expert")
    copies = (lax.axis_size("zhi") * lax.axis_size("zlo") * lax.axis_size("core"))
    place = lax.axis_index("expert")
    tok = tokens.shape[0]
    length = tok * groups
    top = routes.shape[1]
    experts = w_router.shape[1]
    own_experts = w_expert_gu.shape[0]
    capacity = (4 * tok * top + 3 * experts - 1) // (3 * experts)
    inner = INNER // groups
    heads = HEADS // groups
    rows_in = w_in.shape[0]
    rows_out = w_out.shape[0]
    rows_sd = w_shared_down.shape[0]
    own_ff = SHARED_FF // groups
    per_pair = copies // groups
    conv_cols = inner + 2 * STATE
    body = 2 * inner + 2 * STATE

    w_in_low = w_in.astype(bf16)
    z_cols = w_in_low[:, :INNER].reshape(rows_in, groups, inner)
    x_cols = w_in_low[:, INNER : 2 * INNER].reshape(rows_in, groups, inner)
    bc_cols = jnp.broadcast_to(
        w_in_low[:, None, 2 * INNER : 2 * INNER + 2 * STATE], (rows_in, groups, 2 * STATE)
    )
    dt_cols = w_in_low[:, 2 * INNER + 2 * STATE :].reshape(rows_in, groups, heads)
    router_cols = jnp.broadcast_to(
        w_router.astype(bf16)[:, None], (rows_in, groups, experts)
    )
    fill = jnp.zeros((rows_in, groups, LANES - heads - experts), bf16)
    win_pieces = jnp.concatenate(
        [z_cols, x_cols, bc_cols, dt_cols, router_cols, fill], axis=2
    ).transpose(1, 0, 2)
    sgu_pieces = (
        w_shared_gu.astype(bf16)
        .reshape(rows_in, 2, groups, own_ff)
        .transpose(2, 0, 1, 3)
        .reshape(groups, rows_in, 2 * own_ff)
    )
    pairs = pltpu.SemaphoreType.DMA
    route_pad = jnp.pad(routes, ((0, 0), (0, LANES - top)))
    row_shape = jax.ShapeDtypeStruct((groups, tok, D), bf16)
    route_shape = jax.ShapeDtypeStruct((groups, tok, LANES), jnp.int32)
    half = lax.axis_index("zhi")
    held = own_experts // 2
    rows_egu, rows_ed = w_expert_gu.shape[1], w_expert_down.shape[1]
    gu_held = jax.ShapeDtypeStruct((held, rows_egu, 2 * EXPERT_FF), bf16)
    ed_held = jax.ShapeDtypeStruct((held, rows_ed, D), bf16)
    (
        x_all, cot_all, cot_came, routes_two, win, sgu, wout, sd, masks, doc_col, doc_row,
        egu_kept, egu_sent, ed_kept, ed_sent,
    ) = remote_call(
        start_kernel, 7,
        [
            jax.ShapeDtypeStruct((groups, tok, D), bf16),
            jax.ShapeDtypeStruct((groups, tok, D), bf16),
            jax.ShapeDtypeStruct((tok, D), bf16),
            jax.ShapeDtypeStruct((2, groups, tok, LANES), jnp.int32),
            jax.ShapeDtypeStruct((copies,) + win_pieces.shape, bf16),
            jax.ShapeDtypeStruct((copies,) + sgu_pieces.shape, bf16),
            jax.ShapeDtypeStruct((per_pair, groups, rows_out, D), bf16),
            jax.ShapeDtypeStruct((per_pair, groups, rows_sd, D), bf16),
            jax.ShapeDtypeStruct((length, LANES), f32),
            jax.ShapeDtypeStruct((length, 1), jnp.int32),
            jax.ShapeDtypeStruct((1, length), jnp.int32),
            gu_held, gu_held, ed_held, ed_held,
        ],
        [
            ((copies, rows_out, D), bf16), ((copies, rows_sd, D), bf16), ((tok, LANES), jnp.int32),
        ],
        [pairs((7 * (groups - 1),))] * 2
        + [pairs((2 * per_pair * (groups - 1),))] * 2
        + [pairs((2,))] * 2
        + [pairs((9 + 2 * per_pair,))]
        + line_sems(copies // 2) * 4,
        lengths, tokens, cotangent, route_pad, win_pieces, sgu_pieces,
        w_out.astype(bf16), w_shared_down.astype(bf16), w_expert_gu, w_expert_down,
    )
    x_all = x_all.reshape(length, D)
    routes_two = routes_two.reshape(2 * length, LANES)
    win = win.reshape(D, -1)
    sgu = sgu.reshape(D, -1)
    wout = wout.reshape(inner, D)
    sd = sd.reshape(own_ff, D)
    router = win[:, body:]


    own_x = place * inner
    conv_own = jnp.concatenate(
        [
            lax.dynamic_slice_in_dim(conv_params, own_x, inner, axis=1),
            conv_params[:, INNER:],
        ],
        axis=1,
    )
    head_own = lax.dynamic_slice_in_dim(head_params, place * heads, heads, axis=1)
    gain_own = lax.dynamic_slice_in_dim(mixer_gain, own_x, inner, axis=0)

    conv_pad = jnp.pad(conv_own, ((0, 3), (0, 0)))
    rate_abs = jnp.exp(head_own[0])
    head_rows = jnp.pad(jnp.stack([rate_abs, head_own[1]]), ((0, 6), (0, LANES - heads)))
    col_rows = jnp.pad(
        jnp.stack([gain_own, jnp.repeat(head_own[2], HEAD_DIM)]), ((0, 6), (0, 0))
    )
    gain_rows = jnp.pad(norm_gains, ((0, 6), (0, 0)))

    square = ((length, length), f32)
    lane_rows = ((length, LANES), f32)
    lane_cols = ((LANES, length), f32)
    planes_half = copies // 4
    mates = copies // 2
    spread_sems = [pairs((mate_sems(planes_half),))] * 2
    gu_all = jax.ShapeDtypeStruct((mates,) + egu_kept.shape, bf16)
    ed_all = jax.ShapeDtypeStruct((mates,) + ed_kept.shape, bf16)
    packed, dt_raw, full_y, res_part, gu_near, gu_came, cot_two = remote_call(
        forward_kernel, 3,
        [
            jax.ShapeDtypeStruct((length, body), bf16),
            jax.ShapeDtypeStruct((length, LANES), f32),
            jax.ShapeDtypeStruct((length, inner), bf16),
            jax.ShapeDtypeStruct((length, D + LANES), bf16),
            gu_all,
            gu_held,
            jax.ShapeDtypeStruct((2, groups, tok, D), bf16),
        ],
        [((length, D), bf16), square, square, lane_rows, lane_cols, ((length, inner), bf16),
         lane_rows],
        [pairs((groups,))] * 2 + spread_sems + [pairs(()), pairs((2,))],
        x_all, win, gain_rows, conv_pad, masks, head_rows, col_rows, doc_col, doc_row, wout,
        egu_kept, egu_sent, cot_all, cot_came, outside=(12, 13),
    )
    cot_two = cot_two.reshape(2 * length, D)
    hidden, mixer_res, two_own, ed_near, ed_came = remote_call(
        hidden_kernel, 0,
        [
            jax.ShapeDtypeStruct((tok, D), f32),
            jax.ShapeDtypeStruct((tok, D), f32),
            jax.ShapeDtypeStruct((tok, D + LANES), bf16),
            ed_all,
            ed_held,
        ],
        [((groups - 1, tok, D + LANES), bf16)],
        [pairs((groups,))] * 2 + spread_sems + [pairs(())],
        res_part, tokens, gain_rows, ed_kept, ed_sent,
    )
    gathered_shape = jax.ShapeDtypeStruct((groups, tok, D + LANES), bf16)
    own_rows = groups * rows_in
    payload = ((tok, D + LANES), bf16)
    tile = 16
    down_rows = -(-rows_sd // tile) * tile
    two_rows, gu_far, ed_far, shared_out, shared_back, grad_sgu, grad_sd = remote_call(
        share_kernel, 1,
        [
            jax.ShapeDtypeStruct((2, groups, tok, D + LANES), bf16), gu_all, ed_all,
            jax.ShapeDtypeStruct((length, D), bf16),
            jax.ShapeDtypeStruct((length, D), bf16),
            jax.ShapeDtypeStruct((copies // 2, 2, own_rows, 2 * own_ff), bf16),
            jax.ShapeDtypeStruct((copies, down_rows, D), bf16),
        ],
        [
            payload, ((length, D), bf16),
            ((length, own_ff), bf16), ((length, 2 * own_ff), bf16),
        ],
        [pairs((2 * groups - 1,))] * 2 + [pairs((2 * mate_sems(planes_half),))] * 2 + [pairs((4,))],
        two_own, gu_came, ed_came, cot_two, sgu, sd,
    )
    scale_words = two_rows[0, :, :, D:].reshape(length, LANES)
    two_rows = two_rows.reshape(2 * length, D + LANES)

    blocks = 2 * groups
    expert_at = (place * own_experts + half * held).reshape(1)
    slot_rows = blocks * capacity

    def by_block(*shape):
        return pl.BlockSpec(shape, lambda b: (b,) + (0,) * (len(shape) - 1))

    def fixed(*shape):
        return pl.BlockSpec(shape, lambda b: (0,) * len(shape))

    slot_spec = pl.BlockSpec((held, capacity, D), lambda b: (0, b, 0))
    in_smem = pl.BlockSpec(memory_space=pltpu.SMEM)
    slot_shape = jax.ShapeDtypeStruct((held, slot_rows, D), bf16)
    slot_in, slot_top, slot_grad, weights, pick = grid_call(
        functools.partial(route_kernel, top_count=top, heads=heads), blocks,
        [by_block(tok, D + LANES), by_block(tok, D), by_block(tok, LANES), fixed(D, LANES), in_smem],
        [slot_spec] * 3 + [by_block(tok, LANES), by_block(1, tok, held * capacity)],
        [slot_shape] * 3
        + [
            jax.ShapeDtypeStruct((2 * length, LANES), f32),
            jax.ShapeDtypeStruct((blocks, tok, held * capacity), bf16),
        ],
        [],
        two_rows, cot_two, routes_two, router, expert_at,
    )
    packed_rows = 2 * rows_egu + rows_ed * D // EXPERT_FF

    def by_expert(*shape):
        return pl.BlockSpec((1,) + shape, lambda e: (e,) + (0,) * len(shape))

    def weight_spec(rows, columns):
        return pl.BlockSpec((mates, 1, rows, columns), lambda e: (0, e, 0, 0))

    slot_out, slot_back, slot_q, expert_grads = grid_call(
        expert_kernel, held,
        [by_expert(slot_rows, D)] * 3
        + [in_smem]
        + [weight_spec(rows_egu, 2 * EXPERT_FF)] * 2
        + [weight_spec(rows_ed, D)] * 2,
        [by_expert(slot_rows, D)] * 2
        + [
            by_expert(slot_rows, LANES),
            pl.BlockSpec((mates, 1, 2, packed_rows, EXPERT_FF), lambda e: (0, e, 0, 0, 0)),
        ],
        [slot_shape] * 2
        + [
            jax.ShapeDtypeStruct((held, slot_rows, LANES), f32),
            jax.ShapeDtypeStruct((mates, held, 2, packed_rows, EXPERT_FF), bf16),
        ],
        [((slot_rows, EXPERT_FF), bf16), ((slot_rows, 2 * EXPERT_FF), bf16)],
        slot_in, slot_top, slot_grad, half.reshape(1), gu_near, gu_far, ed_near, ed_far,
    )
    own_spec = pl.BlockSpec((tok, D), lambda b: (jnp.minimum(b, groups - 1), 0))
    out_parts, back_parts = grid_call(
        combine_kernel, blocks,
        [
            by_block(1, tok, held * capacity), by_block(tok, LANES), in_smem, slot_spec, slot_spec,
            pl.BlockSpec((held, capacity, LANES), lambda b: (0, b, 0)), own_spec, own_spec,
        ],
        [by_block(tok, D), by_block(tok, D + LANES)],
        [
            jax.ShapeDtypeStruct((2 * length, D), bf16),
            jax.ShapeDtypeStruct((2 * length, D + LANES), bf16),
        ],
        [],
        pick, weights, expert_at, slot_out, slot_back, slot_q, shared_out, shared_back,
    )

    weights_tok = lax.dynamic_slice_in_dim(weights, place * tok, tok, axis=0)
    gathered_shape = jax.ShapeDtypeStruct((groups, tok, D + LANES), bf16)
    hidden_all, grad_hidden, grad_logits, gain_two, expert_sums, came_one = remote_call(
        functools.partial(back_kernel, own_experts=own_experts, heads=heads), 2,
        [
            gathered_shape,
            jax.ShapeDtypeStruct((tok, D), f32),
            jax.ShapeDtypeStruct((tok, LANES), bf16),
            jax.ShapeDtypeStruct((8, D), f32),
            jax.ShapeDtypeStruct((held, 2, packed_rows, EXPERT_FF), bf16),
            jax.ShapeDtypeStruct((packed_rows, EXPERT_FF), bf16),
        ],
        [((groups - 1, tok, D + LANES), bf16)] * 2
        + [payload] * 3
        + [
            ((planes_half - 1, held, 2, packed_rows, EXPERT_FF), bf16),
            ((planes_half, held, 2, packed_rows, EXPERT_FF), bf16),
        ],
        [
            pairs((3 * groups - 2,)), pairs((3 * groups - 2,)),
            pairs((held * (planes_half - 1) + 1,)), pairs((held * (planes_half - 1) + 1,)),
            pairs((held * planes_half,)), pairs((held * planes_half,)),
            pairs(()),
        ],
        back_parts, hidden, mixer_res, cotangent, weights_tok, router, gain_rows,
        expert_grads.reshape((planes_half, 2) + expert_grads.shape[1:]),
    )
    hidden_all = hidden_all.reshape(length, -1)
    grad_gain_two = gain_two[0]

    out_rows = -(-rows_out // tile) * tile
    (
        grad_proj, conv_grads, col_grads, head_grads, expert_sum, grad_wout, out_own, out_other,
    ) = remote_call(
        backward_kernel, 5,
        [
            jax.ShapeDtypeStruct((length, body + LANES), bf16),
            jax.ShapeDtypeStruct((8, conv_cols), f32),
            jax.ShapeDtypeStruct((8, inner), f32),
            jax.ShapeDtypeStruct((8, LANES), f32),
            jax.ShapeDtypeStruct((own_experts, packed_rows, EXPERT_FF), bf16),
            jax.ShapeDtypeStruct((copies, out_rows, D), bf16),
            jax.ShapeDtypeStruct((tok, D), f32),
            jax.ShapeDtypeStruct((tok, D), bf16),
        ],
        [square, square, lane_rows, lane_cols, square, lane_rows, lane_cols, lane_rows, lane_rows,
         ((length, LANES), bf16), ((inner, D), bf16), ((packed_rows, EXPERT_FF), bf16),
         ((2, groups - 1, tok, D), bf16), ((2, tok, D), bf16)],
        [pairs(()), pairs(()), pairs((2 * groups - 2,)), pairs((2 * groups - 2,)), pairs((2,))],
        hidden_all, scale_words, wout, conv_pad, masks, head_rows, col_rows, doc_col, doc_row,
        packed, dt_raw, full_y, expert_sums, came_one, out_parts, outside=(14,),
    )
    wide_out = D * out_rows // own_rows
    wide_down = D * down_rows // own_rows
    chunks_one = (body + LANES) // CHUNK
    chunks_two = -(-(wide_out + wide_down + 2 * own_ff) // CHUNK)
    chunks = chunks_one + chunks_two
    first_shared = chunks_one + (wide_out + wide_down) // CHUNK
    shared_chunks = list(range(chunks_one)) + list(range(first_shared, chunks))
    shared_wide = len(shared_chunks) * CHUNK
    small_wide = conv_cols + inner + LANES + 2 * D
    folds = own_rows // out_rows + own_rows // down_rows
    dense_sems = [pairs((chunks,))] * 2 + [pairs((2 * chunks * (planes_half - 1),))] * 2
    dense_sems += [pairs((chunks,))] * 2 + [pairs((chunks * (groups - 1),))] * 2
    dense_sems += [pairs((groups - 1,))] * 2 + [pairs((1,))] * 2
    dense_sems += [pairs((planes_half + groups,))] * 2
    dense_sems += [pairs((per_pair * folds * (groups - 1),))] * 2
    dense_sems += [pairs((chunks,)), pairs((per_pair * folds,)), pairs((2,))]
    got_rows, sum_out, sum_sd, grad_tokens, output, small = remote_call(
        functools.partial(dense_kernel, shared_chunks=shared_chunks, heads=heads), 6,
        [
            jax.ShapeDtypeStruct((groups, rows_in, shared_wide), bf16),
            jax.ShapeDtypeStruct((out_rows, D), f32),
            jax.ShapeDtypeStruct((down_rows, D), f32),
            jax.ShapeDtypeStruct((tok, D), bf16),
            jax.ShapeDtypeStruct((tok, D), bf16),
            jax.ShapeDtypeStruct((groups, 8, small_wide), f32),
        ],
        [
            ((length, D), bf16),
            ((chunks_one, copies // 2, 2, own_rows, CHUNK), bf16),
            ((copies // 2, 2, own_rows, chunks_two * CHUNK), bf16),
            ((chunks, copies // 2, own_rows, CHUNK), bf16),
            ((chunks, planes_half - 1, 2, own_rows, CHUNK), bf16),
            ((chunks, 2, own_rows, CHUNK), bf16),
            ((chunks, own_rows, CHUNK), bf16),
            ((len(shared_chunks), groups, rows_in, CHUNK), bf16),
            ((length, D), bf16),
            ((groups - 1, tok, D), bf16),
            ((tok, D), bf16),
            ((length, 1), f32),
            ((4, 8, small_wide), f32),
            ((planes_half + 1, 8, small_wide), f32),
        ],
        dense_sems,
        x_all, tokens, win, gain_rows, grad_proj, two_own, grad_logits, grad_sgu, grad_wout,
        grad_sd, grad_hidden, out_own, out_other, hidden, conv_grads, col_grads, head_grads, gain_two,
        outside=(7, 8, 9),
    )
    sum_egu = jnp.concatenate(
        [expert_sum[:, :rows_egu], expert_sum[:, rows_egu : 2 * rows_egu]], axis=2
    ).astype(f32)
    sum_ed = jnp.concatenate(
        [
            expert_sum[:, 2 * rows_egu + k * rows_ed : 2 * rows_egu + (k + 1) * rows_ed]
            for k in range(D // EXPERT_FF)
        ],
        axis=2,
    ).astype(f32)

    sum_conv = jnp.concatenate(
        [
            small[:, : CONV + 1, :inner].transpose(1, 0, 2).reshape(CONV + 1, INNER),
            jnp.sum(small[:, : CONV + 1, inner:conv_cols], axis=0),
        ],
        axis=1,
    )
    start = conv_cols
    sum_mixer = small[:, 0, start : start + inner].reshape(INNER)
    sum_skip = jnp.sum(
        small[:, 1, start : start + inner].reshape(groups, heads, HEAD_DIM), axis=2
    ).reshape(HEADS)
    start = start + inner
    sum_head = jnp.stack(
        [small[:, k, start : start + heads].reshape(HEADS) for k in range(2)] + [sum_skip]
    )
    start = start + LANES
    gain_sums = jnp.sum(small[:, 0, start:], axis=0)
    sum_gains = jnp.stack([gain_sums[D:], gain_sums[:D]])

    def laid(source, start, size):
        return source[:, :, start : start + size].transpose(1, 0, 2).reshape(rows_in, -1)

    win_got = got_rows.astype(f32)
    sum_in = jnp.concatenate(
        [
            laid(win_got, 0, inner),
            laid(win_got, inner, inner),
            jnp.sum(win_got[:, :, 2 * inner : body], axis=0),
            laid(win_got, body, heads),
        ],
        axis=1,
    )
    sum_router = jnp.sum(win_got[:, :, body + heads : body + heads + experts], axis=0)
    start = body + LANES + (wide_out + wide_down) % CHUNK
    sum_sgu = (
        win_got[:, :, start : start + 2 * own_ff]
        .reshape(groups, rows_in, 2, own_ff)
        .transpose(1, 2, 0, 3)
        .reshape(rows_in, 2 * SHARED_FF)
    )
    sum_out = sum_out[:rows_out]
    sum_sd = sum_sd[:rows_sd]
    up_out = adam_step(w_out, w_out_first, w_out_second, sum_out)
    up_sgu = adam_step(w_shared_gu, w_shared_gu_first, w_shared_gu_second, sum_sgu)
    up_sd = adam_step(w_shared_down, w_shared_down_first, w_shared_down_second, sum_sd)
    up_egu = adam_step(w_expert_gu, w_expert_gu_first, w_expert_gu_second, sum_egu)
    up_ed = adam_step(w_expert_down, w_expert_down_first, w_expert_down_second, sum_ed)
    up_gains = adam_step(norm_gains, norm_gains_first, norm_gains_second, sum_gains)
    up_conv = adam_step(conv_params, conv_params_first, conv_params_second, sum_conv)
    up_head = adam_step(head_params, head_params_first, head_params_second, sum_head)
    up_mixer = adam_step(mixer_gain, mixer_gain_first, mixer_gain_second, sum_mixer)

    up_in = adam_step(w_in, w_in_first, w_in_second, sum_in)
    up_router = adam_step(w_router, w_router_first, w_router_second, sum_router)
    large = (up_in, up_out, up_router, up_sgu, up_sd, up_egu, up_ed)
    little = (up_gains, up_conv, up_head, up_mixer)
    return (
        (output, grad_tokens)
        + tuple(part for one in large for part in one[:4])
        + tuple(part for one in little for part in (one[0], one[4], one[2], one[3]))
    )


def solution(mesh):
    copies, groups = mesh.devices.shape
    split = Mesh(mesh.devices.reshape(2, copies // 4, 2, groups), ALL)
    rows = P(ALL, None)
    expert_rows = P("expert", DP, None)
    whole = P()
    return jax.shard_map(
        on_device,
        mesh=split,
        in_specs=(rows, rows, P(DP, None), rows)
        + (rows,) * 15
        + (expert_rows,) * 6
        + (whole,) * 12,
        out_specs=(rows, rows) + (rows,) * 20 + (expert_rows,) * 8 + (whole,) * 16,
        check_vma=False,
    )
```

```python
import functools
import math

import jax
import jax.numpy as jnp
from jax import lax
from jax.experimental import pallas as pl
from jax.experimental.pallas import tpu as pltpu
from jax.sharding import Mesh
from jax.sharding import PartitionSpec as P

D = 1536
HEADS = 48
HEAD_DIM = 64
STATE = 128
CONV = 4
EXPERT_FF = 512
SHARED_FF = 1024
STEP = 3
INNER = 3072
CONV_DIM = 3328
LANES = 128
CHUNK = 384

DP = ("zhi", "zlo", "core")
MATES = ("zlo", "core")
ALL = DP + ("expert",)

norm_eps = 1e-05
beta_one = 0.9
beta_two = 0.95
adam_eps = 1e-08
learn_rate = 0.02
decay_rate = 0.1
highest = lax.Precision.HIGHEST
bf16 = jnp.bfloat16
f32 = jnp.float32


def dot(left, right):
    return jnp.dot(left, right, preferred_element_type=f32)


def dot_nt(left, right):
    return lax.dot_general(left, right, (((1,), (1,)), ((), ())), preferred_element_type=f32)


def dot_tn(left, right):
    return lax.dot_general(left, right, (((0,), (0,)), ((), ())), preferred_element_type=f32)


def swap(pieces, axis):
    return lax.all_to_all(pieces, axis, split_axis=0, concat_axis=0, tiled=True)


def spread(block, axis):
    axes = (axis,) if isinstance(axis, str) else axis
    count = math.prod(lax.axis_size(one) for one in axes)
    return swap(jnp.broadcast_to(block[None], (count,) + block.shape), axis)


def to_partner(value):
    return lax.ppermute(value, "zhi", [(0, 1), (1, 0)])


def rms_scale(values):
    return lax.rsqrt(jnp.mean(values * values, axis=-1, keepdims=True) + norm_eps)


def silu_slope(values):
    sigmoid_value = jax.nn.sigmoid(values)
    return sigmoid_value * (1.0 + values * (1.0 - sigmoid_value))


def norm_back(grad_norm, unit_rows, scale_rows, gain):
    scaled = grad_norm * gain
    return scale_rows * (scaled - unit_rows * jnp.mean(scaled * unit_rows, axis=-1, keepdims=True))


def adam_step(weight, moment_one, moment_two, gradient):
    moment_one = beta_one * moment_one + (1.0 - beta_one) * gradient
    moment_two = beta_two * moment_two + (1.0 - beta_two) * gradient * gradient
    fixed_one = 1.0 - beta_one**STEP
    fixed_two = 1.0 - beta_two**STEP
    change = (
        moment_one / fixed_one / (jnp.sqrt(moment_two / fixed_two) + adam_eps) + decay_rate * weight
    )
    moved = -learn_rate * change
    return (gradient, weight + moved, moment_one, moment_two, moved)


def split_words(value):
    high = value.astype(bf16)
    rest = value - high.astype(f32)
    mid = rest.astype(bf16)
    low = (rest - mid.astype(f32)).astype(bf16)
    return high, mid, low


def join_words(words):
    return words[0].astype(f32) + words[1].astype(f32) + words[2].astype(f32)


def conv_rows(block, masks, params):
    total = params[CONV : CONV + 1] + params[0:1] * block
    for offset in range(1, CONV):
        total = total + params[offset : offset + 1] * (
            pltpu.roll(block, offset, 0) * masks[:, offset : offset + 1]
        )
    return total


def conv_rows_back(grad, block, masks, params):
    length = block.shape[0]
    taps = [jnp.sum(grad * block, axis=0, keepdims=True)]
    rows = params[0:1] * grad
    for offset in range(1, CONV):
        masked = grad * masks[:, offset : offset + 1]
        taps.append(jnp.sum(masked * pltpu.roll(block, offset, 0), axis=0, keepdims=True))
        rows = rows + pltpu.roll(params[offset : offset + 1] * masked, length - offset, 0)
    taps.append(jnp.sum(grad, axis=0, keepdims=True))
    return rows, taps


def dot_words(exact, value, contract):
    total = None
    for word in split_words(value):
        part = lax.dot_general(exact, word, (contract, ((), ())), preferred_element_type=f32)
        total = part if total is None else total + part
    return total


def dot_words_left(value, exact):
    total = None
    for word in split_words(value):
        part = jnp.dot(word, exact, preferred_element_type=f32)
        total = part if total is None else total + part
    return total


def softplus(value):
    return jnp.maximum(value, 0.0) + jnp.log1p(jnp.exp(-jnp.abs(value)))


def head_lanes(pair, transposed=False):
    rows = lax.broadcasted_iota(jnp.int32, (LANES, LANES), 0)
    lanes = lax.broadcasted_iota(jnp.int32, (LANES, LANES), 1)
    if transposed:
        rows, lanes = lanes, rows
    return (rows == 2 * pair + lanes // HEAD_DIM).astype(f32).astype(bf16)


def lane_of(matrix, lane):
    lanes = lax.broadcasted_iota(jnp.int32, matrix.shape, 1)
    return jnp.sum(jnp.where(lanes == lane, matrix, 0.0), axis=1, keepdims=True)


def scan_setup(dt_ref, packed_ref, conv_ref, masks, head_ref, doc_col, doc_row, inner,
               neg_ref, scores_ref, cum_ref, cum_t_ref):
    length = dt_ref.shape[0]
    pre_step = dt_ref[...] + head_ref[1:2]
    dt_step = softplus(pre_step)
    log_decay = -head_ref[0:1] * dt_step
    at = lax.broadcasted_iota(jnp.int32, (length, length), 0)
    to = lax.broadcasted_iota(jnp.int32, (length, length), 1)
    usable = (doc_col == doc_row) & (at >= to)
    neg_ref[...] = jnp.where(usable, 0.0, -1e30)
    exact = usable.astype(f32).astype(bf16)
    cum_ref[...] = dot_words(exact, log_decay, ((1,), (0,)))
    cum_t_ref[...] = cum_ref[...].T
    start = 2 * inner
    b_in = packed_ref[:, start : start + STATE].astype(f32)
    c_in = packed_ref[:, start + STATE : start + 2 * STATE].astype(f32)
    b_out = conv_rows(b_in, masks, conv_ref[:, inner : inner + STATE])
    c_out = conv_rows(c_in, masks, conv_ref[:, inner + STATE : inner + 2 * STATE])
    b_low = jax.nn.silu(b_out).astype(bf16)
    c_low = jax.nn.silu(c_out).astype(bf16)
    scores_ref[...] = dot_nt(c_low, b_low)
    return pre_step, dt_step, log_decay, exact, b_out, c_out, b_low, c_low


def pair_slices(pair, inner):
    at = pl.ds(pl.multiple_of(pair * LANES, LANES), LANES)
    x_at = pl.ds(pl.multiple_of(inner + pair * LANES, LANES), LANES)
    return at, x_at


def forward_kernel(x_ref, win_ref, gain_ref, conv_ref, masks_ref, head_ref, cols_ref, doc_col_ref,
                   doc_row_ref, wout_ref, gu_ref, gu_sent_ref, cot_ref, cot_came_ref,
                   packed_ref, dt_ref, y_ref, out_ref, gu_all_ref, gu_came_ref, cot_two_ref,
                   normed_ref, neg_ref, scores_ref, cum_ref, cum_t_ref, act_ref, square_ref,
                   send_sems, recv_sems, mate_send, mate_recv, mate_local, local_sems):
    greet(group_ids() + near_ids())
    count, me, _ = peers()
    sems = (send_sems, recv_sems)
    over = remote(gu_sent_ref, gu_came_ref, sems, 0, partner_id())
    weights = MateSpread(gu_ref, gu_all_ref, (mate_send, mate_recv), 0, mate_local)
    cots = [
        pltpu.make_async_copy(cot_ref, cot_two_ref.at[0], local_sems.at[0]),
        pltpu.make_async_copy(cot_came_ref, cot_two_ref.at[1, me], local_sems.at[1]),
    ]
    cots += spread_copies(cot_came_ref, cot_two_ref.at[1], sems, 1)
    over.start()
    weights.start()
    for copy in cots:
        copy.start()
    length = x_ref.shape[0]
    inner = wout_ref.shape[0]
    body = packed_ref.shape[1]
    step = 2 * LANES

    @pl.loop(0, length // LANES)
    def _(part):
        rows = pl.ds(pl.multiple_of(part * LANES, LANES), LANES)
        block = x_ref[rows, :].astype(f32)
        scale = lax.rsqrt(jnp.mean(block * block, axis=1, keepdims=True) + norm_eps)
        normed_ref[rows, :] = (block * scale * gain_ref[0:1]).astype(bf16)

    @pl.loop(0, body // step)
    def _(part):
        at = pl.ds(pl.multiple_of(part * step, step), step)
        packed_ref[:, at] = dot(normed_ref[...], win_ref[:, at]).astype(bf16)

    dt_ref[...] = dot(normed_ref[...], win_ref[:, body:])
    masks = masks_ref[...]
    _, dt_step, *_ = scan_setup(
        dt_ref, packed_ref, conv_ref, masks, head_ref, doc_col_ref[...], doc_row_ref[...], inner,
        neg_ref, scores_ref, cum_ref, cum_t_ref,
    )
    square_ref[...] = jnp.zeros_like(square_ref)
    lanes = lax.broadcasted_iota(jnp.int32, (LANES, LANES), 1)

    @pl.loop(0, inner // LANES)
    def _(pair):
        at, x_at = pair_slices(pair, inner)
        values = jax.nn.silu(conv_rows(packed_ref[:, x_at].astype(f32), masks, conv_ref[:, at]))
        dt_wide = dot_words_left(dt_step, head_lanes(pair))
        scaled = (values * dt_wide).astype(bf16)
        cum_cols = [lane_of(cum_ref[...], 2 * pair + k) for k in range(2)]
        cum_rows = [cum_t_ref[pl.ds(2 * pair + k, 1), :] for k in range(2)]
        outs = []
        for part in range(length // LANES):
            rows = slice(part * LANES, (part + 1) * LANES)
            wide = (part + 1) * LANES
            pieces = []
            for k in range(2):
                decay = jnp.exp(cum_cols[k][rows] - cum_rows[k][:, :wide] + neg_ref[rows, :wide])
                mixed = (decay * scores_ref[rows, :wide]).astype(bf16)
                pieces.append(dot(mixed, scaled[:wide]))
            outs.append(jnp.where(lanes < HEAD_DIM, pieces[0], pieces[1]))
        full_y = jnp.concatenate(outs, axis=0) + cols_ref[1:2, at] * values
        y_ref[:, at] = full_y.astype(bf16)
        gated = full_y * jax.nn.silu(packed_ref[:, at].astype(f32))
        square_ref[...] += gated * gated
        act_ref[:, at] = (gated * cols_ref[0:1, at]).astype(bf16)

    @pl.loop(0, D // step)
    def _(part):
        at = pl.ds(pl.multiple_of(part * step, step), step)
        out_ref[:, at] = dot(act_ref[...], wout_ref[:, at]).astype(bf16)

    squares = jnp.sum(square_ref[...], axis=1, keepdims=True)
    out_ref[:, D:] = word_lanes(squares)
    weights.forward()
    for copy in cots:
        copy.wait()
    over.wait()
    weights.finish()


def word_lanes(column):
    lanes = lax.broadcasted_iota(jnp.int32, (column.shape[0], LANES), 1)
    words = [word.astype(f32) for word in split_words(column)]
    row = jnp.where(lanes == 0, words[0], jnp.where(lanes == 1, words[1], words[2]))
    return jnp.where(lanes < 3, row, 0.0).astype(bf16)


def word_sum(words):
    return words[:, 0:1].astype(f32) + words[:, 1:2].astype(f32) + words[:, 2:3].astype(f32)


def backward_kernel(hid_ref, scale_ref, wout_ref, conv_ref, masks_ref, head_ref, cols_ref,
                    doc_col_ref, doc_row_ref, packed_ref, dt_ref, y_ref, sums_ref, came_one_ref, out_ref,
                    proj_ref, conv_grad_ref, cols_grad_ref, head_grad_ref, total_ref, wout_send_ref,
                    out_send_ref,
                    neg_ref, scores_ref, cum_ref, cum_t_ref, grad_scores_ref, row_ref, col_ref,
                    step_ref, scaled_ref, low_ref, wout_grad_ref, theirs_ref, out_got_ref, out_mine_ref, send_sem, recv_sem, out_send, out_recv,
                    out_local):
    greet(group_ids() + [partner_id()])
    tok = out_send_ref.shape[0]
    count = lax.axis_size("expert")
    out_sems = (out_send, out_recv)
    rows_all = out_ref.shape[0] // 2
    out_copies = reduce_copies(out_ref, out_got_ref, out_sems, 0, tok, rows_all)
    yours = pl.ds(pl.multiple_of(rows_all + lax.axis_index("expert") * tok, tok), tok)
    out_copies.append(pltpu.make_async_copy(out_ref.at[yours], out_mine_ref, out_local))
    for copy in out_copies:
        copy.start()
    half = lax.axis_index("zhi")
    held = sums_ref.shape[0]
    across = pltpu.make_async_remote_copy(
        src_ref=sums_ref.at[1, 1 - half], dst_ref=theirs_ref, send_sem=send_sem,
        recv_sem=recv_sem, device_id=partner_id(), device_id_type=pl.DeviceIdType.MESH,
    )
    across.start()
    length = dt_ref.shape[0]
    inner = wout_ref.shape[0]
    body = packed_ref.shape[1]
    scale_mix = word_sum(scale_ref[...])

    @pl.loop(0, inner // LANES)
    def _(pair):
        at, _ = pair_slices(pair, inner)
        gated = y_ref[:, at].astype(f32) * jax.nn.silu(packed_ref[:, at].astype(f32))
        act = (gated * scale_mix * cols_ref[0:1, at]).astype(bf16)
        wout_grad_ref[at, :] = dot_tn(act, hid_ref[:, :D]).astype(bf16)

    owners, rows_out, _ = wout_send_ref.shape
    real = inner // owners
    for k in range(owners):
        wout_send_ref[k, :real, :] = wout_grad_ref[k * real : (k + 1) * real, :]
        if real < rows_out:
            wout_send_ref[k, real:, :] = jnp.zeros((rows_out - real, D), bf16)
    for e in range(held):
        total_ref[half * held + e] = sums_ref[e, half]
    total_ref[(1 - half) * held] = came_one_ref[...]
    masks = masks_ref[...]
    pre_step, dt_step, log_decay, exact, b_out, c_out, b_low, c_low = scan_setup(
        dt_ref, packed_ref, conv_ref, masks, head_ref, doc_col_ref[...], doc_row_ref[...], inner,
        neg_ref, scores_ref, cum_ref, cum_t_ref,
    )
    grad_scores_ref[...] = jnp.zeros_like(grad_scores_ref)
    row_ref[...] = jnp.zeros_like(row_ref)
    col_ref[...] = jnp.zeros_like(col_ref)
    step_ref[...] = jnp.zeros_like(step_ref)
    conv_grad_ref[...] = jnp.zeros_like(conv_grad_ref)
    cols_grad_ref[...] = jnp.zeros_like(cols_grad_ref)
    head_grad_ref[...] = jnp.zeros_like(head_grad_ref)
    row_mean = word_sum(hid_ref[:, D:])
    lanes_all = lax.broadcasted_iota(jnp.int32, (length, LANES), 1)
    lanes = lax.broadcasted_iota(jnp.int32, (LANES, LANES), 1)

    @pl.loop(0, inner // LANES)
    def _(pair):
        at, x_at = pair_slices(pair, inner)
        grad_act = dot_nt(hid_ref[:, :D], wout_ref[at, :])
        conv_in = packed_ref[:, x_at].astype(f32)
        conv_out = conv_rows(conv_in, masks, conv_ref[:, at])
        values = jax.nn.silu(conv_out)
        gate_z = packed_ref[:, at].astype(f32)
        gate_act = jax.nn.silu(gate_z)
        full_y = y_ref[:, at].astype(f32)
        normed_mix = full_y * gate_act * scale_mix
        gain = cols_ref[0:1, at]
        skip = cols_ref[1:2, at]
        cols_grad_ref[0:1, at] = jnp.sum(grad_act * normed_mix, axis=0, keepdims=True)
        grad_gated = scale_mix * (grad_act * gain - normed_mix * row_mean)
        grad_y = grad_gated * gate_act
        proj_ref[:, at] = (grad_gated * full_y * silu_slope(gate_z)).astype(bf16)
        cols_grad_ref[1:2, at] = jnp.sum(grad_y * values, axis=0, keepdims=True)
        dt_wide = dot_words_left(dt_step, head_lanes(pair))
        scaled_low = (values * dt_wide).astype(bf16)
        low_ref[...] = grad_y.astype(bf16)
        scaled_ref[...] = jnp.zeros_like(scaled_ref)
        for k in range(2):
            head = 2 * pair + k
            cum_col = lane_of(cum_ref[...], head)
            cum_row = cum_t_ref[pl.ds(head, 1), :]
            for part in range(length // LANES):
                rows = slice(part * LANES, (part + 1) * LANES)
                wide = (part + 1) * LANES
                decay = jnp.exp(cum_col[rows] - cum_row[:, :wide] + neg_ref[rows, :wide])
                mixed = decay * scores_ref[rows, :wide]
                mine = jnp.where(lanes // HEAD_DIM == k, low_ref[rows, :].astype(f32), 0.0)
                mine = mine.astype(bf16)
                grad_mixed = dot_nt(mine, scaled_low[:wide])
                grad_scores_ref[rows, :wide] += grad_mixed * decay
                product = grad_mixed * mixed
                row_ref[rows, :] += jnp.where(
                    lanes == head, jnp.sum(product, axis=1, keepdims=True), 0.0
                )
                sums = jnp.sum(product, axis=0, keepdims=True)
                if part < length // LANES - 1:
                    sums = jnp.concatenate(
                        [sums, jnp.zeros((1, length - wide), f32)], axis=1
                    )
                col_sums = sums if part == 0 else col_sums + sums
                scaled_ref[:wide, :] += dot_tn(mixed.astype(bf16), mine)
            col_ref[pl.ds(head, 1), :] = col_sums
        grad_scaled = scaled_ref[...]
        step_ref[...] += dot_words_left(grad_scaled * values, head_lanes(pair, True))
        grad_values = grad_scaled * dt_wide + grad_y * skip
        grad_rows, taps = conv_rows_back(
            grad_values * silu_slope(conv_out), conv_in, masks, conv_ref[:, at]
        )
        proj_ref[:, x_at] = grad_rows.astype(bf16)
        for k in range(CONV + 1):
            conv_grad_ref[k : k + 1, at] = taps[k]

    grad_scores = grad_scores_ref[...].astype(bf16)
    for number, (grad, before) in enumerate(
        ((dot_tn(grad_scores, c_low), b_out), (dot(grad_scores, b_low), c_out))
    ):
        start = inner + number * STATE
        conv_in = packed_ref[:, inner + start : inner + start + STATE].astype(f32)
        grad_rows, taps = conv_rows_back(
            grad * silu_slope(before), conv_in, masks, conv_ref[:, start : start + STATE]
        )
        proj_ref[:, inner + start : inner + start + STATE] = grad_rows.astype(bf16)
        for k in range(CONV + 1):
            conv_grad_ref[k : k + 1, start : start + STATE] = taps[k]
    grad_cum = row_ref[...] - col_ref[...].T
    grad_decay = dot_words(exact, grad_cum, ((0,), (0,)))
    rate_abs = head_ref[0:1]
    grad_pre = (step_ref[...] - grad_decay * rate_abs) * jax.nn.sigmoid(pre_step)
    head_grad_ref[0:1] = jnp.sum(grad_decay * log_decay, axis=0, keepdims=True)
    head_grad_ref[1:2] = jnp.sum(grad_pre, axis=0, keepdims=True)
    proj_ref[:, body:] = grad_pre.astype(bf16)
    for copy in out_copies:
        copy.wait()
    total = out_mine_ref[...].astype(f32)
    for number in range(count - 1):
        total = total + out_got_ref[number].astype(f32)
    out_send_ref[...] = total.astype(bf16)
    across.wait()
    total_ref[(1 - half) * held + 1] = theirs_ref[...]


def route_kernel(two_ref, cot_ref, routes_ref, router_ref, ids_ref,
                 in_ref, top_ref, grad_ref, weights_ref, pick_ref, *, top_count, heads):
    tok = two_ref.shape[0]
    held, capacity, _ = in_ref.shape
    rows = two_ref[:, :D]
    logits = pltpu.roll(dot(rows, router_ref[...]), LANES - heads, 1)
    lanes = lax.broadcasted_iota(jnp.int32, (tok, LANES), 1)
    named = lanes < 0
    for k in range(top_count):
        named = named | (lanes == routes_ref[:, k : k + 1])
    top_logit = jnp.max(jnp.where(named, logits, -1e30), axis=1, keepdims=True)
    raised = jnp.where(named, jnp.exp(jnp.where(named, logits - top_logit, 0.0)), 0.0)
    weights = raised / jnp.sum(raised, axis=1, keepdims=True)
    weights_ref[...] = weights
    at = lax.broadcasted_iota(jnp.int32, (tok, tok), 0)
    to = lax.broadcasted_iota(jnp.int32, (tok, tok), 1)
    named_f = named.astype(f32)
    slot = dot((at > to).astype(f32).astype(bf16), named_f.astype(bf16))
    slots = lax.broadcasted_iota(jnp.int32, (tok, capacity), 1).astype(f32)
    picks = []
    for expert in range(held):
        lane = ids_ref[0] + expert
        mine = (lane_of(slot, lane) == slots) & (lane_of(named_f, lane) > 0.0)
        pick = mine.astype(f32).astype(bf16)
        picks.append(pick)
        in_ref[expert] = dot_tn(pick, rows).astype(bf16)
        top = dot_tn(pick, cot_ref[...])
        top_ref[expert] = top.astype(bf16)
        words = word_lanes(lane_of(weights, lane))
        slot_weight = jnp.sum(dot_tn(pick, words), axis=1, keepdims=True)
        grad_ref[expert] = (top * slot_weight).astype(bf16)
    pick_ref[0] = jnp.concatenate(picks, axis=1)


def expert_kernel(in_ref, top_ref, grad_ref, half_ref, gu_near_ref, gu_far_ref, down_near_ref,
                  down_far_ref, out_ref, back_ref, q_ref, sums_ref, mid_ref, act_ref):
    mates, _, rows_gu, _ = gu_near_ref.shape
    rows_down = down_near_ref.shape[2]
    shards = [(h, m) for h in range(2) for m in range(mates)]
    half = half_ref[0]
    sides = (
        (half, gu_near_ref, down_near_ref),
        (1 - half, gu_far_ref, down_far_ref),
    )

    def joined(ref, at, which=range(mates)):
        return jnp.concatenate([ref[m, 0, :, at] for m in which], axis=0)

    def block(place, size, offset=0):
        return pl.ds(pl.multiple_of(offset + place * size, LANES), size)

    wide = D // 2
    tall = EXPERT_FF // 2
    for place, _, down in sides:
        at = block(place, tall)
        up_at = block(place, tall, EXPERT_FF)
        gate = sum(
            dot(in_ref[0, :, block(side, wide)], joined(gu, at)) for side, gu, _ in sides
        )
        up = sum(
            dot(in_ref[0, :, block(side, wide)], joined(gu, up_at)) for side, gu, _ in sides
        )
        silu = jax.nn.silu(gate)
        mid_ref[:, at] = (silu * up).astype(bf16)
        grad_mid = dot_nt(grad_ref[0], joined(down, slice(None)))
        act_ref[:, at] = (grad_mid * up * silu_slope(gate)).astype(bf16)
        act_ref[:, up_at] = (grad_mid * silu).astype(bf16)
    step = 384
    each = step // rows_gu
    for side, gu, _ in sides:
        for part in range(wide // step):
            rows = joined(gu, slice(None), range(part * each, (part + 1) * each))
            at = pl.ds(pl.multiple_of(side * wide + part * step, LANES), step)
            back_ref[0, :, at] = dot_nt(act_ref[...], rows).astype(bf16)
    q = jnp.zeros((in_ref.shape[1], 1), f32)
    for part in range(D // step):
        at = slice(part * step, (part + 1) * step)
        rows = sum(dot(mid_ref[:, block(side, tall)], joined(down, at)) for side, _, down in sides)
        out_ref[0, :, at] = rows.astype(bf16)
        q = q + jnp.sum(rows * top_ref[0, :, at].astype(f32), axis=1, keepdims=True)
        chosen = shards[part * each : (part + 1) * each]
        for number in range(2):
            half_at = slice(number * EXPERT_FF, (number + 1) * EXPERT_FF)
            total = dot_tn(in_ref[0, :, at], act_ref[:, half_at]).astype(bf16)
            for k, (h, m) in enumerate(chosen):
                sums_ref[m, 0, h, number * rows_gu : (number + 1) * rows_gu, :] = total[
                    k * rows_gu : (k + 1) * rows_gu
                ]
    q_ref[0] = jnp.broadcast_to(q, q_ref.shape[1:])
    for part in range(D // EXPERT_FF):
        total = dot_tn(mid_ref[...], grad_ref[0, :, part * EXPERT_FF : (part + 1) * EXPERT_FF])
        total = total.astype(bf16)
        start = 2 * rows_gu + part * rows_down
        for k, (h, m) in enumerate(shards):
            sums_ref[m, 0, h, start : start + rows_down, :] = total[
                k * rows_down : (k + 1) * rows_down
            ]


def combine_kernel(pick_ref, weights_ref, ids_ref, out_ref, back_ref, q_ref, own_out_ref,
                   own_back_ref, mix_ref, rows_ref):
    held = out_ref.shape[0]
    capacity = out_ref.shape[1]
    block = pl.program_id(0)
    own = (block < pl.num_programs(0) // 2).astype(f32)
    picks = [pick_ref[0, :, e * capacity : (e + 1) * capacity] for e in range(held)]
    mix = own_out_ref[...].astype(f32) * own
    back = own_back_ref[...].astype(f32) * own
    lanes = lax.broadcasted_iota(jnp.int32, (pick_ref.shape[1], LANES), 1)
    words = jnp.zeros((pick_ref.shape[1], LANES), f32)
    for expert in range(held):
        weight = lane_of(weights_ref[...], ids_ref[0] + expert)
        mix = mix + weight * dot(picks[expert], out_ref[expert])
        back = back + dot(picks[expert], back_ref[expert])
        token_q = jnp.sum(dot(picks[expert], word_lanes(q_ref[expert, :, :1])), axis=1,
                          keepdims=True)
        for k, word in enumerate(split_words(token_q)):
            words = jnp.where(lanes == k * held + expert, word.astype(f32), words)
    mix_ref[...] = mix.astype(bf16)
    rows_ref[:, :D] = back.astype(bf16)
    rows_ref[:, D:] = words.astype(bf16)


def peers():
    count = lax.axis_size("expert")
    me = lax.axis_index("expert")
    return count, me, [lax.rem(me + step, count) for step in range(1, count)]


def group_ids():
    return [{"expert": other} for other in peers()[2]]


def partner_id():
    return {"zhi": 1 - lax.axis_index("zhi")}


def core_id():
    return {"core": 1 - lax.axis_index("core")}


def mate_ids():
    count, me = lax.axis_size("zlo"), lax.axis_index("zlo")
    return [lax.rem(me + step, count) for step in range(1, count)]


def greet(targets):
    barrier = pltpu.get_barrier_semaphore()
    for target in targets:
        pl.semaphore_signal(
            barrier, inc=1, device_id=target, device_id_type=pl.DeviceIdType.MESH
        )
    pl.semaphore_wait(barrier, len(targets))


def remote(src, dst, sems, number, target):
    return pltpu.make_async_remote_copy(
        src_ref=src, dst_ref=dst, send_sem=sems[0].at[number], recv_sem=sems[1].at[number],
        device_id=target, device_id_type=pl.DeviceIdType.MESH,
    )


def spread_copies(src, dst, sems, base):
    _, me, others = peers()
    return [
        remote(src, dst.at[me], sems, base + number, {"expert": other})
        for number, other in enumerate(others)
    ]


def reduce_copies(src, dst, sems, base, rows, start):
    _, _, others = peers()
    return [
        remote(
            src.at[pl.ds(pl.multiple_of(start + other * rows, rows), rows)],
            dst.at[number], sems, base + number, {"expert": other},
        )
        for number, other in enumerate(others)
    ]


def reduced(src, dst, rows, start, columns):
    _, me, others = peers()
    total = src[pl.ds(pl.multiple_of(start + me * rows, rows), rows), columns].astype(f32)
    for number in range(len(others)):
        total = total + dst[number, :, columns].astype(f32)
    return total


class MateSpread:
    def __init__(self, rows, full, sems, base, local_sem):
        planes = mate_ids()
        core, me = lax.axis_index("core"), lax.axis_index("zlo")
        slot = me * 2 + core
        self.over = [
            remote(rows, full.at[slot], sems, base + number, {"zlo": mate})
            for number, mate in enumerate(planes)
        ]
        count = len(planes)
        self.beside = [remote(rows, full.at[slot], sems, base + count, core_id())]
        size = count + 1
        self.onward = [
            remote(
                full.at[lax.rem(me + size - 1 - number, size) * 2 + core],
                full.at[lax.rem(me + size - 1 - number, size) * 2 + core],
                sems, base + count + 1 + number, core_id(),
            )
            for number in range(count)
        ]
        self.own = pltpu.make_async_copy(rows, full.at[slot], local_sem)

    def start(self):
        for copy in self.over + self.beside + [self.own]:
            copy.start()

    def forward(self):
        for copy, onward in zip(self.over, self.onward):
            copy.wait()
            onward.start()

    def finish(self):
        for copy in self.beside + self.onward + [self.own]:
            copy.wait()


def mate_sems(planes):
    return 2 * planes - 1


def near_ids():
    return [partner_id(), core_id()] + [{"zlo": mate} for mate in mate_ids()]


def plane_place():
    planes = lax.axis_size("zlo")
    return lax.axis_index("zhi") * planes + lax.axis_index("zlo"), 2 * planes


def plane_id(plane):
    planes = lax.axis_size("zlo")
    return {"zhi": plane // planes, "zlo": lax.rem(plane, planes)}


def line_sems(count):
    return [
        pltpu.SemaphoreType.DMA((count - 1,)), pltpu.SemaphoreType.DMA((count - 1,)),
        pltpu.SemaphoreType.DMA((count - 1,)), pltpu.SemaphoreType.DMA((count - 1,)),
        pltpu.SemaphoreType.DMA((2 * count - 1,)), pltpu.SemaphoreType.DMA((2 * count - 1,)),
    ]


class LineGather:
    def __init__(self, full, sems):
        self.full = full
        self.up, self.down, self.side = sems[0:2], sems[2:4], sems[4:6]
        self.core = lax.axis_index("core")
        self.at, self.count = plane_place()

    def block(self, plane):
        return self.full.at[plane * 2 + self.core]

    def move(self, plane, sems, number, target):
        return remote(self.block(plane), self.block(plane), sems, number, target)

    def upward(self, step):
        return self.move(self.at - step, self.up, step, plane_id(self.at + 1))

    def downward(self, step):
        return self.move(self.at + step, self.down, step, plane_id(self.at - 1))

    def sends_up(self, step):
        return (self.at < self.count - 1) & (self.at >= step)

    def sends_down(self, step):
        return (self.at > 0) & (self.at + step < self.count)

    def gets_up(self, step):
        return self.at >= step + 1

    def gets_down(self, step):
        return self.at + step + 1 < self.count

    def beside(self, plane, number):
        return self.move(plane, self.side, number, core_id())

    def start(self):
        pl.when(self.sends_up(0))(lambda: self.upward(0).start())
        pl.when(self.sends_down(0))(lambda: self.downward(0).start())
        self.beside(self.at, 0).start()

    def step(self, step):
        def from_below():
            self.move(self.at - step - 1, self.up, step, plane_id(self.at)).wait_recv()
            self.beside(self.at - step - 1, 1 + step).start()

        def from_above():
            self.move(self.at + step + 1, self.down, step, plane_id(self.at)).wait_recv()
            self.beside(self.at + step + 1, self.count + step).start()

        pl.when(self.gets_up(step))(from_below)
        if step + 1 < self.count - 1:
            pl.when(self.sends_up(step + 1))(lambda: self.upward(step + 1).start())
        pl.when(self.gets_down(step))(from_above)
        if step + 1 < self.count - 1:
            pl.when(self.sends_down(step + 1))(lambda: self.downward(step + 1).start())

    def finish(self):
        self.beside(self.at, 0).wait()
        for step in range(self.count - 1):
            pl.when(self.sends_up(step))(lambda step=step: self.upward(step).wait_send())
            pl.when(self.sends_down(step))(lambda step=step: self.downward(step).wait_send())
            pl.when(self.gets_up(step))(
                lambda step=step: self.beside(self.at - step - 1, 1 + step).wait()
            )
            pl.when(self.gets_down(step))(
                lambda step=step: self.beside(self.at + step + 1, self.count + step).wait()
            )


def start_kernel(lengths_ref, x_ref, cot_ref, routes_ref, w_in_ref, w_router_ref, w_sgu_ref, w_out_ref,
                 w_sd_ref, gu_ref, down_ref, conv_ref, head_ref, mixer_ref,
                 x_all_ref, cot_all_ref, cot_came_ref, routes_two_ref, win_all_ref, sgu_all_ref,
                 wout_own_ref, sd_own_ref, masks_ref, doc_col_ref, doc_row_ref, gu_kept_ref,
                 gu_sent_ref, down_kept_ref, down_sent_ref, conv_own_ref, head_own_ref, cols_ref,
                 wout_all_ref, sd_all_ref, routes_came_ref, win_ref, sgu_ref, wout_ref, sd_ref,
                 tail_ref, send_sems, recv_sems, out_send, out_recv, near_send, near_recv,
                 local_sems, *line):
    count, me, others = peers()
    at, planes = plane_place()
    half = lax.axis_index("zhi")
    sems = (send_sems, recv_sems)
    near = (near_send, near_recv)
    barrier = pltpu.get_barrier_semaphore()

    def tell(target):
        pl.semaphore_signal(
            barrier, inc=1, device_id=target, device_id_type=pl.DeviceIdType.MESH
        )

    for target in group_ids() + [partner_id(), core_id()]:
        tell(target)
    pl.when(at > 0)(lambda: tell(plane_id(at - 1)))
    pl.when(at < planes - 1)(lambda: tell(plane_id(at + 1)))
    ends = (at > 0).astype(jnp.int32) + (at < planes - 1).astype(jnp.int32)
    pl.semaphore_wait(barrier, count + 1 + ends)

    slot = at * 2 + lax.axis_index("core")
    peer_count = len(others)

    def pieces(src, dst, base, local):
        copies = [
            remote(src.at[other], dst.at[slot, me], sems, base + number, {"expert": other})
            for number, other in enumerate(others)
        ]
        return copies + [pltpu.make_async_copy(src.at[me], dst.at[slot, me], local)]

    def shared_rows(src, dst, base, local):
        return spread_copies(src, dst, sems, base) + [
            pltpu.make_async_copy(src, dst.at[me], local)
        ]

    def started(copies):
        for copy in copies:
            copy.start()
        return copies

    def ended(copies):
        for copy in copies:
            copy.wait()

    lines = [
        LineGather(full, line[6 * k : 6 * k + 6])
        for k, full in enumerate((win_all_ref, wout_all_ref, sgu_all_ref, sd_all_ref))
    ]
    inner = INNER // count
    heads = HEADS // count
    own_ff = SHARED_FF // count
    body = 2 * inner + 2 * STATE
    tail_ref[...] = jnp.zeros_like(tail_ref)
    tail_ref[0, :, :HEADS] = w_in_ref[:, 2 * INNER + 2 * STATE :]
    tail_ref[1, :, : w_router_ref.shape[1]] = w_router_ref[...]
    lanes_in = lax.broadcasted_iota(jnp.int32, tail_ref.shape[1:], 1)
    routers = pltpu.roll(tail_ref[1], heads, 1)
    for g in range(count):
        win_ref[g, :, :inner] = w_in_ref[:, g * inner : (g + 1) * inner].astype(bf16)
        win_ref[g, :, inner : 2 * inner] = w_in_ref[
            :, INNER + g * inner : INNER + (g + 1) * inner
        ].astype(bf16)
        win_ref[g, :, 2 * inner : body] = w_in_ref[:, 2 * INNER : 2 * INNER + 2 * STATE].astype(
            bf16
        )
        steps = pltpu.roll(tail_ref[0], LANES - g * heads, 1) if g else tail_ref[0]
        win_ref[g, :, body:] = jnp.where(lanes_in < heads, steps, routers).astype(bf16)
    win_copies = started(pieces(win_ref, win_all_ref, 0, local_sems.at[0]))
    wout_ref[...] = w_out_ref[...].astype(bf16)
    sd_ref[...] = w_sd_ref[...].astype(bf16)
    for g in range(count):
        for k in range(2):
            start = k * SHARED_FF + g * own_ff
            sgu_ref[g, :, k * own_ff : (k + 1) * own_ff] = w_sgu_ref[
                :, start : start + own_ff
            ].astype(bf16)
    keep = started([
        pltpu.make_async_copy(wout_ref, wout_all_ref.at[slot], local_sems.at[1]),
        pltpu.make_async_copy(sd_ref, sd_all_ref.at[slot], local_sems.at[2]),
    ])
    ended(keep)
    lines[1].start()
    lines[3].start()
    sgu_copies = started(pieces(sgu_ref, sgu_all_ref, peer_count, local_sems.at[3]))
    routes_over = started([remote(routes_ref, routes_came_ref, near, 1, partner_id())])
    ended(win_copies)
    lines[0].start()
    wide = started(
        shared_rows(x_ref, x_all_ref, 2 * peer_count, local_sems.at[4])
        + shared_rows(cot_ref, cot_all_ref, 4 * peer_count, local_sems.at[6])
        + shared_rows(routes_ref, routes_two_ref.at[0], 3 * peer_count, local_sems.at[5])
    )
    for step in range(planes - 1):
        lines[1].step(step)
        lines[3].step(step)
    lines[1].finish()
    lines[3].finish()
    rows = wout_own_ref.shape[0]
    out_copies = []
    for j in range(rows):
        for k, (full, own) in enumerate(
            ((wout_all_ref, wout_own_ref), (sd_all_ref, sd_own_ref))
        ):
            base = (2 * j + k) * peer_count
            for number, other in enumerate(others):
                out_copies.append(remote(
                    full.at[other * rows + j], own.at[j, me], (out_send, out_recv),
                    base + number, {"expert": other},
                ))
            out_copies.append(pltpu.make_async_copy(
                full.at[me * rows + j], own.at[j, me], local_sems.at[9 + 2 * j + k]
            ))
    started(out_copies)
    lines[0].step(0)
    ended(sgu_copies)
    lines[2].start()
    cot_over = started([remote(cot_ref, cot_came_ref, near, 0, partner_id())])

    at_inner = pl.ds(pl.multiple_of(me * inner, LANES), inner)
    conv_own_ref[...] = jnp.zeros_like(conv_own_ref)
    conv_own_ref[: CONV + 1, :inner] = conv_ref[:, at_inner]
    conv_own_ref[: CONV + 1, inner:] = conv_ref[:, INNER:]
    tail_ref[0] = jnp.zeros_like(tail_ref[0])
    tail_ref[0, :3, :HEADS] = head_ref[...]
    mine = tail_ref[0, :8, :]
    for g in range(1, count):
        moved = pltpu.roll(tail_ref[0, :8, :], LANES - g * heads, 1)
        mine = jnp.where(me == g, moved, mine)
    lane_eight = lax.broadcasted_iota(jnp.int32, mine.shape, 1)
    row_eight = lax.broadcasted_iota(jnp.int32, mine.shape, 0)
    mine = jnp.where((lane_eight < heads) & (row_eight < 3), mine, 0.0)
    head_own_ref[...] = jnp.where(
        (row_eight == 0) & (lane_eight < heads), jnp.exp(mine), mine
    )
    cols_ref[...] = jnp.zeros_like(cols_ref)
    cols_ref[0:1, :] = mixer_ref[:, at_inner]
    for pair in range(inner // LANES):
        cols_ref[1:2, pair * LANES : (pair + 1) * LANES] = dot_words_left(
            mine, head_lanes(pair)
        )[2:3]
    length = masks_ref.shape[0]
    place = lax.broadcasted_iota(jnp.int32, (length, LANES), 0)
    lane = lax.broadcasted_iota(jnp.int32, (length, LANES), 1)
    across = lax.broadcasted_iota(jnp.int32, (1, length), 1)
    doc, earlier, doc_row = place * 0 - 1, place * 0 - 1, across * 0 - 1
    start = 0
    for k in range(lengths_ref.shape[1]):
        doc = doc + (place >= start).astype(jnp.int32)
        earlier = earlier + (place - lane >= start).astype(jnp.int32)
        doc_row = doc_row + (across >= start).astype(jnp.int32)
        start = start + lengths_ref[0, k]
    masks_ref[...] = (doc == earlier).astype(f32)
    doc_col_ref[...] = doc[:, :1]
    doc_row_ref[...] = doc_row
    held = gu_kept_ref.shape[0]
    for e in range(held):
        gu_kept_ref[e] = gu_ref[half * held + e].astype(bf16)
        gu_sent_ref[e] = gu_ref[(1 - half) * held + e].astype(bf16)
        down_kept_ref[e] = down_ref[half * held + e].astype(bf16)
        down_sent_ref[e] = down_ref[(1 - half) * held + e].astype(bf16)

    ended(routes_over)
    wide += started(
        shared_rows(routes_came_ref, routes_two_ref.at[1], 5 * peer_count, local_sems.at[7])
    )
    for step in range(1, planes - 1):
        lines[0].step(step)
        lines[2].step(step - 1)
    lines[2].step(planes - 2)
    lines[0].finish()
    lines[2].finish()
    ended(wide + out_copies + cot_over)


def hidden_kernel(part_ref, tokens_ref, gain_ref, down_ref, down_sent_ref,
                  hidden_ref, res_ref, two_ref, down_all_ref, down_came_ref,
                  got_ref, send_sems, recv_sems, mate_send, mate_recv, mate_local):
    tok = tokens_ref.shape[0]
    sems = (send_sems, recv_sems)
    greet(group_ids() + near_ids())
    copies = reduce_copies(part_ref, got_ref, sems, 0, tok, 0)
    over = remote(down_sent_ref, down_came_ref, sems, len(copies), partner_id())
    weights = MateSpread(down_ref, down_all_ref, (mate_send, mate_recv), 0, mate_local)
    for copy in copies + [over]:
        copy.start()
    weights.start()
    for copy in copies:
        copy.wait()
    squares = word_sum(reduced(part_ref, got_ref, tok, 0, slice(D, D + LANES)))
    scale_mix = lax.rsqrt(squares / INNER + norm_eps)
    res = reduced(part_ref, got_ref, tok, 0, slice(0, D)) * scale_mix
    res_ref[...] = res
    hidden = tokens_ref[...].astype(f32) + res
    hidden_ref[...] = hidden
    scale = lax.rsqrt(jnp.mean(hidden * hidden, axis=1, keepdims=True) + norm_eps)
    two_ref[:, :D] = (hidden * scale * gain_ref[1:2]).astype(bf16)
    two_ref[:, D:] = word_lanes(scale_mix)
    weights.forward()
    over.wait()
    weights.finish()


def share_kernel(two_ref, gu_ref, down_ref, cot_ref, sgu_ref, sd_ref,
                 two_all_ref, gu_all_ref, down_all_ref, out_ref, back_ref, grad_gu_ref,
                 grad_down_ref, came_ref, rows_ref, mid_ref, act_ref,
                 send_sems, recv_sems, mate_send, mate_recv, local_sems):
    count, me, _ = peers()
    sems = (send_sems, recv_sems)
    mate = (mate_send, mate_recv)
    own_ref, other_ref = two_all_ref.at[0], two_all_ref.at[1]
    greet(group_ids() + near_ids())
    over = remote(two_ref, came_ref, sems, 0, partner_id())
    over.start()
    first = spread_copies(two_ref, own_ref, sems, 1)
    for copy in first:
        copy.start()
    mine = pltpu.make_async_copy(two_ref, own_ref.at[me], local_sems.at[0])
    mine.start()
    step = (mate_send.shape[0]) // 2
    gu_weights = MateSpread(gu_ref, gu_all_ref, mate, 0, local_sems.at[1])
    down_weights = MateSpread(down_ref, down_all_ref, mate, step, local_sems.at[2])
    gu_weights.start()
    down_weights.start()
    over.wait()
    second = spread_copies(came_ref, other_ref, sems, count)
    for copy in second:
        copy.start()
    theirs = pltpu.make_async_copy(came_ref, other_ref.at[me], local_sems.at[3])
    theirs.start()
    for copy in first:
        copy.wait()
    mine.wait()

    length, width = rows_ref.shape[0], sd_ref.shape[0]
    tok = two_ref.shape[0]
    for g in range(count):
        rows_ref[g * tok : (g + 1) * tok, :] = two_all_ref[0, g, :, :D]
    gate = dot(rows_ref[...], sgu_ref[:, :width])
    up = dot(rows_ref[...], sgu_ref[:, width:])
    silu = jax.nn.silu(gate)
    mid_ref[...] = (silu * up).astype(bf16)
    grad_mid = dot_nt(cot_ref[:length, :], sd_ref[...])
    act_ref[:, :width] = (grad_mid * up * silu_slope(gate)).astype(bf16)
    act_ref[:, width:] = (grad_mid * silu).astype(bf16)
    gu_weights.forward()

    @pl.loop(0, D // 256)
    def _(part):
        at = pl.ds(pl.multiple_of(part * 256, 256), 256)
        out_ref[:, at] = dot(mid_ref[...], sd_ref[:, at]).astype(bf16)
        back_ref[:, at] = dot_nt(act_ref[...], sgu_ref[at, :]).astype(bf16)

    owners, rows_down, _ = grad_down_ref.shape
    real = width // owners
    total = dot_tn(mid_ref[...], cot_ref[:length, :]).astype(bf16)
    for k in range(owners):
        grad_down_ref[k, :real, :] = total[k * real : (k + 1) * real]
        if real < rows_down:
            grad_down_ref[k, real:, :] = jnp.zeros((rows_down - real, D), bf16)
    each = D // owners
    wide = max(each, 384)
    for part in range(D // wide):
        total = dot_tn(rows_ref[:, part * wide : (part + 1) * wide], act_ref[...]).astype(bf16)
        for k in range(wide // each):
            owner = part * (wide // each) + k
            grad_gu_ref[owner // 2, owner % 2] = total[k * each : (k + 1) * each]
    for copy in second:
        copy.wait()
    theirs.wait()
    down_weights.forward()
    gu_weights.finish()
    down_weights.finish()


def q_lanes(sources, held, own_experts, half):
    lanes = lax.broadcasted_iota(jnp.int32, sources[0][1].shape, 1)
    total = jnp.zeros(lanes.shape, f32)
    for place, words in sources:
        for expert in range(held):
            value = sum(
                words[:, k * held + expert : k * held + expert + 1].astype(f32) for k in range(3)
            )
            lane = place * own_experts + half * held + expert
            total = jnp.where(lanes == lane, value, total)
    return total


def sum_plane(sums_ref, part_ref, slots_ref, expert):
    me = lax.axis_index("zlo")
    for h in range(sums_ref.shape[1]):
        total = part_ref[me, expert, h].astype(f32)
        for number in range(slots_ref.shape[0]):
            total = total + slots_ref[number, expert, h].astype(f32)
        sums_ref[expert, h] = total.astype(bf16)


def back_kernel(back_ref, hidden_ref, res_ref, cot_ref, weights_ref, router_ref, gain_ref, grads_ref,
                all_ref, grad_hidden_ref, grad_logits_ref, gain_grad_ref, sums_ref, theirs_ref,
                got_other_ref, got_own_ref, send_ref, came_ref, low_ref, slots_ref, core_ref, mine_ref,
                send_sems, recv_sems, plane_send, plane_recv, core_send, core_recv, mine_sems,
                local_sem, *, own_experts, heads):
    tok = cot_ref.shape[0]
    length = back_ref.shape[0] // 2
    held = own_experts // 2
    count, me, others = peers()
    half = lax.axis_index("zhi")
    sems = (send_sems, recv_sems)
    words_at = slice(D, D + LANES)
    mates = mate_ids()
    greet(group_ids() + near_ids())
    core = lax.axis_index("core")
    planes_here = core_ref.shape[0]
    core_copies = [
        [
            remote(
                grads_ref.at[z, 1 - core, expert], core_ref.at[z, expert], (core_send, core_recv),
                expert * planes_here + z, core_id(),
            )
            for z in range(planes_here)
        ]
        for expert in range(held)
    ]
    plane_sems = (plane_send, plane_recv)
    planes = [
        [
            remote(
                core_ref.at[mate, expert], slots_ref.at[number, expert], plane_sems,
                expert * len(mates) + number, {"zlo": mate},
            )
            for number, mate in enumerate(mates)
        ]
        for expert in range(held)
    ]
    first = reduce_copies(back_ref, got_other_ref, sems, 0, tok, length)
    second = reduce_copies(back_ref, got_own_ref, sems, count - 1, tok, 0)
    loads = [
        pltpu.make_async_copy(grads_ref.at[z, core], mine_ref.at[z], mine_sems.at[z])
        for z in range(planes_here)
    ]
    for copy in loads + first + core_copies[0] + core_copies[1]:
        copy.start()
    for copy in loads:
        copy.wait()
    for expert in range(held):
        for z, copy in enumerate(core_copies[expert]):
            copy.wait()
            for h in range(2):
                core_ref[z, expert, h] = (
                    core_ref[z, expert, h].astype(f32) + mine_ref[z, expert, h].astype(f32)
                ).astype(bf16)
        if expert == 0:
            for copy in planes[0]:
                copy.start()

    def q_of(start, slots):
        mine = back_ref[pl.ds(pl.multiple_of(start + me * tok, tok), tok), words_at]
        sources = [(me, mine)]
        for number in range(count - 1):
            sources.append((lax.rem(me + count - 1 - number, count), slots[number, :, words_at]))
        return q_lanes(sources, held, own_experts, half)

    for copy in first:
        copy.wait()
    send_ref[:, :D] = reduced(back_ref, got_other_ref, tok, length, slice(0, D)).astype(bf16)
    lanes = lax.broadcasted_iota(jnp.int32, (tok, LANES), 1)
    words = jnp.zeros((tok, LANES), f32)
    shift = LANES // 4
    for k, word in enumerate(split_words(q_of(length, got_other_ref))):
        placed = word.astype(f32) if k == 0 else pltpu.roll(word.astype(f32), k * shift, 1)
        words = words + placed
    send_ref[:, D:] = words.astype(bf16)
    over = remote(send_ref, came_ref, sems, 2 * (count - 1), {"zhi": 1 - half})
    over.start()
    for copy in second:
        copy.start()
    for copy in planes[0]:
        copy.wait()
    for copy in planes[1]:
        copy.start()
    sum_plane(sums_ref, core_ref, slots_ref, 0)
    across = remote(
        sums_ref.at[0, 1 - half], theirs_ref, plane_sems, held * len(mates), partner_id()
    )
    for copy in second:
        copy.wait()
    q_own = q_of(0, got_own_ref)
    total = reduced(back_ref, got_own_ref, tok, 0, slice(0, D))
    over.wait()
    across.start()
    came = came_ref[:, D:].astype(f32)
    came = came + pltpu.roll(came, LANES - shift, 1) + pltpu.roll(came, LANES - 2 * shift, 1)
    q = q_own + jnp.where(lanes < shift, came, 0.0)
    weights = weights_ref[...]
    grad_logits = weights * (q - jnp.sum(weights * q, axis=1, keepdims=True))
    grad_logits_ref[...] = grad_logits.astype(bf16)
    placed_logits = pltpu.roll(grad_logits, heads, 1).astype(bf16)
    total = total + came_ref[:, :D].astype(f32) + dot_nt(placed_logits, router_ref[...])
    hidden = hidden_ref[...]
    scale = lax.rsqrt(jnp.mean(hidden * hidden, axis=1, keepdims=True) + norm_eps)
    unit = hidden * scale
    gain_grad_ref[...] = jnp.broadcast_to(
        jnp.sum(total * unit, axis=0, keepdims=True), gain_grad_ref.shape
    )
    grad_hidden = cot_ref[...].astype(f32) + norm_back(total, unit, scale, gain_ref[1:2])
    grad_hidden_ref[...] = grad_hidden
    low_ref[:, :D] = grad_hidden.astype(bf16)
    row_mean = jnp.sum(low_ref[:, :D].astype(f32) * res_ref[...], axis=1, keepdims=True) / INNER
    low_ref[:, D:] = word_lanes(row_mean)
    third = spread_copies(low_ref, all_ref, sems, 2 * count - 1)
    for copy in third:
        copy.start()
    mine = pltpu.make_async_copy(low_ref, all_ref.at[me], local_sem)
    mine.start()
    for copy in planes[1]:
        copy.wait()
    sum_plane(sums_ref, core_ref, slots_ref, 1)
    for copy in third:
        copy.wait()
    mine.wait()
    across.wait()


def dense_kernel(x_ref, tokens_ref, win_ref, gain_ref, proj_ref, two_ref, logits_ref, sgu_ref,
                 wout_ref, down_ref, grad_hidden_ref, out_ref, out_send_ref, hidden_ref,
                 conv_ref, cols_ref,
                 head_ref, gain_two_ref,
                 got_ref, own_out_ref, own_down_ref, tokens_grad_ref, output_ref, all_small_ref,
                 normed_ref, first_ref, second_ref, core_ref, slots_ref, plane_ref, came_ref,
                 send_ref, one_ref, one_got_ref, out_came_ref, out_got_ref, out_mine_ref, scale_ref,
                 step_ref, step_came_ref, core_send, core_recv, plane_send,
                 plane_recv, half_send, half_recv, row_send, row_recv, one_send, one_recv, out_send,
                 out_recv, small_send, small_recv, fold_send, fold_recv, local_sems, fold_sems,
                 own_sems, *, shared_chunks, heads):
    length = x_ref.shape[0]
    tok = tokens_ref.shape[0]
    chunks_one = first_ref.shape[0]
    chunks = core_ref.shape[0]
    own_rows = first_ref.shape[3]
    rows_in = send_ref.shape[2]
    core, half, zlo = lax.axis_index("core"), lax.axis_index("zhi"), lax.axis_index("zlo")
    mates = mate_ids()
    count, me, others = peers()
    planes = core_ref.shape[1] // 2
    greet(group_ids() + near_ids())

    def source(chunk):
        if chunk < chunks_one:
            return first_ref.at[chunk]
        start = (chunk - chunks_one) * CHUNK
        return second_ref.at[:, :, :, start : start + CHUNK]

    wide_out = D * wout_ref.shape[1] // own_rows
    wide_down = D * down_ref.shape[1] // own_rows
    start = wide_out + wide_down
    beside = pltpu.make_async_copy(
        sgu_ref, second_ref.at[:, :, :, start : start + sgu_ref.shape[3]], own_sems.at[0]
    )
    beside.start()
    each = wout_ref.shape[0] // count
    fold_copies = []
    number = 0
    local = 0
    for full, width, offset in ((wout_ref, wide_out, 0), (down_ref, wide_down, wide_out)):
        rows = full.shape[1]
        for j in range(each):
            for fold in range(D // width):
                columns = slice(fold * width, (fold + 1) * width)
                place = pl.ds(fold * rows, rows)
                owner = me * each + j
                target = second_ref.at[
                    owner // 2, lax.rem(owner, 2), place, offset : offset + width
                ]
                for other in others:
                    fold_copies.append(remote(
                        full.at[j * count + other, :, columns], target, (fold_send, fold_recv),
                        number, {"expert": other},
                    ))
                    number += 1
                fold_copies.append(pltpu.make_async_copy(
                    full.at[j * count + me, :, columns], target, fold_sems.at[local]
                ))
                local += 1
    for copy in fold_copies:
        copy.start()

    core_copies, plane_copies, half_copies, row_copies = {}, {}, {}, {}

    def send_core(chunk):
        copies = [
            pltpu.make_async_remote_copy(
                src_ref=source(chunk).at[:, 1 - core],
                dst_ref=core_ref.at[chunk], send_sem=core_send.at[chunk],
                recv_sem=core_recv.at[chunk], device_id=core_id(),
                device_id_type=pl.DeviceIdType.MESH,
            )
        ]
        for copy in copies:
            copy.start()
        core_copies[chunk] = copies

    def send_plane(chunk):
        for copy in core_copies[chunk]:
            copy.wait()
        for k in range(2 * planes):
            core_ref[chunk, k] = (
                source(chunk)[k, core].astype(f32) + core_ref[chunk, k].astype(f32)
            ).astype(bf16)
        copies = [
            remote(
                core_ref.at[chunk, pl.ds(h * planes + mate, 1)],
                slots_ref.at[chunk, number, pl.ds(h, 1)],
                (plane_send, plane_recv), (chunk * len(mates) + number) * 2 + h, {"zlo": mate},
            )
            for number, mate in enumerate(mates)
            for h in range(2)
        ]
        for copy in copies:
            copy.start()
        plane_copies[chunk] = copies

    def send_half(chunk):
        for copy in plane_copies[chunk]:
            copy.wait()
        for h in range(2):
            total = core_ref[chunk, h * planes + zlo].astype(f32)
            for number in range(len(mates)):
                total = total + slots_ref[chunk, number, h].astype(f32)
            plane_ref[chunk, h] = total.astype(bf16)
        copy = remote(
            plane_ref.at[chunk, 1 - half], came_ref.at[chunk], (half_send, half_recv), chunk,
            partner_id(),
        )
        copy.start()
        half_copies[chunk] = copy

    def send_rows(chunk):
        half_copies[chunk].wait()
        total = plane_ref[chunk, half].astype(f32) + came_ref[chunk].astype(f32)
        for block in range(CHUNK // LANES):
            at = (chunk - chunks_one) * CHUNK + block * LANES
            columns = total[:, block * LANES : (block + 1) * LANES]
            if 0 <= at < wide_out:
                put(own_out_ref, columns, wide_out, at)
            elif wide_out <= at < wide_out + wide_down:
                put(own_down_ref, columns, wide_down, at - wide_out)
        if chunk not in shared_chunks:
            return
        spot = shared_chunks.index(chunk)
        columns = slice(spot * CHUNK, (spot + 1) * CHUNK)
        low = total.astype(bf16)
        for place in range(count):
            send_ref[spot, place] = low[place * rows_in : (place + 1) * rows_in]
        copies = [
            remote(
                send_ref.at[spot, other], got_ref.at[me, :, columns], (row_send, row_recv),
                chunk * (count - 1) + number, {"expert": other},
            )
            for number, other in enumerate(others)
        ]
        mine = pltpu.make_async_copy(
            send_ref.at[spot, me], got_ref.at[me, :, columns], local_sems.at[chunk]
        )
        for copy in copies + [mine]:
            copy.start()
        row_copies[chunk] = copies + [mine]

    def put(ref, columns, width, at):
        rows = ref.shape[0]
        for fold in range(D // width):
            ref[:, fold * width + at : fold * width + at + LANES] = columns[
                fold * rows : (fold + 1) * rows
            ]

    alone = [chunk for chunk in range(chunks_one, chunks)
             if (chunk - chunks_one) * CHUNK >= wide_out + wide_down]
    mixed = [chunk for chunk in range(chunks_one, chunks) if chunk not in alone]
    order = alone + list(range(chunks_one)) + mixed
    ready = set()

    @pl.loop(0, length // LANES)
    def _(part):
        rows = pl.ds(pl.multiple_of(part * LANES, LANES), LANES)
        block = x_ref[rows, :].astype(f32)
        scale = lax.rsqrt(jnp.mean(block * block, axis=1, keepdims=True) + norm_eps)
        normed_ref[rows, :] = (block * scale * gain_ref[0:1]).astype(bf16)
        scale_ref[rows, :] = scale

    out_sems = (out_send, out_recv)
    out_over = remote(out_send_ref, out_came_ref, out_sems, 0, partner_id())
    out_copies = reduce_copies(out_ref, out_got_ref, out_sems, 1, tok, 0)
    out_copies.append(pltpu.make_async_copy(
        out_ref.at[pl.ds(pl.multiple_of(me * tok, tok), tok)], out_mine_ref, own_sems.at[2]
    ))

    def produce(chunk):
        if chunk in ready:
            return
        ready.add(chunk)
        if chunk in alone:
            beside.wait()
        elif chunk in mixed:
            if not any(one in ready for one in mixed if one != chunk):
                for copy in fold_copies:
                    copy.wait()
                if not alone:
                    beside.wait()
            for one in mixed:
                ready.add(one)
                send_core(one)
            return
        else:
            at = slice(chunk * CHUNK, (chunk + 1) * CHUNK)
            total = dot_tn(normed_ref[...], proj_ref[:, at])
            if chunk == chunks_one - 1:
                logits = pltpu.roll(logits_ref[...].astype(f32), heads, 1).astype(bf16)
                router = dot_tn(two_ref[:, :D], logits)
                total = total + jnp.concatenate(
                    [jnp.zeros((D, CHUNK - LANES), f32), router], axis=1
                )
            low = total.astype(bf16)
            for k in range(D // own_rows):
                first_ref[chunk, k // 2, k % 2] = low[k * own_rows : (k + 1) * own_rows]
        send_core(chunk)

    begin = conv_ref.shape[1]
    step_ref[0, :, :begin] = conv_ref[...]
    step_ref[0, :, begin : begin + cols_ref.shape[1]] = cols_ref[...]
    begin += cols_ref.shape[1]
    step_ref[0, :, begin : begin + LANES] = head_ref[...]
    begin += LANES
    for k in range(D // CHUNK):
        step_ref[0, k : k + 1, begin:] = gain_two_ref[0:1, k * CHUNK : (k + 1) * CHUNK]

    def input_part(part):
        at = slice(part * CHUNK, (part + 1) * CHUNK)
        one = dot_nt(proj_ref[...], win_ref[at, :])
        gains = jnp.sum(one * (x_ref[:, at].astype(f32) * scale_ref[...]), axis=0, keepdims=True)
        row = D // CHUNK + part
        step_ref[0, row : row + 1, begin:] = gains
        one_ref[:, at] = one.astype(bf16)

    one_copies = reduce_copies(one_ref, one_got_ref, (one_send, one_recv), 0, tok, 0)

    small_sems = (small_send, small_recv)
    rounds = [[core_id()], [{"zlo": mate} for mate in mates], [partner_id()]]
    bases = [sum(len(targets) for targets in rounds[:level]) for level in range(4)]
    small_copies = [
        [
            remote(
                step_ref.at[level], step_came_ref.at[bases[level] + k], small_sems,
                bases[level] + k, target,
            )
            for k, target in enumerate(targets)
        ]
        for level, targets in enumerate(rounds)
    ]
    small_copies.append([
        remote(
            step_ref.at[3], all_small_ref.at[me], small_sems, bases[3] + number, {"expert": other}
        )
        for number, other in enumerate(others)
    ])
    small_copies[3].append(
        pltpu.make_async_copy(step_ref.at[3], all_small_ref.at[me], own_sems.at[1])
    )

    def small_start(level):
        for copy in small_copies[level]:
            copy.start()

    def small_sum(level):
        total = step_ref[level]
        for k, copy in enumerate(small_copies[level]):
            copy.wait()
            total = total + step_came_ref[bases[level] + k]
        step_ref[level + 1] = total

    amount = len(order)
    parts = D // CHUNK
    small_every = max(1, (amount + 4 - parts) // 3)
    produce(order[0])
    for tick in range(amount + 4):
        if tick + 1 < amount:
            produce(order[tick + 1])
        if tick < amount:
            send_plane(order[tick])
        if tick == 2:
            out_over.start()
        if tick == parts:
            for copy in out_copies:
                copy.start()
        if 2 <= tick < amount + 2:
            send_half(order[tick - 2])
        if 4 <= tick:
            send_rows(order[tick - 4])
        if tick < parts:
            input_part(tick)
        if tick == parts - 1:
            for copy in one_copies:
                copy.start()
            small_start(0)
        level = (tick - parts) // small_every
        if tick >= parts and (tick - parts) % small_every == small_every - 1 and level < 3:
            small_sum(level)
            small_start(level + 1)
    for copy in one_copies:
        copy.wait()
    total = reduced(one_ref, one_got_ref, tok, 0, slice(0, D))
    block = tokens_ref[...].astype(f32)
    scale = lax.rsqrt(jnp.mean(block * block, axis=1, keepdims=True) + norm_eps)
    tokens_grad_ref[...] = (
        grad_hidden_ref[...] + norm_back(total, block * scale, scale, gain_ref[0:1])
    ).astype(bf16)
    for copy in out_copies + [out_over]:
        copy.wait()
    total = hidden_ref[...] + out_came_ref[...].astype(f32) + out_mine_ref[...].astype(f32)
    for number in range(count - 1):
        total = total + out_got_ref[number].astype(f32)
    output_ref[...] = total.astype(bf16)
    for copy in small_copies[3]:
        copy.wait()
    for copies in row_copies.values():
        for copy in copies:
            copy.wait()


def kernel_room(shapes):
    total = 0
    for shape, dtype in shapes:
        size = jnp.dtype(dtype).itemsize
        rows = shape[-2] if len(shape) > 1 else 1
        padded = -(-rows // 16) * 16 * -(-shape[-1] // LANES) * LANES
        total += math.prod(shape[:-2]) * padded * size
    rows = max([0] + [shape[0] for shape, _ in shapes if len(shape) == 2 and shape[0] == shape[1]])
    total += 20 * rows * rows + 5 * 1024 * 1024
    return min(max(total, 47 * 1024 * 1024), 62 * 1024 * 1024)


def remote_call(kernel, number, out_shapes, scratch, sems, *operands, outside=(), left=()):
    spec = pl.BlockSpec(memory_space=pltpu.VMEM)
    scalars = pl.BlockSpec(memory_space=pltpu.SMEM)
    anywhere = pl.BlockSpec(memory_space=pl.ANY)
    inside = [one for k, one in enumerate(operands) if k not in outside]
    inside += [one for k, one in enumerate(out_shapes) if k not in left]
    return pl.pallas_call(
        kernel,
        out_shape=out_shapes,
        in_specs=[
            anywhere if k in outside
            else scalars if one.dtype == jnp.int32 and one.size < LANES else spec
            for k, one in enumerate(operands)
        ],
        out_specs=[anywhere if k in left else spec for k in range(len(out_shapes))],
        scratch_shapes=[pltpu.VMEM(shape, dtype) for shape, dtype in scratch] + sems,
        compiler_params=pltpu.CompilerParams(
            collective_id=number, has_side_effects=True,
            vmem_limit_bytes=kernel_room(
                [(one.shape, one.dtype) for one in inside] + scratch
            ),
        ),
    )(*operands)


def vmem_call(kernel, out_shapes, scratch, *operands):
    spec = pl.BlockSpec(memory_space=pltpu.VMEM)
    return pl.pallas_call(
        kernel,
        out_shape=out_shapes,
        in_specs=[spec] * len(operands),
        out_specs=[spec] * len(out_shapes),
        scratch_shapes=[pltpu.VMEM(shape, dtype) for shape, dtype in scratch],
        compiler_params=pltpu.CompilerParams(vmem_limit_bytes=56 * 1024 * 1024),
    )(*operands)


def grid_call(kernel, steps, in_specs, out_specs, out_shapes, scratch, *operands):
    return pl.pallas_call(
        kernel,
        grid=(steps,),
        out_shape=out_shapes,
        in_specs=in_specs,
        out_specs=out_specs,
        scratch_shapes=[pltpu.VMEM(shape, dtype) for shape, dtype in scratch],
        compiler_params=pltpu.CompilerParams(vmem_limit_bytes=56 * 1024 * 1024),
    )(*operands)


def update_kernel(got_ref, sum_out_ref, sum_down_ref, *refs, inner, own_ff, heads):
    groups, _, _ = got_ref.shape
    names = 4
    given = [refs[3 * k : 3 * k + 3] for k in range(names)]
    made = [refs[3 * names + 4 * k : 3 * names + 4 * k + 4] for k in range(names)]
    router_ref = refs[7 * names]

    def step(which, at, gradient):
        weight, first, second = (ref[:, at] for ref in given[which])
        parts = adam_step(weight, first, second, gradient)[:4]
        for ref, part in zip(made[which], parts):
            ref[:, at] = part

    def piece(place, start, size):
        return got_ref[place, :, start : start + size].astype(f32)

    body = 2 * inner + 2 * STATE
    for place in range(groups):
        for k in range(2):
            start = k * INNER + place * inner
            step(0, slice(start, start + inner), piece(place, k * inner, inner))
    step(0, slice(2 * INNER, 2 * INNER + 2 * STATE),
         sum(piece(place, 2 * inner, 2 * STATE) for place in range(groups)))
    blocks = [piece(place, body, LANES) for place in range(groups)]
    lanes = lax.broadcasted_iota(jnp.int32, blocks[0].shape, 1)
    steps = sum(
        pltpu.roll(jnp.where(lanes < heads, block, 0.0), place * heads, 1)
        if place else jnp.where(lanes < heads, block, 0.0)
        for place, block in enumerate(blocks)
    )
    step(0, slice(2 * INNER + 2 * STATE, 2 * INNER + 2 * STATE + groups * heads),
         steps[:, : groups * heads])
    router_ref[...] = pltpu.roll(sum(blocks), LANES - heads, 1)
    step(1, slice(0, D), sum_out_ref[: given[1][0].shape[0], :])
    step(3, slice(0, D), sum_down_ref[: given[3][0].shape[0], :])
    start = got_ref.shape[2] - 2 * own_ff
    for place in range(groups):
        for k in range(2):
            at = k * SHARED_FF + place * own_ff
            step(2, slice(at, at + own_ff), piece(place, start + k * own_ff, own_ff))


def on_device(
    tokens, cotangent, lengths, routes,
    w_in, w_in_first, w_in_second,
    w_out, w_out_first, w_out_second,
    w_router, w_router_first, w_router_second,
    w_shared_gu, w_shared_gu_first, w_shared_gu_second,
    w_shared_down, w_shared_down_first, w_shared_down_second,
    w_expert_gu, w_expert_gu_first, w_expert_gu_second,
    w_expert_down, w_expert_down_first, w_expert_down_second,
    norm_gains, norm_gains_first, norm_gains_second,
    conv_params, conv_params_first, conv_params_second,
    head_params, head_params_first, head_params_second,
    mixer_gain, mixer_gain_first, mixer_gain_second,
):
    groups = lax.axis_size("expert")
    copies = (lax.axis_size("zhi") * lax.axis_size("zlo") * lax.axis_size("core"))
    place = lax.axis_index("expert")
    tok = tokens.shape[0]
    length = tok * groups
    top = routes.shape[1]
    experts = w_router.shape[1]
    own_experts = w_expert_gu.shape[0]
    capacity = (4 * tok * top + 3 * experts - 1) // (3 * experts)
    inner = INNER // groups
    heads = HEADS // groups
    rows_in = w_in.shape[0]
    rows_out = w_out.shape[0]
    rows_sd = w_shared_down.shape[0]
    own_ff = SHARED_FF // groups
    per_pair = copies // groups
    conv_cols = inner + 2 * STATE
    body = 2 * inner + 2 * STATE

    pairs = pltpu.SemaphoreType.DMA
    route_pad = jnp.pad(routes, ((0, 0), (0, LANES - top)))
    row_shape = jax.ShapeDtypeStruct((groups, tok, D), bf16)
    route_shape = jax.ShapeDtypeStruct((groups, tok, LANES), jnp.int32)
    half = lax.axis_index("zhi")
    held = own_experts // 2
    rows_egu, rows_ed = w_expert_gu.shape[1], w_expert_down.shape[1]
    gu_held = jax.ShapeDtypeStruct((held, rows_egu, 2 * EXPERT_FF), bf16)
    ed_held = jax.ShapeDtypeStruct((held, rows_ed, D), bf16)
    (
        x_all, cot_all, cot_came, routes_two, win, sgu, wout, sd, masks, doc_col, doc_row,
        egu_kept, egu_sent, ed_kept, ed_sent, conv_pad, head_rows, col_rows,
    ) = remote_call(
        start_kernel, 7,
        [
            jax.ShapeDtypeStruct((groups, tok, D), bf16),
            jax.ShapeDtypeStruct((groups, tok, D), bf16),
            jax.ShapeDtypeStruct((tok, D), bf16),
            jax.ShapeDtypeStruct((2, groups, tok, LANES), jnp.int32),
            jax.ShapeDtypeStruct((copies, groups, rows_in, body + LANES), bf16),
            jax.ShapeDtypeStruct((copies, groups, rows_in, 2 * own_ff), bf16),
            jax.ShapeDtypeStruct((per_pair, groups, rows_out, D), bf16),
            jax.ShapeDtypeStruct((per_pair, groups, rows_sd, D), bf16),
            jax.ShapeDtypeStruct((length, LANES), f32),
            jax.ShapeDtypeStruct((length, 1), jnp.int32),
            jax.ShapeDtypeStruct((1, length), jnp.int32),
            gu_held, gu_held, ed_held, ed_held,
            jax.ShapeDtypeStruct((8, conv_cols), f32),
            jax.ShapeDtypeStruct((8, LANES), f32),
            jax.ShapeDtypeStruct((8, inner), f32),
        ],
        [
            ((copies, rows_out, D), bf16), ((copies, rows_sd, D), bf16), ((tok, LANES), jnp.int32),
            ((groups, rows_in, body + LANES), bf16), ((groups, rows_in, 2 * own_ff), bf16),
            ((rows_out, D), bf16), ((rows_sd, D), bf16), ((2, max(8, rows_in), LANES), f32),
        ],
        [pairs((7 * (groups - 1),))] * 2
        + [pairs((2 * per_pair * (groups - 1),))] * 2
        + [pairs((2,))] * 2
        + [pairs((9 + 2 * per_pair,))]
        + line_sems(copies // 2) * 4,
        lengths, tokens, cotangent, route_pad, w_in, w_router, w_shared_gu, w_out,
        w_shared_down, w_expert_gu, w_expert_down, conv_params, head_params,
        mixer_gain.reshape(1, INNER),
    )
    x_all = x_all.reshape(length, D)
    routes_two = routes_two.reshape(2 * length, LANES)
    win = win.reshape(D, -1)
    sgu = sgu.reshape(D, -1)
    wout = wout.reshape(inner, D)
    sd = sd.reshape(own_ff, D)
    router = win[:, body:]


    square = ((length, length), f32)
    lane_rows = ((length, LANES), f32)
    lane_cols = ((LANES, length), f32)
    planes_half = copies // 4
    mates = copies // 2
    spread_sems = [pairs((mate_sems(planes_half),))] * 2
    gu_all = jax.ShapeDtypeStruct((mates,) + egu_kept.shape, bf16)
    ed_all = jax.ShapeDtypeStruct((mates,) + ed_kept.shape, bf16)
    packed, dt_raw, full_y, res_part, gu_near, gu_came, cot_two = remote_call(
        forward_kernel, 3,
        [
            jax.ShapeDtypeStruct((length, body), bf16),
            jax.ShapeDtypeStruct((length, LANES), f32),
            jax.ShapeDtypeStruct((length, inner), bf16),
            jax.ShapeDtypeStruct((length, D + LANES), bf16),
            gu_all,
            gu_held,
            jax.ShapeDtypeStruct((2, groups, tok, D), bf16),
        ],
        [((length, D), bf16), square, square, lane_rows, lane_cols, ((length, inner), bf16),
         lane_rows],
        [pairs((groups,))] * 2 + spread_sems + [pairs(()), pairs((2,))],
        x_all, win, norm_gains, conv_pad, masks, head_rows, col_rows, doc_col, doc_row, wout,
        egu_kept, egu_sent, cot_all, cot_came,
    )
    cot_two = cot_two.reshape(2 * length, D)
    hidden, mixer_res, two_own, ed_near, ed_came = remote_call(
        hidden_kernel, 0,
        [
            jax.ShapeDtypeStruct((tok, D), f32),
            jax.ShapeDtypeStruct((tok, D), f32),
            jax.ShapeDtypeStruct((tok, D + LANES), bf16),
            ed_all,
            ed_held,
        ],
        [((groups - 1, tok, D + LANES), bf16)],
        [pairs((groups,))] * 2 + spread_sems + [pairs(())],
        res_part, tokens, norm_gains, ed_kept, ed_sent,
    )
    gathered_shape = jax.ShapeDtypeStruct((groups, tok, D + LANES), bf16)
    own_rows = groups * rows_in
    payload = ((tok, D + LANES), bf16)
    tile = 16
    down_rows = -(-rows_sd // tile) * tile
    two_rows, gu_far, ed_far, shared_out, shared_back, grad_sgu, grad_sd = remote_call(
        share_kernel, 1,
        [
            jax.ShapeDtypeStruct((2, groups, tok, D + LANES), bf16), gu_all, ed_all,
            jax.ShapeDtypeStruct((length, D), bf16),
            jax.ShapeDtypeStruct((length, D), bf16),
            jax.ShapeDtypeStruct((copies // 2, 2, own_rows, 2 * own_ff), bf16),
            jax.ShapeDtypeStruct((copies, down_rows, D), bf16),
        ],
        [
            payload, ((length, D), bf16),
            ((length, own_ff), bf16), ((length, 2 * own_ff), bf16),
        ],
        [pairs((2 * groups - 1,))] * 2 + [pairs((2 * mate_sems(planes_half),))] * 2 + [pairs((4,))],
        two_own, gu_came, ed_came, cot_two, sgu, sd,
    )
    scale_words = two_rows[0, :, :, D:].reshape(length, LANES)
    two_rows = two_rows.reshape(2 * length, D + LANES)

    blocks = 2 * groups
    expert_at = (place * own_experts + half * held).reshape(1)
    slot_rows = blocks * capacity

    def by_block(*shape):
        return pl.BlockSpec(shape, lambda b: (b,) + (0,) * (len(shape) - 1))

    def fixed(*shape):
        return pl.BlockSpec(shape, lambda b: (0,) * len(shape))

    slot_spec = pl.BlockSpec((held, capacity, D), lambda b: (0, b, 0))
    in_smem = pl.BlockSpec(memory_space=pltpu.SMEM)
    slot_shape = jax.ShapeDtypeStruct((held, slot_rows, D), bf16)
    slot_in, slot_top, slot_grad, weights, pick = grid_call(
        functools.partial(route_kernel, top_count=top, heads=heads), blocks,
        [by_block(tok, D + LANES), by_block(tok, D), by_block(tok, LANES), fixed(D, LANES), in_smem],
        [slot_spec] * 3 + [by_block(tok, LANES), by_block(1, tok, held * capacity)],
        [slot_shape] * 3
        + [
            jax.ShapeDtypeStruct((2 * length, LANES), f32),
            jax.ShapeDtypeStruct((blocks, tok, held * capacity), bf16),
        ],
        [],
        two_rows, cot_two, routes_two, router, expert_at,
    )
    packed_rows = 2 * rows_egu + rows_ed * D // EXPERT_FF

    def by_expert(*shape):
        return pl.BlockSpec((1,) + shape, lambda e: (e,) + (0,) * len(shape))

    def weight_spec(rows, columns):
        return pl.BlockSpec((mates, 1, rows, columns), lambda e: (0, e, 0, 0))

    slot_out, slot_back, slot_q, expert_grads = grid_call(
        expert_kernel, held,
        [by_expert(slot_rows, D)] * 3
        + [in_smem]
        + [weight_spec(rows_egu, 2 * EXPERT_FF)] * 2
        + [weight_spec(rows_ed, D)] * 2,
        [by_expert(slot_rows, D)] * 2
        + [
            by_expert(slot_rows, LANES),
            pl.BlockSpec((mates, 1, 2, packed_rows, EXPERT_FF), lambda e: (0, e, 0, 0, 0)),
        ],
        [slot_shape] * 2
        + [
            jax.ShapeDtypeStruct((held, slot_rows, LANES), f32),
            jax.ShapeDtypeStruct((mates, held, 2, packed_rows, EXPERT_FF), bf16),
        ],
        [((slot_rows, EXPERT_FF), bf16), ((slot_rows, 2 * EXPERT_FF), bf16)],
        slot_in, slot_top, slot_grad, half.reshape(1), gu_near, gu_far, ed_near, ed_far,
    )
    own_spec = pl.BlockSpec((tok, D), lambda b: (jnp.minimum(b, groups - 1), 0))
    out_parts, back_parts = grid_call(
        combine_kernel, blocks,
        [
            by_block(1, tok, held * capacity), by_block(tok, LANES), in_smem, slot_spec, slot_spec,
            pl.BlockSpec((held, capacity, LANES), lambda b: (0, b, 0)), own_spec, own_spec,
        ],
        [by_block(tok, D), by_block(tok, D + LANES)],
        [
            jax.ShapeDtypeStruct((2 * length, D), bf16),
            jax.ShapeDtypeStruct((2 * length, D + LANES), bf16),
        ],
        [],
        pick, weights, expert_at, slot_out, slot_back, slot_q, shared_out, shared_back,
    )

    weights_tok = lax.dynamic_slice_in_dim(weights, place * tok, tok, axis=0)
    gathered_shape = jax.ShapeDtypeStruct((groups, tok, D + LANES), bf16)
    hidden_all, grad_hidden, grad_logits, gain_two, expert_sums, came_one = remote_call(
        functools.partial(back_kernel, own_experts=own_experts, heads=heads), 2,
        [
            gathered_shape,
            jax.ShapeDtypeStruct((tok, D), f32),
            jax.ShapeDtypeStruct((tok, LANES), bf16),
            jax.ShapeDtypeStruct((8, D), f32),
            jax.ShapeDtypeStruct((held, 2, packed_rows, EXPERT_FF), bf16),
            jax.ShapeDtypeStruct((packed_rows, EXPERT_FF), bf16),
        ],
        [((groups - 1, tok, D + LANES), bf16)] * 2
        + [payload] * 3
        + [
            ((planes_half - 1, held, 2, packed_rows, EXPERT_FF), bf16),
            ((planes_half, held, 2, packed_rows, EXPERT_FF), bf16),
            ((planes_half, held, 2, packed_rows, EXPERT_FF), bf16),
        ],
        [
            pairs((3 * groups - 2,)), pairs((3 * groups - 2,)),
            pairs((held * (planes_half - 1) + 1,)), pairs((held * (planes_half - 1) + 1,)),
            pairs((held * planes_half,)), pairs((held * planes_half,)),
            pairs((planes_half,)), pairs(()),
        ],
        back_parts, hidden, mixer_res, cotangent, weights_tok, router, norm_gains,
        expert_grads.reshape((planes_half, 2) + expert_grads.shape[1:]), outside=(7,),
    )
    hidden_all = hidden_all.reshape(length, -1)
    grad_gain_two = gain_two[0]

    out_rows = -(-rows_out // tile) * tile
    (
        grad_proj, conv_grads, col_grads, head_grads, expert_sum, grad_wout, out_other,
    ) = remote_call(
        backward_kernel, 5,
        [
            jax.ShapeDtypeStruct((length, body + LANES), bf16),
            jax.ShapeDtypeStruct((8, conv_cols), f32),
            jax.ShapeDtypeStruct((8, inner), f32),
            jax.ShapeDtypeStruct((8, LANES), f32),
            jax.ShapeDtypeStruct((own_experts, packed_rows, EXPERT_FF), bf16),
            jax.ShapeDtypeStruct((copies, out_rows, D), bf16),
            jax.ShapeDtypeStruct((tok, D), bf16),
        ],
        [square, square, lane_rows, lane_cols, square, lane_rows, lane_cols, lane_rows, lane_rows,
         ((length, LANES), bf16), ((inner, D), bf16), ((packed_rows, EXPERT_FF), bf16),
         ((groups - 1, tok, D), bf16), ((tok, D), bf16)],
        [pairs(()), pairs(()), pairs((groups - 1,)), pairs((groups - 1,)), pairs(())],
        hidden_all, scale_words, wout, conv_pad, masks, head_rows, col_rows, doc_col, doc_row,
        packed, dt_raw, full_y, expert_sums, came_one, out_parts, outside=(14,),
    )
    wide_out = D * out_rows // own_rows
    wide_down = D * down_rows // own_rows
    chunks_one = (body + LANES) // CHUNK
    chunks_two = -(-(wide_out + wide_down + 2 * own_ff) // CHUNK)
    chunks = chunks_one + chunks_two
    first_shared = chunks_one + (wide_out + wide_down) // CHUNK
    shared_chunks = list(range(chunks_one)) + list(range(first_shared, chunks))
    shared_wide = len(shared_chunks) * CHUNK
    small_wide = conv_cols + inner + LANES + CHUNK
    folds = own_rows // out_rows + own_rows // down_rows
    dense_sems = [pairs((chunks,))] * 2 + [pairs((2 * chunks * (planes_half - 1),))] * 2
    dense_sems += [pairs((chunks,))] * 2 + [pairs((chunks * (groups - 1),))] * 2
    dense_sems += [pairs((groups - 1,))] * 2 + [pairs((groups,))] * 2
    dense_sems += [pairs((planes_half + groups,))] * 2
    dense_sems += [pairs((per_pair * folds * (groups - 1),))] * 2
    dense_sems += [pairs((chunks,)), pairs((per_pair * folds,)), pairs((3,))]
    got_rows, sum_out, sum_sd, grad_tokens, output, small = remote_call(
        functools.partial(dense_kernel, shared_chunks=shared_chunks, heads=heads), 6,
        [
            jax.ShapeDtypeStruct((groups, rows_in, shared_wide), bf16),
            jax.ShapeDtypeStruct((out_rows, D), f32),
            jax.ShapeDtypeStruct((down_rows, D), f32),
            jax.ShapeDtypeStruct((tok, D), bf16),
            jax.ShapeDtypeStruct((tok, D), bf16),
            jax.ShapeDtypeStruct((groups, 8, small_wide), f32),
        ],
        [
            ((length, D), bf16),
            ((chunks_one, copies // 2, 2, own_rows, CHUNK), bf16),
            ((copies // 2, 2, own_rows, chunks_two * CHUNK), bf16),
            ((chunks, copies // 2, own_rows, CHUNK), bf16),
            ((chunks, planes_half - 1, 2, own_rows, CHUNK), bf16),
            ((chunks, 2, own_rows, CHUNK), bf16),
            ((chunks, own_rows, CHUNK), bf16),
            ((len(shared_chunks), groups, rows_in, CHUNK), bf16),
            ((length, D), bf16),
            ((groups - 1, tok, D), bf16),
            ((tok, D), bf16),
            ((groups - 1, tok, D), bf16),
            ((tok, D), bf16),
            ((length, 1), f32),
            ((4, 8, small_wide), f32),
            ((planes_half + 1, 8, small_wide), f32),
        ],
        dense_sems,
        x_all, tokens, win, norm_gains, grad_proj, two_own, grad_logits, grad_sgu, grad_wout,
        grad_sd, grad_hidden, out_parts, out_other, hidden, conv_grads, col_grads, head_grads, gain_two,
        outside=(7, 8, 9, 11),
    )
    sum_egu = jnp.concatenate(
        [expert_sum[:, :rows_egu], expert_sum[:, rows_egu : 2 * rows_egu]], axis=2
    ).astype(f32)
    sum_ed = jnp.concatenate(
        [
            expert_sum[:, 2 * rows_egu + k * rows_ed : 2 * rows_egu + (k + 1) * rows_ed]
            for k in range(D // EXPERT_FF)
        ],
        axis=2,
    ).astype(f32)

    sum_conv = jnp.concatenate(
        [
            small[:, : CONV + 1, :inner].transpose(1, 0, 2).reshape(CONV + 1, INNER),
            jnp.sum(small[:, : CONV + 1, inner:conv_cols], axis=0),
        ],
        axis=1,
    )
    start = conv_cols
    sum_mixer = small[:, 0, start : start + inner].reshape(INNER)
    sum_skip = jnp.sum(
        small[:, 1, start : start + inner].reshape(groups, heads, HEAD_DIM), axis=2
    ).reshape(HEADS)
    start = start + inner
    sum_head = jnp.stack(
        [small[:, k, start : start + heads].reshape(HEADS) for k in range(2)] + [sum_skip]
    )
    start = start + LANES
    gain_sums = jnp.sum(small[:, :, start:], axis=0)
    sum_gains = jnp.stack(
        [gain_sums[D // CHUNK :].reshape(D), gain_sums[: D // CHUNK].reshape(D)]
    )

    given = (
        (w_in, w_in_first, w_in_second),
        (w_out, w_out_first, w_out_second),
        (w_shared_gu, w_shared_gu_first, w_shared_gu_second),
        (w_shared_down, w_shared_down_first, w_shared_down_second),
    )
    updated = vmem_call(
        functools.partial(
            update_kernel, inner=inner, own_ff=own_ff, heads=heads
        ),
        [jax.ShapeDtypeStruct(one[0].shape, f32) for one in given for _ in range(4)]
        + [jax.ShapeDtypeStruct((rows_in, LANES), f32)],
        [],
        got_rows, sum_out, sum_sd, *[part for one in given for part in one],
    )
    up_in, up_out, up_sgu, up_sd = (updated[4 * k : 4 * k + 4] for k in range(4))
    up_router = tuple(
        part.T
        for part in adam_step(
            w_router.T, w_router_first.T, w_router_second.T, updated[16].T[:experts]
        )
    )
    up_egu = adam_step(w_expert_gu, w_expert_gu_first, w_expert_gu_second, sum_egu)
    up_ed = adam_step(w_expert_down, w_expert_down_first, w_expert_down_second, sum_ed)
    up_gains = adam_step(norm_gains, norm_gains_first, norm_gains_second, sum_gains)
    up_conv = adam_step(conv_params, conv_params_first, conv_params_second, sum_conv)
    up_head = adam_step(head_params, head_params_first, head_params_second, sum_head)
    up_mixer = adam_step(mixer_gain, mixer_gain_first, mixer_gain_second, sum_mixer)

    large = (up_in, up_out, up_router, up_sgu, up_sd, up_egu, up_ed)
    little = (up_gains, up_conv, up_head, up_mixer)
    return (
        (output, grad_tokens)
        + tuple(part for one in large for part in tuple(one)[:4])
        + tuple(part for one in little for part in (one[0], one[4], one[2], one[3]))
    )


def solution(mesh):
    copies, groups = mesh.devices.shape
    split = Mesh(mesh.devices.reshape(2, copies // 4, 2, groups), ALL)
    rows = P(ALL, None)
    expert_rows = P("expert", DP, None)
    whole = P()
    return jax.shard_map(
        on_device,
        mesh=split,
        in_specs=(rows, rows, P(DP, None), rows)
        + (rows,) * 15
        + (expert_rows,) * 6
        + (whole,) * 12,
        out_specs=(rows, rows) + (rows,) * 20 + (expert_rows,) * 8 + (whole,) * 16,
        check_vma=False,
    )
```

```python
import functools
import math

import jax
import jax.numpy as jnp
from jax import lax
from jax.experimental import pallas as pl
from jax.experimental.pallas import tpu as pltpu
from jax.sharding import Mesh
from jax.sharding import PartitionSpec as P

D = 1536
HEADS = 48
HEAD_DIM = 64
STATE = 128
CONV = 4
EXPERT_FF = 512
SHARED_FF = 1024
STEP = 3
INNER = 3072
CONV_DIM = 3328
LANES = 128
CHUNK = 384

DP = ("zhi", "zlo", "core")
MATES = ("zlo", "core")
ALL = DP + ("expert",)

norm_eps = 1e-05
beta_one = 0.9
beta_two = 0.95
adam_eps = 1e-08
learn_rate = 0.02
decay_rate = 0.1
highest = lax.Precision.HIGHEST
bf16 = jnp.bfloat16
f32 = jnp.float32


def dot(left, right):
    return jnp.dot(left, right, preferred_element_type=f32)


def dot_nt(left, right):
    return lax.dot_general(left, right, (((1,), (1,)), ((), ())), preferred_element_type=f32)


def dot_tn(left, right):
    return lax.dot_general(left, right, (((0,), (0,)), ((), ())), preferred_element_type=f32)


def swap(pieces, axis):
    return lax.all_to_all(pieces, axis, split_axis=0, concat_axis=0, tiled=True)


def spread(block, axis):
    axes = (axis,) if isinstance(axis, str) else axis
    count = math.prod(lax.axis_size(one) for one in axes)
    return swap(jnp.broadcast_to(block[None], (count,) + block.shape), axis)


def to_partner(value):
    return lax.ppermute(value, "zhi", [(0, 1), (1, 0)])


def rms_scale(values):
    return lax.rsqrt(jnp.mean(values * values, axis=-1, keepdims=True) + norm_eps)


def silu_slope(values):
    sigmoid_value = jax.nn.sigmoid(values)
    return sigmoid_value * (1.0 + values * (1.0 - sigmoid_value))


def norm_back(grad_norm, unit_rows, scale_rows, gain):
    scaled = grad_norm * gain
    return scale_rows * (scaled - unit_rows * jnp.mean(scaled * unit_rows, axis=-1, keepdims=True))


def adam_step(weight, moment_one, moment_two, gradient):
    moment_one = beta_one * moment_one + (1.0 - beta_one) * gradient
    moment_two = beta_two * moment_two + (1.0 - beta_two) * gradient * gradient
    fixed_one = 1.0 - beta_one**STEP
    fixed_two = 1.0 - beta_two**STEP
    change = (
        moment_one / fixed_one / (jnp.sqrt(moment_two / fixed_two) + adam_eps) + decay_rate * weight
    )
    moved = -learn_rate * change
    return (gradient, weight + moved, moment_one, moment_two, moved)


def split_words(value):
    high = value.astype(bf16)
    rest = value - high.astype(f32)
    mid = rest.astype(bf16)
    low = (rest - mid.astype(f32)).astype(bf16)
    return high, mid, low


def join_words(words):
    return words[0].astype(f32) + words[1].astype(f32) + words[2].astype(f32)


def conv_rows(block, masks, params):
    total = params[CONV : CONV + 1] + params[0:1] * block
    for offset in range(1, CONV):
        total = total + params[offset : offset + 1] * (
            pltpu.roll(block, offset, 0) * masks[:, offset : offset + 1]
        )
    return total


def conv_rows_back(grad, block, masks, params):
    length = block.shape[0]
    taps = [jnp.sum(grad * block, axis=0, keepdims=True)]
    rows = params[0:1] * grad
    for offset in range(1, CONV):
        masked = grad * masks[:, offset : offset + 1]
        taps.append(jnp.sum(masked * pltpu.roll(block, offset, 0), axis=0, keepdims=True))
        rows = rows + pltpu.roll(params[offset : offset + 1] * masked, length - offset, 0)
    taps.append(jnp.sum(grad, axis=0, keepdims=True))
    return rows, taps


def dot_words(exact, value, contract):
    total = None
    for word in split_words(value):
        part = lax.dot_general(exact, word, (contract, ((), ())), preferred_element_type=f32)
        total = part if total is None else total + part
    return total


def dot_words_left(value, exact):
    total = None
    for word in split_words(value):
        part = jnp.dot(word, exact, preferred_element_type=f32)
        total = part if total is None else total + part
    return total


def softplus(value):
    return jnp.maximum(value, 0.0) + jnp.log1p(jnp.exp(-jnp.abs(value)))


def head_lanes(pair, transposed=False):
    rows = lax.broadcasted_iota(jnp.int32, (LANES, LANES), 0)
    lanes = lax.broadcasted_iota(jnp.int32, (LANES, LANES), 1)
    if transposed:
        rows, lanes = lanes, rows
    return (rows == 2 * pair + lanes // HEAD_DIM).astype(f32).astype(bf16)


def lane_of(matrix, lane):
    lanes = lax.broadcasted_iota(jnp.int32, matrix.shape, 1)
    return jnp.sum(jnp.where(lanes == lane, matrix, 0.0), axis=1, keepdims=True)


def scan_setup(dt_ref, packed_ref, conv_ref, masks, head_ref, doc_col, doc_row, inner,
               neg_ref, scores_ref, cum_ref, cum_t_ref):
    length = dt_ref.shape[0]
    pre_step = dt_ref[...] + head_ref[1:2]
    dt_step = softplus(pre_step)
    log_decay = -head_ref[0:1] * dt_step
    at = lax.broadcasted_iota(jnp.int32, (length, length), 0)
    to = lax.broadcasted_iota(jnp.int32, (length, length), 1)
    usable = (doc_col == doc_row) & (at >= to)
    neg_ref[...] = jnp.where(usable, 0.0, -1e30)
    exact = usable.astype(f32).astype(bf16)
    cum_ref[...] = dot_words(exact, log_decay, ((1,), (0,)))
    cum_t_ref[...] = cum_ref[...].T
    start = 2 * inner
    b_in = packed_ref[:, start : start + STATE].astype(f32)
    c_in = packed_ref[:, start + STATE : start + 2 * STATE].astype(f32)
    b_out = conv_rows(b_in, masks, conv_ref[:, inner : inner + STATE])
    c_out = conv_rows(c_in, masks, conv_ref[:, inner + STATE : inner + 2 * STATE])
    b_low = jax.nn.silu(b_out).astype(bf16)
    c_low = jax.nn.silu(c_out).astype(bf16)
    scores_ref[...] = dot_nt(c_low, b_low)
    return pre_step, dt_step, log_decay, exact, b_out, c_out, b_low, c_low


def pair_slices(pair, inner):
    at = pl.ds(pl.multiple_of(pair * LANES, LANES), LANES)
    x_at = pl.ds(pl.multiple_of(inner + pair * LANES, LANES), LANES)
    return at, x_at


def forward_kernel(x_ref, win_ref, gain_ref, conv_ref, masks_ref, head_ref, cols_ref, doc_col_ref,
                   doc_row_ref, wout_ref, gu_ref, gu_sent_ref, cot_ref, cot_came_ref,
                   packed_ref, dt_ref, y_ref, out_ref, gu_all_ref, gu_came_ref, cot_two_ref,
                   normed_ref, neg_ref, scores_ref, cum_ref, cum_t_ref, act_ref, square_ref,
                   send_sems, recv_sems, mate_send, mate_recv, mate_local, local_sems):
    greet(group_ids() + near_ids())
    count, me, _ = peers()
    sems = (send_sems, recv_sems)
    over = remote(gu_sent_ref, gu_came_ref, sems, 0, partner_id())
    weights = MateSpread(gu_ref, gu_all_ref, (mate_send, mate_recv), 0, mate_local)
    cots = [
        pltpu.make_async_copy(cot_ref, cot_two_ref.at[0], local_sems.at[0]),
        pltpu.make_async_copy(cot_came_ref, cot_two_ref.at[1, me], local_sems.at[1]),
    ]
    cots += spread_copies(cot_came_ref, cot_two_ref.at[1], sems, 1)
    over.start()
    weights.start()
    for copy in cots:
        copy.start()
    length = x_ref.shape[0]
    inner = wout_ref.shape[0]
    body = packed_ref.shape[1]
    step = 2 * LANES

    @pl.loop(0, length // LANES)
    def _(part):
        rows = pl.ds(pl.multiple_of(part * LANES, LANES), LANES)
        block = x_ref[rows, :].astype(f32)
        scale = lax.rsqrt(jnp.mean(block * block, axis=1, keepdims=True) + norm_eps)
        normed_ref[rows, :] = (block * scale * gain_ref[0:1]).astype(bf16)

    @pl.loop(0, body // step)
    def _(part):
        at = pl.ds(pl.multiple_of(part * step, step), step)
        packed_ref[:, at] = dot(normed_ref[...], win_ref[:, at]).astype(bf16)

    dt_ref[...] = dot(normed_ref[...], win_ref[:, body:])
    masks = masks_ref[...]
    _, dt_step, *_ = scan_setup(
        dt_ref, packed_ref, conv_ref, masks, head_ref, doc_col_ref[...], doc_row_ref[...], inner,
        neg_ref, scores_ref, cum_ref, cum_t_ref,
    )
    square_ref[...] = jnp.zeros_like(square_ref)
    lanes = lax.broadcasted_iota(jnp.int32, (LANES, LANES), 1)

    @pl.loop(0, inner // LANES)
    def _(pair):
        at, x_at = pair_slices(pair, inner)
        values = jax.nn.silu(conv_rows(packed_ref[:, x_at].astype(f32), masks, conv_ref[:, at]))
        dt_wide = dot_words_left(dt_step, head_lanes(pair))
        scaled = (values * dt_wide).astype(bf16)
        cum_cols = [lane_of(cum_ref[...], 2 * pair + k) for k in range(2)]
        cum_rows = [cum_t_ref[pl.ds(2 * pair + k, 1), :] for k in range(2)]
        outs = []
        for part in range(length // LANES):
            rows = slice(part * LANES, (part + 1) * LANES)
            wide = (part + 1) * LANES
            pieces = []
            for k in range(2):
                decay = jnp.exp(cum_cols[k][rows] - cum_rows[k][:, :wide] + neg_ref[rows, :wide])
                mixed = (decay * scores_ref[rows, :wide]).astype(bf16)
                pieces.append(dot(mixed, scaled[:wide]))
            outs.append(jnp.where(lanes < HEAD_DIM, pieces[0], pieces[1]))
        full_y = jnp.concatenate(outs, axis=0) + cols_ref[1:2, at] * values
        y_ref[:, at] = full_y.astype(bf16)
        gated = full_y * jax.nn.silu(packed_ref[:, at].astype(f32))
        square_ref[...] += gated * gated
        act_ref[:, at] = (gated * cols_ref[0:1, at]).astype(bf16)

    @pl.loop(0, D // step)
    def _(part):
        at = pl.ds(pl.multiple_of(part * step, step), step)
        out_ref[:, at] = dot(act_ref[...], wout_ref[:, at]).astype(bf16)

    squares = jnp.sum(square_ref[...], axis=1, keepdims=True)
    out_ref[:, D:] = word_lanes(squares)
    weights.forward()
    for copy in cots:
        copy.wait()
    over.wait()
    weights.finish()


def word_lanes(column):
    lanes = lax.broadcasted_iota(jnp.int32, (column.shape[0], LANES), 1)
    words = [word.astype(f32) for word in split_words(column)]
    row = jnp.where(lanes == 0, words[0], jnp.where(lanes == 1, words[1], words[2]))
    return jnp.where(lanes < 3, row, 0.0).astype(bf16)


def word_sum(words):
    return words[:, 0:1].astype(f32) + words[:, 1:2].astype(f32) + words[:, 2:3].astype(f32)


def backward_kernel(hid_ref, scale_ref, wout_ref, conv_ref, masks_ref, head_ref, cols_ref,
                    doc_col_ref, doc_row_ref, packed_ref, dt_ref, y_ref, sums_ref, came_one_ref, out_ref,
                    sgu_ref,
                    proj_ref, conv_grad_ref, cols_grad_ref, head_grad_ref, total_ref, wout_send_ref,
                    out_send_ref, sgu_got_ref,
                    neg_ref, scores_ref, cum_ref, cum_t_ref, grad_scores_ref, row_ref, col_ref,
                    step_ref, scaled_ref, low_ref, wout_grad_ref, theirs_ref, out_got_ref, out_mine_ref, sgu_core_ref, sgu_mine_ref,
                    sgu_slots_ref, sgu_plane_ref, sgu_came_ref, sgu_send_ref, send_sem, recv_sem,
                    out_send, out_recv, out_local, sgu_send_sems, sgu_recv_sems, sgu_local_sems):
    greet(group_ids() + near_ids())
    core, zlo = lax.axis_index("core"), lax.axis_index("zlo")
    sgu_sems = (sgu_send_sems, sgu_recv_sems)
    sgu_core = remote(sgu_ref.at[:, 1 - core], sgu_core_ref, sgu_sems, 0, core_id())
    sgu_mine = pltpu.make_async_copy(sgu_ref.at[:, core], sgu_mine_ref, sgu_local_sems.at[0])
    sgu_core.start()
    sgu_mine.start()
    tok = out_send_ref.shape[0]
    count = lax.axis_size("expert")
    out_sems = (out_send, out_recv)
    rows_all = out_ref.shape[0] // 2
    out_copies = reduce_copies(out_ref, out_got_ref, out_sems, 0, tok, rows_all)
    yours = pl.ds(pl.multiple_of(rows_all + lax.axis_index("expert") * tok, tok), tok)
    out_copies.append(pltpu.make_async_copy(out_ref.at[yours], out_mine_ref, out_local))
    for copy in out_copies:
        copy.start()
    half = lax.axis_index("zhi")
    held = sums_ref.shape[0]
    across = pltpu.make_async_remote_copy(
        src_ref=sums_ref.at[1, 1 - half], dst_ref=theirs_ref, send_sem=send_sem,
        recv_sem=recv_sem, device_id=partner_id(), device_id_type=pl.DeviceIdType.MESH,
    )
    across.start()
    length = dt_ref.shape[0]
    inner = wout_ref.shape[0]
    body = packed_ref.shape[1]
    scale_mix = word_sum(scale_ref[...])

    @pl.loop(0, inner // LANES)
    def _(pair):
        at, _ = pair_slices(pair, inner)
        gated = y_ref[:, at].astype(f32) * jax.nn.silu(packed_ref[:, at].astype(f32))
        act = (gated * scale_mix * cols_ref[0:1, at]).astype(bf16)
        wout_grad_ref[at, :] = dot_tn(act, hid_ref[:, :D]).astype(bf16)

    sgu_mine.wait()
    sgu_core.wait()
    mates = mate_ids()
    planes = len(mates) + 1
    for k in range(2 * planes):
        sgu_core_ref[k] = (sgu_core_ref[k].astype(f32) + sgu_mine_ref[k].astype(f32)).astype(bf16)
    sgu_planes = [
        remote(
            sgu_core_ref.at[pl.ds(h * planes + mate, 1)], sgu_slots_ref.at[number, pl.ds(h, 1)],
            sgu_sems, 1 + 2 * number + h, {"zlo": mate},
        )
        for number, mate in enumerate(mates)
        for h in range(2)
    ]
    for copy in sgu_planes:
        copy.start()

    owners, rows_out, _ = wout_send_ref.shape
    real = inner // owners
    for k in range(owners):
        wout_send_ref[k, :real, :] = wout_grad_ref[k * real : (k + 1) * real, :]
        if real < rows_out:
            wout_send_ref[k, real:, :] = jnp.zeros((rows_out - real, D), bf16)
    for e in range(held):
        total_ref[half * held + e] = sums_ref[e, half]
    total_ref[(1 - half) * held] = came_one_ref[...]
    masks = masks_ref[...]
    pre_step, dt_step, log_decay, exact, b_out, c_out, b_low, c_low = scan_setup(
        dt_ref, packed_ref, conv_ref, masks, head_ref, doc_col_ref[...], doc_row_ref[...], inner,
        neg_ref, scores_ref, cum_ref, cum_t_ref,
    )
    grad_scores_ref[...] = jnp.zeros_like(grad_scores_ref)
    row_ref[...] = jnp.zeros_like(row_ref)
    col_ref[...] = jnp.zeros_like(col_ref)
    step_ref[...] = jnp.zeros_like(step_ref)
    conv_grad_ref[...] = jnp.zeros_like(conv_grad_ref)
    cols_grad_ref[...] = jnp.zeros_like(cols_grad_ref)
    head_grad_ref[...] = jnp.zeros_like(head_grad_ref)
    row_mean = word_sum(hid_ref[:, D:])
    lanes_all = lax.broadcasted_iota(jnp.int32, (length, LANES), 1)
    lanes = lax.broadcasted_iota(jnp.int32, (LANES, LANES), 1)

    base = 1 + 2 * len(mates)
    sgu_half = remote(sgu_plane_ref.at[1 - half], sgu_came_ref, sgu_sems, base, partner_id())

    def sgu_middle():
        for copy in sgu_planes:
            copy.wait()
        for h in range(2):
            total = sgu_core_ref[h * planes + zlo].astype(f32)
            for number in range(len(mates)):
                total = total + sgu_slots_ref[number, h].astype(f32)
            sgu_plane_ref[h] = total.astype(bf16)
        sgu_half.start()

    @pl.loop(0, inner // LANES)
    def _(pair):
        pl.when(pair == inner // LANES // 2)(sgu_middle)
        at, x_at = pair_slices(pair, inner)
        grad_act = dot_nt(hid_ref[:, :D], wout_ref[at, :])
        conv_in = packed_ref[:, x_at].astype(f32)
        conv_out = conv_rows(conv_in, masks, conv_ref[:, at])
        values = jax.nn.silu(conv_out)
        gate_z = packed_ref[:, at].astype(f32)
        gate_act = jax.nn.silu(gate_z)
        full_y = y_ref[:, at].astype(f32)
        normed_mix = full_y * gate_act * scale_mix
        gain = cols_ref[0:1, at]
        skip = cols_ref[1:2, at]
        cols_grad_ref[0:1, at] = jnp.sum(grad_act * normed_mix, axis=0, keepdims=True)
        grad_gated = scale_mix * (grad_act * gain - normed_mix * row_mean)
        grad_y = grad_gated * gate_act
        proj_ref[:, at] = (grad_gated * full_y * silu_slope(gate_z)).astype(bf16)
        cols_grad_ref[1:2, at] = jnp.sum(grad_y * values, axis=0, keepdims=True)
        dt_wide = dot_words_left(dt_step, head_lanes(pair))
        scaled_low = (values * dt_wide).astype(bf16)
        low_ref[...] = grad_y.astype(bf16)
        scaled_ref[...] = jnp.zeros_like(scaled_ref)
        for k in range(2):
            head = 2 * pair + k
            cum_col = lane_of(cum_ref[...], head)
            cum_row = cum_t_ref[pl.ds(head, 1), :]
            for part in range(length // LANES):
                rows = slice(part * LANES, (part + 1) * LANES)
                wide = (part + 1) * LANES
                decay = jnp.exp(cum_col[rows] - cum_row[:, :wide] + neg_ref[rows, :wide])
                mixed = decay * scores_ref[rows, :wide]
                mine = jnp.where(lanes // HEAD_DIM == k, low_ref[rows, :].astype(f32), 0.0)
                mine = mine.astype(bf16)
                grad_mixed = dot_nt(mine, scaled_low[:wide])
                grad_scores_ref[rows, :wide] += grad_mixed * decay
                product = grad_mixed * mixed
                row_ref[rows, :] += jnp.where(
                    lanes == head, jnp.sum(product, axis=1, keepdims=True), 0.0
                )
                sums = jnp.sum(product, axis=0, keepdims=True)
                if part < length // LANES - 1:
                    sums = jnp.concatenate(
                        [sums, jnp.zeros((1, length - wide), f32)], axis=1
                    )
                col_sums = sums if part == 0 else col_sums + sums
                scaled_ref[:wide, :] += dot_tn(mixed.astype(bf16), mine)
            col_ref[pl.ds(head, 1), :] = col_sums
        grad_scaled = scaled_ref[...]
        step_ref[...] += dot_words_left(grad_scaled * values, head_lanes(pair, True))
        grad_values = grad_scaled * dt_wide + grad_y * skip
        grad_rows, taps = conv_rows_back(
            grad_values * silu_slope(conv_out), conv_in, masks, conv_ref[:, at]
        )
        proj_ref[:, x_at] = grad_rows.astype(bf16)
        for k in range(CONV + 1):
            conv_grad_ref[k : k + 1, at] = taps[k]

    sgu_half.wait()
    low = (sgu_plane_ref[half].astype(f32) + sgu_came_ref[...].astype(f32)).astype(bf16)
    rows_in = sgu_send_ref.shape[1]
    for place in range(count):
        sgu_send_ref[place] = low[place * rows_in : (place + 1) * rows_in]
    me = lax.axis_index("expert")
    sgu_rows = [
        remote(
            sgu_send_ref.at[other], sgu_got_ref.at[me], sgu_sems, base + 1 + number,
            {"expert": other},
        )
        for number, other in enumerate(peers()[2])
    ]
    sgu_rows.append(
        pltpu.make_async_copy(sgu_send_ref.at[me], sgu_got_ref.at[me], sgu_local_sems.at[1])
    )
    for copy in sgu_rows:
        copy.start()
    grad_scores = grad_scores_ref[...].astype(bf16)
    for number, (grad, before) in enumerate(
        ((dot_tn(grad_scores, c_low), b_out), (dot(grad_scores, b_low), c_out))
    ):
        start = inner + number * STATE
        conv_in = packed_ref[:, inner + start : inner + start + STATE].astype(f32)
        grad_rows, taps = conv_rows_back(
            grad * silu_slope(before), conv_in, masks, conv_ref[:, start : start + STATE]
        )
        proj_ref[:, inner + start : inner + start + STATE] = grad_rows.astype(bf16)
        for k in range(CONV + 1):
            conv_grad_ref[k : k + 1, start : start + STATE] = taps[k]
    grad_cum = row_ref[...] - col_ref[...].T
    grad_decay = dot_words(exact, grad_cum, ((0,), (0,)))
    rate_abs = head_ref[0:1]
    grad_pre = (step_ref[...] - grad_decay * rate_abs) * jax.nn.sigmoid(pre_step)
    head_grad_ref[0:1] = jnp.sum(grad_decay * log_decay, axis=0, keepdims=True)
    head_grad_ref[1:2] = jnp.sum(grad_pre, axis=0, keepdims=True)
    proj_ref[:, body:] = grad_pre.astype(bf16)
    for copy in out_copies + sgu_rows:
        copy.wait()
    total = out_mine_ref[...].astype(f32)
    for number in range(count - 1):
        total = total + out_got_ref[number].astype(f32)
    out_send_ref[...] = total.astype(bf16)
    across.wait()
    total_ref[(1 - half) * held + 1] = theirs_ref[...]


def route_kernel(two_ref, cot_ref, routes_ref, router_ref, ids_ref,
                 in_ref, top_ref, grad_ref, weights_ref, pick_ref, *, top_count, heads):
    tok = two_ref.shape[0]
    held, capacity, _ = in_ref.shape
    rows = two_ref[:, :D]
    logits = pltpu.roll(dot(rows, router_ref[...]), LANES - heads, 1)
    lanes = lax.broadcasted_iota(jnp.int32, (tok, LANES), 1)
    named = lanes < 0
    for k in range(top_count):
        named = named | (lanes == routes_ref[:, k : k + 1])
    top_logit = jnp.max(jnp.where(named, logits, -1e30), axis=1, keepdims=True)
    raised = jnp.where(named, jnp.exp(jnp.where(named, logits - top_logit, 0.0)), 0.0)
    weights = raised / jnp.sum(raised, axis=1, keepdims=True)
    weights_ref[...] = weights
    at = lax.broadcasted_iota(jnp.int32, (tok, tok), 0)
    to = lax.broadcasted_iota(jnp.int32, (tok, tok), 1)
    named_f = named.astype(f32)
    slot = dot((at > to).astype(f32).astype(bf16), named_f.astype(bf16))
    slots = lax.broadcasted_iota(jnp.int32, (tok, capacity), 1).astype(f32)
    picks = []
    for expert in range(held):
        lane = ids_ref[0] + expert
        mine = (lane_of(slot, lane) == slots) & (lane_of(named_f, lane) > 0.0)
        pick = mine.astype(f32).astype(bf16)
        picks.append(pick)
        in_ref[expert] = dot_tn(pick, rows).astype(bf16)
        top = dot_tn(pick, cot_ref[...])
        top_ref[expert] = top.astype(bf16)
        words = word_lanes(lane_of(weights, lane))
        slot_weight = jnp.sum(dot_tn(pick, words), axis=1, keepdims=True)
        grad_ref[expert] = (top * slot_weight).astype(bf16)
    pick_ref[0] = jnp.concatenate(picks, axis=1)


def expert_kernel(in_ref, top_ref, grad_ref, half_ref, gu_near_ref, gu_far_ref, down_near_ref,
                  down_far_ref, out_ref, back_ref, q_ref, sums_ref, mid_ref, act_ref):
    mates, _, rows_gu, _ = gu_near_ref.shape
    rows_down = down_near_ref.shape[2]
    shards = [(h, m) for h in range(2) for m in range(mates)]
    half = half_ref[0]
    sides = (
        (half, gu_near_ref, down_near_ref),
        (1 - half, gu_far_ref, down_far_ref),
    )

    def joined(ref, at, which=range(mates)):
        return jnp.concatenate([ref[m, 0, :, at] for m in which], axis=0)

    def block(place, size, offset=0):
        return pl.ds(pl.multiple_of(offset + place * size, LANES), size)

    wide = D // 2
    tall = EXPERT_FF // 2
    for place, _, down in sides:
        at = block(place, tall)
        up_at = block(place, tall, EXPERT_FF)
        gate = sum(
            dot(in_ref[0, :, block(side, wide)], joined(gu, at)) for side, gu, _ in sides
        )
        up = sum(
            dot(in_ref[0, :, block(side, wide)], joined(gu, up_at)) for side, gu, _ in sides
        )
        silu = jax.nn.silu(gate)
        mid_ref[:, at] = (silu * up).astype(bf16)
        grad_mid = dot_nt(grad_ref[0], joined(down, slice(None)))
        act_ref[:, at] = (grad_mid * up * silu_slope(gate)).astype(bf16)
        act_ref[:, up_at] = (grad_mid * silu).astype(bf16)
    step = 384
    each = step // rows_gu
    for side, gu, _ in sides:
        for part in range(wide // step):
            rows = joined(gu, slice(None), range(part * each, (part + 1) * each))
            at = pl.ds(pl.multiple_of(side * wide + part * step, LANES), step)
            back_ref[0, :, at] = dot_nt(act_ref[...], rows).astype(bf16)
    q = jnp.zeros((in_ref.shape[1], 1), f32)
    for part in range(D // step):
        at = slice(part * step, (part + 1) * step)
        rows = sum(dot(mid_ref[:, block(side, tall)], joined(down, at)) for side, _, down in sides)
        out_ref[0, :, at] = rows.astype(bf16)
        q = q + jnp.sum(rows * top_ref[0, :, at].astype(f32), axis=1, keepdims=True)
        chosen = shards[part * each : (part + 1) * each]
        for number in range(2):
            half_at = slice(number * EXPERT_FF, (number + 1) * EXPERT_FF)
            total = dot_tn(in_ref[0, :, at], act_ref[:, half_at]).astype(bf16)
            for k, (h, m) in enumerate(chosen):
                sums_ref[m, 0, h, number * rows_gu : (number + 1) * rows_gu, :] = total[
                    k * rows_gu : (k + 1) * rows_gu
                ]
    q_ref[0] = jnp.broadcast_to(q, q_ref.shape[1:])
    for part in range(D // EXPERT_FF):
        total = dot_tn(mid_ref[...], grad_ref[0, :, part * EXPERT_FF : (part + 1) * EXPERT_FF])
        total = total.astype(bf16)
        start = 2 * rows_gu + part * rows_down
        for k, (h, m) in enumerate(shards):
            sums_ref[m, 0, h, start : start + rows_down, :] = total[
                k * rows_down : (k + 1) * rows_down
            ]


def combine_kernel(pick_ref, weights_ref, ids_ref, out_ref, back_ref, q_ref, own_out_ref,
                   own_back_ref, mix_ref, rows_ref):
    held = out_ref.shape[0]
    capacity = out_ref.shape[1]
    block = pl.program_id(0)
    own = (block < pl.num_programs(0) // 2).astype(f32)
    picks = [pick_ref[0, :, e * capacity : (e + 1) * capacity] for e in range(held)]
    mix = own_out_ref[...].astype(f32) * own
    back = own_back_ref[...].astype(f32) * own
    lanes = lax.broadcasted_iota(jnp.int32, (pick_ref.shape[1], LANES), 1)
    words = jnp.zeros((pick_ref.shape[1], LANES), f32)
    for expert in range(held):
        weight = lane_of(weights_ref[...], ids_ref[0] + expert)
        mix = mix + weight * dot(picks[expert], out_ref[expert])
        back = back + dot(picks[expert], back_ref[expert])
        token_q = jnp.sum(dot(picks[expert], word_lanes(q_ref[expert, :, :1])), axis=1,
                          keepdims=True)
        for k, word in enumerate(split_words(token_q)):
            words = jnp.where(lanes == k * held + expert, word.astype(f32), words)
    mix_ref[...] = mix.astype(bf16)
    rows_ref[:, :D] = back.astype(bf16)
    rows_ref[:, D:] = words.astype(bf16)


def peers():
    count = lax.axis_size("expert")
    me = lax.axis_index("expert")
    return count, me, [lax.rem(me + step, count) for step in range(1, count)]


def group_ids():
    return [{"expert": other} for other in peers()[2]]


def partner_id():
    return {"zhi": 1 - lax.axis_index("zhi")}


def core_id():
    return {"core": 1 - lax.axis_index("core")}


def mate_ids():
    count, me = lax.axis_size("zlo"), lax.axis_index("zlo")
    return [lax.rem(me + step, count) for step in range(1, count)]


def greet(targets):
    barrier = pltpu.get_barrier_semaphore()
    for target in targets:
        pl.semaphore_signal(
            barrier, inc=1, device_id=target, device_id_type=pl.DeviceIdType.MESH
        )
    pl.semaphore_wait(barrier, len(targets))


def remote(src, dst, sems, number, target):
    return pltpu.make_async_remote_copy(
        src_ref=src, dst_ref=dst, send_sem=sems[0].at[number], recv_sem=sems[1].at[number],
        device_id=target, device_id_type=pl.DeviceIdType.MESH,
    )


def spread_copies(src, dst, sems, base):
    _, me, others = peers()
    return [
        remote(src, dst.at[me], sems, base + number, {"expert": other})
        for number, other in enumerate(others)
    ]


def reduce_copies(src, dst, sems, base, rows, start):
    _, _, others = peers()
    return [
        remote(
            src.at[pl.ds(pl.multiple_of(start + other * rows, rows), rows)],
            dst.at[number], sems, base + number, {"expert": other},
        )
        for number, other in enumerate(others)
    ]


def reduced(src, dst, rows, start, columns):
    _, me, others = peers()
    total = src[pl.ds(pl.multiple_of(start + me * rows, rows), rows), columns].astype(f32)
    for number in range(len(others)):
        total = total + dst[number, :, columns].astype(f32)
    return total


class MateSpread:
    def __init__(self, rows, full, sems, base, local_sem):
        planes = mate_ids()
        core, me = lax.axis_index("core"), lax.axis_index("zlo")
        slot = me * 2 + core
        self.over = [
            remote(rows, full.at[slot], sems, base + number, {"zlo": mate})
            for number, mate in enumerate(planes)
        ]
        count = len(planes)
        self.beside = [remote(rows, full.at[slot], sems, base + count, core_id())]
        size = count + 1
        self.onward = [
            remote(
                full.at[lax.rem(me + size - 1 - number, size) * 2 + core],
                full.at[lax.rem(me + size - 1 - number, size) * 2 + core],
                sems, base + count + 1 + number, core_id(),
            )
            for number in range(count)
        ]
        self.own = pltpu.make_async_copy(rows, full.at[slot], local_sem)

    def start(self):
        for copy in self.over + self.beside + [self.own]:
            copy.start()

    def forward(self):
        for copy, onward in zip(self.over, self.onward):
            copy.wait()
            onward.start()

    def finish(self):
        for copy in self.beside + self.onward + [self.own]:
            copy.wait()


def mate_sems(planes):
    return 2 * planes - 1


def near_ids():
    return [partner_id(), core_id()] + [{"zlo": mate} for mate in mate_ids()]


def plane_place():
    planes = lax.axis_size("zlo")
    return lax.axis_index("zhi") * planes + lax.axis_index("zlo"), 2 * planes


def plane_id(plane):
    planes = lax.axis_size("zlo")
    return {"zhi": plane // planes, "zlo": lax.rem(plane, planes)}


def line_sems(count):
    return [
        pltpu.SemaphoreType.DMA((count - 1,)), pltpu.SemaphoreType.DMA((count - 1,)),
        pltpu.SemaphoreType.DMA((count - 1,)), pltpu.SemaphoreType.DMA((count - 1,)),
        pltpu.SemaphoreType.DMA((2 * count - 1,)), pltpu.SemaphoreType.DMA((2 * count - 1,)),
    ]


class LineGather:
    def __init__(self, full, sems):
        self.full = full
        self.up, self.down, self.side = sems[0:2], sems[2:4], sems[4:6]
        self.core = lax.axis_index("core")
        self.at, self.count = plane_place()

    def block(self, plane):
        return self.full.at[plane * 2 + self.core]

    def move(self, plane, sems, number, target):
        return remote(self.block(plane), self.block(plane), sems, number, target)

    def upward(self, step):
        return self.move(self.at - step, self.up, step, plane_id(self.at + 1))

    def downward(self, step):
        return self.move(self.at + step, self.down, step, plane_id(self.at - 1))

    def sends_up(self, step):
        return (self.at < self.count - 1) & (self.at >= step)

    def sends_down(self, step):
        return (self.at > 0) & (self.at + step < self.count)

    def gets_up(self, step):
        return self.at >= step + 1

    def gets_down(self, step):
        return self.at + step + 1 < self.count

    def beside(self, plane, number):
        return self.move(plane, self.side, number, core_id())

    def start(self):
        pl.when(self.sends_up(0))(lambda: self.upward(0).start())
        pl.when(self.sends_down(0))(lambda: self.downward(0).start())
        self.beside(self.at, 0).start()

    def step(self, step):
        def from_below():
            self.move(self.at - step - 1, self.up, step, plane_id(self.at)).wait_recv()
            self.beside(self.at - step - 1, 1 + step).start()

        def from_above():
            self.move(self.at + step + 1, self.down, step, plane_id(self.at)).wait_recv()
            self.beside(self.at + step + 1, self.count + step).start()

        pl.when(self.gets_up(step))(from_below)
        if step + 1 < self.count - 1:
            pl.when(self.sends_up(step + 1))(lambda: self.upward(step + 1).start())
        pl.when(self.gets_down(step))(from_above)
        if step + 1 < self.count - 1:
            pl.when(self.sends_down(step + 1))(lambda: self.downward(step + 1).start())

    def finish(self):
        self.beside(self.at, 0).wait()
        for step in range(self.count - 1):
            pl.when(self.sends_up(step))(lambda step=step: self.upward(step).wait_send())
            pl.when(self.sends_down(step))(lambda step=step: self.downward(step).wait_send())
            pl.when(self.gets_up(step))(
                lambda step=step: self.beside(self.at - step - 1, 1 + step).wait()
            )
            pl.when(self.gets_down(step))(
                lambda step=step: self.beside(self.at + step + 1, self.count + step).wait()
            )


def start_kernel(lengths_ref, x_ref, cot_ref, routes_ref, w_in_ref, w_router_ref, w_sgu_ref, w_out_ref,
                 w_sd_ref, gu_ref, down_ref, conv_ref, head_ref, mixer_ref,
                 x_all_ref, cot_all_ref, cot_came_ref, routes_two_ref, win_all_ref, sgu_all_ref,
                 wout_own_ref, sd_own_ref, masks_ref, doc_col_ref, doc_row_ref, gu_kept_ref,
                 gu_sent_ref, down_kept_ref, down_sent_ref, conv_own_ref, head_own_ref, cols_ref,
                 wout_all_ref, sd_all_ref, routes_came_ref, win_ref, sgu_ref, wout_ref, sd_ref,
                 tail_ref, send_sems, recv_sems, out_send, out_recv, near_send, near_recv,
                 local_sems, *line):
    count, me, others = peers()
    at, planes = plane_place()
    half = lax.axis_index("zhi")
    sems = (send_sems, recv_sems)
    near = (near_send, near_recv)
    barrier = pltpu.get_barrier_semaphore()

    def tell(target):
        pl.semaphore_signal(
            barrier, inc=1, device_id=target, device_id_type=pl.DeviceIdType.MESH
        )

    for target in group_ids() + [partner_id(), core_id()]:
        tell(target)
    pl.when(at > 0)(lambda: tell(plane_id(at - 1)))
    pl.when(at < planes - 1)(lambda: tell(plane_id(at + 1)))
    ends = (at > 0).astype(jnp.int32) + (at < planes - 1).astype(jnp.int32)
    pl.semaphore_wait(barrier, count + 1 + ends)

    slot = at * 2 + lax.axis_index("core")
    peer_count = len(others)

    def pieces(src, dst, base, local):
        copies = [
            remote(src.at[other], dst.at[slot, me], sems, base + number, {"expert": other})
            for number, other in enumerate(others)
        ]
        return copies + [pltpu.make_async_copy(src.at[me], dst.at[slot, me], local)]

    def shared_rows(src, dst, base, local):
        return spread_copies(src, dst, sems, base) + [
            pltpu.make_async_copy(src, dst.at[me], local)
        ]

    def started(copies):
        for copy in copies:
            copy.start()
        return copies

    def ended(copies):
        for copy in copies:
            copy.wait()

    lines = [
        LineGather(full, line[6 * k : 6 * k + 6])
        for k, full in enumerate((win_all_ref, wout_all_ref, sgu_all_ref, sd_all_ref))
    ]
    inner = INNER // count
    heads = HEADS // count
    own_ff = SHARED_FF // count
    body = 2 * inner + 2 * STATE
    tail_ref[...] = jnp.zeros_like(tail_ref)
    tail_ref[0, :, :HEADS] = w_in_ref[:, 2 * INNER + 2 * STATE :]
    tail_ref[1, :, : w_router_ref.shape[1]] = w_router_ref[...]
    lanes_in = lax.broadcasted_iota(jnp.int32, tail_ref.shape[1:], 1)
    routers = pltpu.roll(tail_ref[1], heads, 1)
    for g in range(count):
        win_ref[g, :, :inner] = w_in_ref[:, g * inner : (g + 1) * inner].astype(bf16)
        win_ref[g, :, inner : 2 * inner] = w_in_ref[
            :, INNER + g * inner : INNER + (g + 1) * inner
        ].astype(bf16)
        win_ref[g, :, 2 * inner : body] = w_in_ref[:, 2 * INNER : 2 * INNER + 2 * STATE].astype(
            bf16
        )
        steps = pltpu.roll(tail_ref[0], LANES - g * heads, 1) if g else tail_ref[0]
        win_ref[g, :, body:] = jnp.where(lanes_in < heads, steps, routers).astype(bf16)
    win_copies = started(pieces(win_ref, win_all_ref, 0, local_sems.at[0]))
    wout_ref[...] = w_out_ref[...].astype(bf16)
    sd_ref[...] = w_sd_ref[...].astype(bf16)
    for g in range(count):
        for k in range(2):
            start = k * SHARED_FF + g * own_ff
            sgu_ref[g, :, k * own_ff : (k + 1) * own_ff] = w_sgu_ref[
                :, start : start + own_ff
            ].astype(bf16)
    keep = started([
        pltpu.make_async_copy(wout_ref, wout_all_ref.at[slot], local_sems.at[1]),
        pltpu.make_async_copy(sd_ref, sd_all_ref.at[slot], local_sems.at[2]),
    ])
    ended(keep)
    lines[1].start()
    lines[3].start()
    sgu_copies = started(pieces(sgu_ref, sgu_all_ref, peer_count, local_sems.at[3]))
    routes_over = started([remote(routes_ref, routes_came_ref, near, 1, partner_id())])
    ended(win_copies)
    lines[0].start()
    wide = started(
        shared_rows(x_ref, x_all_ref, 2 * peer_count, local_sems.at[4])
        + shared_rows(cot_ref, cot_all_ref, 4 * peer_count, local_sems.at[6])
        + shared_rows(routes_ref, routes_two_ref.at[0], 3 * peer_count, local_sems.at[5])
    )
    for step in range(planes - 1):
        lines[1].step(step)
        lines[3].step(step)
    lines[1].finish()
    lines[3].finish()
    rows = wout_own_ref.shape[0]
    out_copies = []
    for j in range(rows):
        for k, (full, own) in enumerate(
            ((wout_all_ref, wout_own_ref), (sd_all_ref, sd_own_ref))
        ):
            base = (2 * j + k) * peer_count
            for number, other in enumerate(others):
                out_copies.append(remote(
                    full.at[other * rows + j], own.at[j, me], (out_send, out_recv),
                    base + number, {"expert": other},
                ))
            out_copies.append(pltpu.make_async_copy(
                full.at[me * rows + j], own.at[j, me], local_sems.at[9 + 2 * j + k]
            ))
    started(out_copies)
    lines[0].step(0)
    ended(sgu_copies)
    lines[2].start()
    cot_over = started([remote(cot_ref, cot_came_ref, near, 0, partner_id())])

    at_inner = pl.ds(pl.multiple_of(me * inner, LANES), inner)
    conv_own_ref[...] = jnp.zeros_like(conv_own_ref)
    conv_own_ref[: CONV + 1, :inner] = conv_ref[:, at_inner]
    conv_own_ref[: CONV + 1, inner:] = conv_ref[:, INNER:]
    tail_ref[0] = jnp.zeros_like(tail_ref[0])
    tail_ref[0, :3, :HEADS] = head_ref[...]
    mine = tail_ref[0, :8, :]
    for g in range(1, count):
        moved = pltpu.roll(tail_ref[0, :8, :], LANES - g * heads, 1)
        mine = jnp.where(me == g, moved, mine)
    lane_eight = lax.broadcasted_iota(jnp.int32, mine.shape, 1)
    row_eight = lax.broadcasted_iota(jnp.int32, mine.shape, 0)
    mine = jnp.where((lane_eight < heads) & (row_eight < 3), mine, 0.0)
    head_own_ref[...] = jnp.where(
        (row_eight == 0) & (lane_eight < heads), jnp.exp(mine), mine
    )
    cols_ref[...] = jnp.zeros_like(cols_ref)
    cols_ref[0:1, :] = mixer_ref[:, at_inner]
    for pair in range(inner // LANES):
        cols_ref[1:2, pair * LANES : (pair + 1) * LANES] = dot_words_left(
            mine, head_lanes(pair)
        )[2:3]
    length = masks_ref.shape[0]
    place = lax.broadcasted_iota(jnp.int32, (length, LANES), 0)
    lane = lax.broadcasted_iota(jnp.int32, (length, LANES), 1)
    across = lax.broadcasted_iota(jnp.int32, (1, length), 1)
    doc, earlier, doc_row = place * 0 - 1, place * 0 - 1, across * 0 - 1
    start = 0
    for k in range(lengths_ref.shape[1]):
        doc = doc + (place >= start).astype(jnp.int32)
        earlier = earlier + (place - lane >= start).astype(jnp.int32)
        doc_row = doc_row + (across >= start).astype(jnp.int32)
        start = start + lengths_ref[0, k]
    masks_ref[...] = (doc == earlier).astype(f32)
    doc_col_ref[...] = doc[:, :1]
    doc_row_ref[...] = doc_row
    held = gu_kept_ref.shape[0]
    for e in range(held):
        gu_kept_ref[e] = gu_ref[half * held + e].astype(bf16)
        gu_sent_ref[e] = gu_ref[(1 - half) * held + e].astype(bf16)
        down_kept_ref[e] = down_ref[half * held + e].astype(bf16)
        down_sent_ref[e] = down_ref[(1 - half) * held + e].astype(bf16)

    ended(routes_over)
    wide += started(
        shared_rows(routes_came_ref, routes_two_ref.at[1], 5 * peer_count, local_sems.at[7])
    )
    for step in range(1, planes - 1):
        lines[0].step(step)
        lines[2].step(step - 1)
    lines[2].step(planes - 2)
    lines[0].finish()
    lines[2].finish()
    ended(wide + out_copies + cot_over)


def hidden_kernel(part_ref, tokens_ref, gain_ref, down_ref, down_sent_ref,
                  hidden_ref, res_ref, two_ref, down_all_ref, down_came_ref,
                  got_ref, send_sems, recv_sems, mate_send, mate_recv, mate_local):
    tok = tokens_ref.shape[0]
    sems = (send_sems, recv_sems)
    greet(group_ids() + near_ids())
    copies = reduce_copies(part_ref, got_ref, sems, 0, tok, 0)
    over = remote(down_sent_ref, down_came_ref, sems, len(copies), partner_id())
    weights = MateSpread(down_ref, down_all_ref, (mate_send, mate_recv), 0, mate_local)
    for copy in copies + [over]:
        copy.start()
    weights.start()
    for copy in copies:
        copy.wait()
    squares = word_sum(reduced(part_ref, got_ref, tok, 0, slice(D, D + LANES)))
    scale_mix = lax.rsqrt(squares / INNER + norm_eps)
    res = reduced(part_ref, got_ref, tok, 0, slice(0, D)) * scale_mix
    res_ref[...] = res
    hidden = tokens_ref[...].astype(f32) + res
    hidden_ref[...] = hidden
    scale = lax.rsqrt(jnp.mean(hidden * hidden, axis=1, keepdims=True) + norm_eps)
    two_ref[:, :D] = (hidden * scale * gain_ref[1:2]).astype(bf16)
    two_ref[:, D:] = word_lanes(scale_mix)
    weights.forward()
    over.wait()
    weights.finish()


def share_kernel(two_ref, gu_ref, down_ref, cot_ref, sgu_ref, sd_ref,
                 two_all_ref, gu_all_ref, down_all_ref, out_ref, back_ref, grad_gu_ref,
                 grad_down_ref, came_ref, rows_ref, mid_ref, act_ref,
                 send_sems, recv_sems, mate_send, mate_recv, local_sems):
    count, me, _ = peers()
    sems = (send_sems, recv_sems)
    mate = (mate_send, mate_recv)
    own_ref, other_ref = two_all_ref.at[0], two_all_ref.at[1]
    greet(group_ids() + near_ids())
    over = remote(two_ref, came_ref, sems, 0, partner_id())
    over.start()
    first = spread_copies(two_ref, own_ref, sems, 1)
    for copy in first:
        copy.start()
    mine = pltpu.make_async_copy(two_ref, own_ref.at[me], local_sems.at[0])
    mine.start()
    step = (mate_send.shape[0]) // 2
    gu_weights = MateSpread(gu_ref, gu_all_ref, mate, 0, local_sems.at[1])
    down_weights = MateSpread(down_ref, down_all_ref, mate, step, local_sems.at[2])
    gu_weights.start()
    down_weights.start()
    over.wait()
    second = spread_copies(came_ref, other_ref, sems, count)
    for copy in second:
        copy.start()
    theirs = pltpu.make_async_copy(came_ref, other_ref.at[me], local_sems.at[3])
    theirs.start()
    for copy in first:
        copy.wait()
    mine.wait()

    length, width = rows_ref.shape[0], sd_ref.shape[0]
    tok = two_ref.shape[0]
    for g in range(count):
        rows_ref[g * tok : (g + 1) * tok, :] = two_all_ref[0, g, :, :D]
    gate = dot(rows_ref[...], sgu_ref[:, :width])
    up = dot(rows_ref[...], sgu_ref[:, width:])
    silu = jax.nn.silu(gate)
    mid_ref[...] = (silu * up).astype(bf16)
    grad_mid = dot_nt(cot_ref[:length, :], sd_ref[...])
    act_ref[:, :width] = (grad_mid * up * silu_slope(gate)).astype(bf16)
    act_ref[:, width:] = (grad_mid * silu).astype(bf16)
    gu_weights.forward()

    @pl.loop(0, D // 256)
    def _(part):
        at = pl.ds(pl.multiple_of(part * 256, 256), 256)
        out_ref[:, at] = dot(mid_ref[...], sd_ref[:, at]).astype(bf16)
        back_ref[:, at] = dot_nt(act_ref[...], sgu_ref[at, :]).astype(bf16)

    owners, rows_down, _ = grad_down_ref.shape
    real = width // owners
    total = dot_tn(mid_ref[...], cot_ref[:length, :]).astype(bf16)
    for k in range(owners):
        grad_down_ref[k, :real, :] = total[k * real : (k + 1) * real]
        if real < rows_down:
            grad_down_ref[k, real:, :] = jnp.zeros((rows_down - real, D), bf16)
    each = D // owners
    wide = max(each, 384)
    for part in range(D // wide):
        total = dot_tn(rows_ref[:, part * wide : (part + 1) * wide], act_ref[...]).astype(bf16)
        for k in range(wide // each):
            owner = part * (wide // each) + k
            grad_gu_ref[owner // 2, owner % 2] = total[k * each : (k + 1) * each]
    for copy in second:
        copy.wait()
    theirs.wait()
    down_weights.forward()
    gu_weights.finish()
    down_weights.finish()


def q_lanes(sources, held, own_experts, half):
    lanes = lax.broadcasted_iota(jnp.int32, sources[0][1].shape, 1)
    total = jnp.zeros(lanes.shape, f32)
    for place, words in sources:
        for expert in range(held):
            value = sum(
                words[:, k * held + expert : k * held + expert + 1].astype(f32) for k in range(3)
            )
            lane = place * own_experts + half * held + expert
            total = jnp.where(lanes == lane, value, total)
    return total


def sum_plane(sums_ref, part_ref, slots_ref, expert):
    me = lax.axis_index("zlo")
    for h in range(sums_ref.shape[1]):
        total = part_ref[me, expert, h].astype(f32)
        for number in range(slots_ref.shape[0]):
            total = total + slots_ref[number, expert, h].astype(f32)
        sums_ref[expert, h] = total.astype(bf16)


def back_kernel(back_ref, hidden_ref, res_ref, cot_ref, weights_ref, router_ref, gain_ref, grads_ref,
                all_ref, grad_hidden_ref, grad_logits_ref, gain_grad_ref, sums_ref, theirs_ref,
                got_other_ref, got_own_ref, send_ref, came_ref, low_ref, slots_ref, core_ref, mine_ref,
                send_sems, recv_sems, plane_send, plane_recv, core_send, core_recv, mine_sems,
                local_sem, *, own_experts, heads):
    tok = cot_ref.shape[0]
    length = back_ref.shape[0] // 2
    held = own_experts // 2
    count, me, others = peers()
    half = lax.axis_index("zhi")
    sems = (send_sems, recv_sems)
    words_at = slice(D, D + LANES)
    mates = mate_ids()
    greet(group_ids() + near_ids())
    core = lax.axis_index("core")
    planes_here = core_ref.shape[0]
    core_copies = [
        [
            remote(
                grads_ref.at[z, 1 - core, expert], core_ref.at[z, expert], (core_send, core_recv),
                expert * planes_here + z, core_id(),
            )
            for z in range(planes_here)
        ]
        for expert in range(held)
    ]
    plane_sems = (plane_send, plane_recv)
    planes = [
        [
            remote(
                core_ref.at[mate, expert], slots_ref.at[number, expert], plane_sems,
                expert * len(mates) + number, {"zlo": mate},
            )
            for number, mate in enumerate(mates)
        ]
        for expert in range(held)
    ]
    first = reduce_copies(back_ref, got_other_ref, sems, 0, tok, length)
    second = reduce_copies(back_ref, got_own_ref, sems, count - 1, tok, 0)
    loads = [
        pltpu.make_async_copy(grads_ref.at[z, core], mine_ref.at[z], mine_sems.at[z])
        for z in range(planes_here)
    ]
    for copy in loads + first + core_copies[0] + core_copies[1]:
        copy.start()
    for copy in loads:
        copy.wait()
    for expert in range(held):
        for z, copy in enumerate(core_copies[expert]):
            copy.wait()
            for h in range(2):
                core_ref[z, expert, h] = (
                    core_ref[z, expert, h].astype(f32) + mine_ref[z, expert, h].astype(f32)
                ).astype(bf16)
        if expert == 0:
            for copy in planes[0]:
                copy.start()

    def q_of(start, slots):
        mine = back_ref[pl.ds(pl.multiple_of(start + me * tok, tok), tok), words_at]
        sources = [(me, mine)]
        for number in range(count - 1):
            sources.append((lax.rem(me + count - 1 - number, count), slots[number, :, words_at]))
        return q_lanes(sources, held, own_experts, half)

    for copy in first:
        copy.wait()
    send_ref[:, :D] = reduced(back_ref, got_other_ref, tok, length, slice(0, D)).astype(bf16)
    lanes = lax.broadcasted_iota(jnp.int32, (tok, LANES), 1)
    words = jnp.zeros((tok, LANES), f32)
    shift = LANES // 4
    for k, word in enumerate(split_words(q_of(length, got_other_ref))):
        placed = word.astype(f32) if k == 0 else pltpu.roll(word.astype(f32), k * shift, 1)
        words = words + placed
    send_ref[:, D:] = words.astype(bf16)
    over = remote(send_ref, came_ref, sems, 2 * (count - 1), {"zhi": 1 - half})
    over.start()
    for copy in second:
        copy.start()
    for copy in planes[0]:
        copy.wait()
    for copy in planes[1]:
        copy.start()
    sum_plane(sums_ref, core_ref, slots_ref, 0)
    across = remote(
        sums_ref.at[0, 1 - half], theirs_ref, plane_sems, held * len(mates), partner_id()
    )
    for copy in second:
        copy.wait()
    q_own = q_of(0, got_own_ref)
    total = reduced(back_ref, got_own_ref, tok, 0, slice(0, D))
    over.wait()
    across.start()
    came = came_ref[:, D:].astype(f32)
    came = came + pltpu.roll(came, LANES - shift, 1) + pltpu.roll(came, LANES - 2 * shift, 1)
    q = q_own + jnp.where(lanes < shift, came, 0.0)
    weights = weights_ref[...]
    grad_logits = weights * (q - jnp.sum(weights * q, axis=1, keepdims=True))
    grad_logits_ref[...] = grad_logits.astype(bf16)
    placed_logits = pltpu.roll(grad_logits, heads, 1).astype(bf16)
    total = total + came_ref[:, :D].astype(f32) + dot_nt(placed_logits, router_ref[...])
    hidden = hidden_ref[...]
    scale = lax.rsqrt(jnp.mean(hidden * hidden, axis=1, keepdims=True) + norm_eps)
    unit = hidden * scale
    gain_grad_ref[...] = jnp.broadcast_to(
        jnp.sum(total * unit, axis=0, keepdims=True), gain_grad_ref.shape
    )
    grad_hidden = cot_ref[...].astype(f32) + norm_back(total, unit, scale, gain_ref[1:2])
    grad_hidden_ref[...] = grad_hidden
    low_ref[:, :D] = grad_hidden.astype(bf16)
    row_mean = jnp.sum(low_ref[:, :D].astype(f32) * res_ref[...], axis=1, keepdims=True) / INNER
    low_ref[:, D:] = word_lanes(row_mean)
    third = spread_copies(low_ref, all_ref, sems, 2 * count - 1)
    for copy in third:
        copy.start()
    mine = pltpu.make_async_copy(low_ref, all_ref.at[me], local_sem)
    mine.start()
    for copy in planes[1]:
        copy.wait()
    sum_plane(sums_ref, core_ref, slots_ref, 1)
    for copy in third:
        copy.wait()
    mine.wait()
    across.wait()


def dense_kernel(x_ref, tokens_ref, win_ref, gain_ref, proj_ref, two_ref, logits_ref,
                 wout_ref, down_ref, grad_hidden_ref, out_ref, out_send_ref, hidden_ref,
                 conv_ref, cols_ref,
                 head_ref, gain_two_ref,
                 got_ref, own_out_ref, own_down_ref, tokens_grad_ref, output_ref, all_small_ref,
                 normed_ref, first_ref, second_ref, core_ref, slots_ref, plane_ref, came_ref,
                 send_ref, one_ref, one_got_ref, out_came_ref, out_got_ref, out_mine_ref, scale_ref,
                 step_ref, step_came_ref, core_send, core_recv, plane_send,
                 plane_recv, half_send, half_recv, row_send, row_recv, one_send, one_recv, out_send,
                 out_recv, small_send, small_recv, fold_send, fold_recv, local_sems, fold_sems,
                 own_sems, *, shared_chunks, heads):
    length = x_ref.shape[0]
    tok = tokens_ref.shape[0]
    chunks_one = first_ref.shape[0]
    chunks = core_ref.shape[0]
    own_rows = first_ref.shape[3]
    rows_in = send_ref.shape[2]
    core, half, zlo = lax.axis_index("core"), lax.axis_index("zhi"), lax.axis_index("zlo")
    mates = mate_ids()
    count, me, others = peers()
    planes = core_ref.shape[1] // 2
    greet(group_ids() + near_ids())

    def source(chunk):
        if chunk < chunks_one:
            return first_ref.at[chunk]
        start = (chunk - chunks_one) * CHUNK
        return second_ref.at[:, :, :, start : start + CHUNK]

    wide_out = D * wout_ref.shape[1] // own_rows
    wide_down = D * down_ref.shape[1] // own_rows
    filled = wide_out + wide_down
    if filled < second_ref.shape[3]:
        second_ref[:, :, :, filled:] = jnp.zeros(
            second_ref.shape[:3] + (second_ref.shape[3] - filled,), bf16
        )
    each = wout_ref.shape[0] // count
    fold_copies = []
    number = 0
    local = 0
    for full, width, offset in ((wout_ref, wide_out, 0), (down_ref, wide_down, wide_out)):
        rows = full.shape[1]
        for j in range(each):
            for fold in range(D // width):
                columns = slice(fold * width, (fold + 1) * width)
                place = pl.ds(fold * rows, rows)
                owner = me * each + j
                target = second_ref.at[
                    owner // 2, lax.rem(owner, 2), place, offset : offset + width
                ]
                for other in others:
                    fold_copies.append(remote(
                        full.at[j * count + other, :, columns], target, (fold_send, fold_recv),
                        number, {"expert": other},
                    ))
                    number += 1
                fold_copies.append(pltpu.make_async_copy(
                    full.at[j * count + me, :, columns], target, fold_sems.at[local]
                ))
                local += 1
    for copy in fold_copies:
        copy.start()

    core_copies, plane_copies, half_copies, row_copies = {}, {}, {}, {}

    def send_core(chunk):
        copies = [
            pltpu.make_async_remote_copy(
                src_ref=source(chunk).at[:, 1 - core],
                dst_ref=core_ref.at[chunk], send_sem=core_send.at[chunk],
                recv_sem=core_recv.at[chunk], device_id=core_id(),
                device_id_type=pl.DeviceIdType.MESH,
            )
        ]
        for copy in copies:
            copy.start()
        core_copies[chunk] = copies

    def send_plane(chunk):
        for copy in core_copies[chunk]:
            copy.wait()
        for k in range(2 * planes):
            core_ref[chunk, k] = (
                source(chunk)[k, core].astype(f32) + core_ref[chunk, k].astype(f32)
            ).astype(bf16)
        copies = [
            remote(
                core_ref.at[chunk, pl.ds(h * planes + mate, 1)],
                slots_ref.at[chunk, number, pl.ds(h, 1)],
                (plane_send, plane_recv), (chunk * len(mates) + number) * 2 + h, {"zlo": mate},
            )
            for number, mate in enumerate(mates)
            for h in range(2)
        ]
        for copy in copies:
            copy.start()
        plane_copies[chunk] = copies

    def send_half(chunk):
        for copy in plane_copies[chunk]:
            copy.wait()
        for h in range(2):
            total = core_ref[chunk, h * planes + zlo].astype(f32)
            for number in range(len(mates)):
                total = total + slots_ref[chunk, number, h].astype(f32)
            plane_ref[chunk, h] = total.astype(bf16)
        copy = remote(
            plane_ref.at[chunk, 1 - half], came_ref.at[chunk], (half_send, half_recv), chunk,
            partner_id(),
        )
        copy.start()
        half_copies[chunk] = copy

    def send_rows(chunk):
        half_copies[chunk].wait()
        total = plane_ref[chunk, half].astype(f32) + came_ref[chunk].astype(f32)
        for block in range(CHUNK // LANES):
            at = (chunk - chunks_one) * CHUNK + block * LANES
            columns = total[:, block * LANES : (block + 1) * LANES]
            if 0 <= at < wide_out:
                put(own_out_ref, columns, wide_out, at)
            elif wide_out <= at < wide_out + wide_down:
                put(own_down_ref, columns, wide_down, at - wide_out)
        if chunk not in shared_chunks:
            return
        spot = shared_chunks.index(chunk)
        columns = slice(spot * CHUNK, (spot + 1) * CHUNK)
        low = total.astype(bf16)
        for place in range(count):
            send_ref[spot, place] = low[place * rows_in : (place + 1) * rows_in]
        copies = [
            remote(
                send_ref.at[spot, other], got_ref.at[me, :, columns], (row_send, row_recv),
                chunk * (count - 1) + number, {"expert": other},
            )
            for number, other in enumerate(others)
        ]
        mine = pltpu.make_async_copy(
            send_ref.at[spot, me], got_ref.at[me, :, columns], local_sems.at[chunk]
        )
        for copy in copies + [mine]:
            copy.start()
        row_copies[chunk] = copies + [mine]

    def put(ref, columns, width, at):
        rows = ref.shape[0]
        for fold in range(D // width):
            ref[:, fold * width + at : fold * width + at + LANES] = columns[
                fold * rows : (fold + 1) * rows
            ]

    mixed = list(range(chunks_one, chunks))
    order = list(range(chunks_one)) + mixed
    ready = set()

    @pl.loop(0, length // LANES)
    def _(part):
        rows = pl.ds(pl.multiple_of(part * LANES, LANES), LANES)
        block = x_ref[rows, :].astype(f32)
        scale = lax.rsqrt(jnp.mean(block * block, axis=1, keepdims=True) + norm_eps)
        normed_ref[rows, :] = (block * scale * gain_ref[0:1]).astype(bf16)
        scale_ref[rows, :] = scale

    out_sems = (out_send, out_recv)
    out_over = remote(out_send_ref, out_came_ref, out_sems, 0, partner_id())
    out_copies = reduce_copies(out_ref, out_got_ref, out_sems, 1, tok, 0)
    out_copies.append(pltpu.make_async_copy(
        out_ref.at[pl.ds(pl.multiple_of(me * tok, tok), tok)], out_mine_ref, own_sems.at[2]
    ))

    def produce(chunk):
        if chunk in ready:
            return
        ready.add(chunk)
        if chunk in mixed:
            if not any(one in ready for one in mixed if one != chunk):
                for copy in fold_copies:
                    copy.wait()
            for one in mixed:
                ready.add(one)
                send_core(one)
            return
        else:
            at = slice(chunk * CHUNK, (chunk + 1) * CHUNK)
            total = dot_tn(normed_ref[...], proj_ref[:, at])
            if chunk == chunks_one - 1:
                logits = pltpu.roll(logits_ref[...].astype(f32), heads, 1).astype(bf16)
                router = dot_tn(two_ref[:, :D], logits)
                total = total + jnp.concatenate(
                    [jnp.zeros((D, CHUNK - LANES), f32), router], axis=1
                )
            low = total.astype(bf16)
            for k in range(D // own_rows):
                first_ref[chunk, k // 2, k % 2] = low[k * own_rows : (k + 1) * own_rows]
        send_core(chunk)

    begin = conv_ref.shape[1]
    step_ref[0, :, :begin] = conv_ref[...]
    step_ref[0, :, begin : begin + cols_ref.shape[1]] = cols_ref[...]
    begin += cols_ref.shape[1]
    step_ref[0, :, begin : begin + LANES] = head_ref[...]
    begin += LANES
    for k in range(D // CHUNK):
        step_ref[0, k : k + 1, begin:] = gain_two_ref[0:1, k * CHUNK : (k + 1) * CHUNK]

    def input_part(part):
        at = slice(part * CHUNK, (part + 1) * CHUNK)
        one = dot_nt(proj_ref[...], win_ref[at, :])
        gains = jnp.sum(one * (x_ref[:, at].astype(f32) * scale_ref[...]), axis=0, keepdims=True)
        row = D // CHUNK + part
        step_ref[0, row : row + 1, begin:] = gains
        one_ref[:, at] = one.astype(bf16)

    one_copies = reduce_copies(one_ref, one_got_ref, (one_send, one_recv), 0, tok, 0)

    small_sems = (small_send, small_recv)
    rounds = [[core_id()], [{"zlo": mate} for mate in mates], [partner_id()]]
    bases = [sum(len(targets) for targets in rounds[:level]) for level in range(4)]
    small_copies = [
        [
            remote(
                step_ref.at[level], step_came_ref.at[bases[level] + k], small_sems,
                bases[level] + k, target,
            )
            for k, target in enumerate(targets)
        ]
        for level, targets in enumerate(rounds)
    ]
    small_copies.append([
        remote(
            step_ref.at[3], all_small_ref.at[me], small_sems, bases[3] + number, {"expert": other}
        )
        for number, other in enumerate(others)
    ])
    small_copies[3].append(
        pltpu.make_async_copy(step_ref.at[3], all_small_ref.at[me], own_sems.at[1])
    )

    def small_start(level):
        for copy in small_copies[level]:
            copy.start()

    def small_sum(level):
        total = step_ref[level]
        for k, copy in enumerate(small_copies[level]):
            copy.wait()
            total = total + step_came_ref[bases[level] + k]
        step_ref[level + 1] = total

    amount = len(order)
    parts = D // CHUNK
    small_every = max(1, (amount + 4 - parts) // 3)
    produce(order[0])
    for tick in range(amount + 4):
        if tick + 1 < amount:
            produce(order[tick + 1])
        if tick < amount:
            send_plane(order[tick])
        if tick == 2:
            out_over.start()
        if tick == parts:
            for copy in out_copies:
                copy.start()
        if 2 <= tick < amount + 2:
            send_half(order[tick - 2])
        if 4 <= tick:
            send_rows(order[tick - 4])
        if tick < parts:
            input_part(tick)
        if tick == parts - 1:
            for copy in one_copies:
                copy.start()
            small_start(0)
        level = (tick - parts) // small_every
        if tick >= parts and (tick - parts) % small_every == small_every - 1 and level < 3:
            small_sum(level)
            small_start(level + 1)
    for copy in one_copies:
        copy.wait()
    total = reduced(one_ref, one_got_ref, tok, 0, slice(0, D))
    block = tokens_ref[...].astype(f32)
    scale = lax.rsqrt(jnp.mean(block * block, axis=1, keepdims=True) + norm_eps)
    tokens_grad_ref[...] = (
        grad_hidden_ref[...] + norm_back(total, block * scale, scale, gain_ref[0:1])
    ).astype(bf16)
    for copy in out_copies + [out_over]:
        copy.wait()
    total = hidden_ref[...] + out_came_ref[...].astype(f32) + out_mine_ref[...].astype(f32)
    for number in range(count - 1):
        total = total + out_got_ref[number].astype(f32)
    output_ref[...] = total.astype(bf16)
    for copy in small_copies[3]:
        copy.wait()
    for copies in row_copies.values():
        for copy in copies:
            copy.wait()


def kernel_room(shapes):
    total = 0
    for shape, dtype in shapes:
        size = jnp.dtype(dtype).itemsize
        rows = shape[-2] if len(shape) > 1 else 1
        padded = -(-rows // 16) * 16 * -(-shape[-1] // LANES) * LANES
        total += math.prod(shape[:-2]) * padded * size
    rows = max([0] + [shape[0] for shape, _ in shapes if len(shape) == 2 and shape[0] == shape[1]])
    total += 20 * rows * rows + 5 * 1024 * 1024
    return min(max(total, 47 * 1024 * 1024), 62 * 1024 * 1024)


def remote_call(kernel, number, out_shapes, scratch, sems, *operands, outside=(), left=()):
    spec = pl.BlockSpec(memory_space=pltpu.VMEM)
    scalars = pl.BlockSpec(memory_space=pltpu.SMEM)
    anywhere = pl.BlockSpec(memory_space=pl.ANY)
    inside = [one for k, one in enumerate(operands) if k not in outside]
    inside += [one for k, one in enumerate(out_shapes) if k not in left]
    return pl.pallas_call(
        kernel,
        out_shape=out_shapes,
        in_specs=[
            anywhere if k in outside
            else scalars if one.dtype == jnp.int32 and one.size < LANES else spec
            for k, one in enumerate(operands)
        ],
        out_specs=[anywhere if k in left else spec for k in range(len(out_shapes))],
        scratch_shapes=[pltpu.VMEM(shape, dtype) for shape, dtype in scratch] + sems,
        compiler_params=pltpu.CompilerParams(
            collective_id=number, has_side_effects=True,
            vmem_limit_bytes=kernel_room(
                [(one.shape, one.dtype) for one in inside] + scratch
            ),
        ),
    )(*operands)


def vmem_call(kernel, out_shapes, scratch, *operands):
    spec = pl.BlockSpec(memory_space=pltpu.VMEM)
    return pl.pallas_call(
        kernel,
        out_shape=out_shapes,
        in_specs=[spec] * len(operands),
        out_specs=[spec] * len(out_shapes),
        scratch_shapes=[pltpu.VMEM(shape, dtype) for shape, dtype in scratch],
        compiler_params=pltpu.CompilerParams(vmem_limit_bytes=56 * 1024 * 1024),
    )(*operands)


def grid_call(kernel, steps, in_specs, out_specs, out_shapes, scratch, *operands):
    return pl.pallas_call(
        kernel,
        grid=(steps,),
        out_shape=out_shapes,
        in_specs=in_specs,
        out_specs=out_specs,
        scratch_shapes=[pltpu.VMEM(shape, dtype) for shape, dtype in scratch],
        compiler_params=pltpu.CompilerParams(vmem_limit_bytes=56 * 1024 * 1024),
    )(*operands)


def update_kernel(got_ref, got_sgu_ref, sum_out_ref, sum_down_ref, *refs, inner, own_ff, heads):
    groups, _, _ = got_ref.shape
    names = 4
    given = [refs[3 * k : 3 * k + 3] for k in range(names)]
    made = [refs[3 * names + 4 * k : 3 * names + 4 * k + 4] for k in range(names)]
    router_ref = refs[7 * names]

    def step(which, at, gradient):
        weight, first, second = (ref[:, at] for ref in given[which])
        parts = adam_step(weight, first, second, gradient)[:4]
        for ref, part in zip(made[which], parts):
            ref[:, at] = part

    def piece(place, start, size):
        return got_ref[place, :, start : start + size].astype(f32)

    body = 2 * inner + 2 * STATE
    for place in range(groups):
        for k in range(2):
            start = k * INNER + place * inner
            step(0, slice(start, start + inner), piece(place, k * inner, inner))
    step(0, slice(2 * INNER, 2 * INNER + 2 * STATE),
         sum(piece(place, 2 * inner, 2 * STATE) for place in range(groups)))
    blocks = [piece(place, body, LANES) for place in range(groups)]
    lanes = lax.broadcasted_iota(jnp.int32, blocks[0].shape, 1)
    steps = sum(
        pltpu.roll(jnp.where(lanes < heads, block, 0.0), place * heads, 1)
        if place else jnp.where(lanes < heads, block, 0.0)
        for place, block in enumerate(blocks)
    )
    step(0, slice(2 * INNER + 2 * STATE, 2 * INNER + 2 * STATE + groups * heads),
         steps[:, : groups * heads])
    router_ref[...] = pltpu.roll(sum(blocks), LANES - heads, 1)
    step(1, slice(0, D), sum_out_ref[: given[1][0].shape[0], :])
    step(3, slice(0, D), sum_down_ref[: given[3][0].shape[0], :])
    for place in range(groups):
        for k in range(2):
            at = k * SHARED_FF + place * own_ff
            columns = slice(k * own_ff, (k + 1) * own_ff)
            step(2, slice(at, at + own_ff), got_sgu_ref[place, :, columns].astype(f32))


def on_device(
    tokens, cotangent, lengths, routes,
    w_in, w_in_first, w_in_second,
    w_out, w_out_first, w_out_second,
    w_router, w_router_first, w_router_second,
    w_shared_gu, w_shared_gu_first, w_shared_gu_second,
    w_shared_down, w_shared_down_first, w_shared_down_second,
    w_expert_gu, w_expert_gu_first, w_expert_gu_second,
    w_expert_down, w_expert_down_first, w_expert_down_second,
    norm_gains, norm_gains_first, norm_gains_second,
    conv_params, conv_params_first, conv_params_second,
    head_params, head_params_first, head_params_second,
    mixer_gain, mixer_gain_first, mixer_gain_second,
):
    groups = lax.axis_size("expert")
    copies = (lax.axis_size("zhi") * lax.axis_size("zlo") * lax.axis_size("core"))
    place = lax.axis_index("expert")
    tok = tokens.shape[0]
    length = tok * groups
    top = routes.shape[1]
    experts = w_router.shape[1]
    own_experts = w_expert_gu.shape[0]
    capacity = (4 * tok * top + 3 * experts - 1) // (3 * experts)
    inner = INNER // groups
    heads = HEADS // groups
    rows_in = w_in.shape[0]
    rows_out = w_out.shape[0]
    rows_sd = w_shared_down.shape[0]
    own_ff = SHARED_FF // groups
    per_pair = copies // groups
    conv_cols = inner + 2 * STATE
    body = 2 * inner + 2 * STATE

    pairs = pltpu.SemaphoreType.DMA
    route_pad = jnp.pad(routes, ((0, 0), (0, LANES - top)))
    row_shape = jax.ShapeDtypeStruct((groups, tok, D), bf16)
    route_shape = jax.ShapeDtypeStruct((groups, tok, LANES), jnp.int32)
    half = lax.axis_index("zhi")
    held = own_experts // 2
    rows_egu, rows_ed = w_expert_gu.shape[1], w_expert_down.shape[1]
    gu_held = jax.ShapeDtypeStruct((held, rows_egu, 2 * EXPERT_FF), bf16)
    ed_held = jax.ShapeDtypeStruct((held, rows_ed, D), bf16)
    (
        x_all, cot_all, cot_came, routes_two, win, sgu, wout, sd, masks, doc_col, doc_row,
        egu_kept, egu_sent, ed_kept, ed_sent, conv_pad, head_rows, col_rows,
    ) = remote_call(
        start_kernel, 7,
        [
            jax.ShapeDtypeStruct((groups, tok, D), bf16),
            jax.ShapeDtypeStruct((groups, tok, D), bf16),
            jax.ShapeDtypeStruct((tok, D), bf16),
            jax.ShapeDtypeStruct((2, groups, tok, LANES), jnp.int32),
            jax.ShapeDtypeStruct((copies, groups, rows_in, body + LANES), bf16),
            jax.ShapeDtypeStruct((copies, groups, rows_in, 2 * own_ff), bf16),
            jax.ShapeDtypeStruct((per_pair, groups, rows_out, D), bf16),
            jax.ShapeDtypeStruct((per_pair, groups, rows_sd, D), bf16),
            jax.ShapeDtypeStruct((length, LANES), f32),
            jax.ShapeDtypeStruct((length, 1), jnp.int32),
            jax.ShapeDtypeStruct((1, length), jnp.int32),
            gu_held, gu_held, ed_held, ed_held,
            jax.ShapeDtypeStruct((8, conv_cols), f32),
            jax.ShapeDtypeStruct((8, LANES), f32),
            jax.ShapeDtypeStruct((8, inner), f32),
        ],
        [
            ((copies, rows_out, D), bf16), ((copies, rows_sd, D), bf16), ((tok, LANES), jnp.int32),
            ((groups, rows_in, body + LANES), bf16), ((groups, rows_in, 2 * own_ff), bf16),
            ((rows_out, D), bf16), ((rows_sd, D), bf16), ((2, max(8, rows_in), LANES), f32),
        ],
        [pairs((7 * (groups - 1),))] * 2
        + [pairs((2 * per_pair * (groups - 1),))] * 2
        + [pairs((2,))] * 2
        + [pairs((9 + 2 * per_pair,))]
        + line_sems(copies // 2) * 4,
        lengths, tokens, cotangent, route_pad, w_in, w_router, w_shared_gu, w_out,
        w_shared_down, w_expert_gu, w_expert_down, conv_params, head_params,
        mixer_gain.reshape(1, INNER),
    )
    x_all = x_all.reshape(length, D)
    routes_two = routes_two.reshape(2 * length, LANES)
    win = win.reshape(D, -1)
    sgu = sgu.reshape(D, -1)
    wout = wout.reshape(inner, D)
    sd = sd.reshape(own_ff, D)
    router = win[:, body:]


    square = ((length, length), f32)
    lane_rows = ((length, LANES), f32)
    lane_cols = ((LANES, length), f32)
    planes_half = copies // 4
    mates = copies // 2
    spread_sems = [pairs((mate_sems(planes_half),))] * 2
    gu_all = jax.ShapeDtypeStruct((mates,) + egu_kept.shape, bf16)
    ed_all = jax.ShapeDtypeStruct((mates,) + ed_kept.shape, bf16)
    packed, dt_raw, full_y, res_part, gu_near, gu_came, cot_two = remote_call(
        forward_kernel, 3,
        [
            jax.ShapeDtypeStruct((length, body), bf16),
            jax.ShapeDtypeStruct((length, LANES), f32),
            jax.ShapeDtypeStruct((length, inner), bf16),
            jax.ShapeDtypeStruct((length, D + LANES), bf16),
            gu_all,
            gu_held,
            jax.ShapeDtypeStruct((2, groups, tok, D), bf16),
        ],
        [((length, D), bf16), square, square, lane_rows, lane_cols, ((length, inner), bf16),
         lane_rows],
        [pairs((groups,))] * 2 + spread_sems + [pairs(()), pairs((2,))],
        x_all, win, norm_gains, conv_pad, masks, head_rows, col_rows, doc_col, doc_row, wout,
        egu_kept, egu_sent, cot_all, cot_came,
    )
    cot_two = cot_two.reshape(2 * length, D)
    hidden, mixer_res, two_own, ed_near, ed_came = remote_call(
        hidden_kernel, 0,
        [
            jax.ShapeDtypeStruct((tok, D), f32),
            jax.ShapeDtypeStruct((tok, D), f32),
            jax.ShapeDtypeStruct((tok, D + LANES), bf16),
            ed_all,
            ed_held,
        ],
        [((groups - 1, tok, D + LANES), bf16)],
        [pairs((groups,))] * 2 + spread_sems + [pairs(())],
        res_part, tokens, norm_gains, ed_kept, ed_sent,
    )
    gathered_shape = jax.ShapeDtypeStruct((groups, tok, D + LANES), bf16)
    own_rows = groups * rows_in
    payload = ((tok, D + LANES), bf16)
    tile = 16
    down_rows = -(-rows_sd // tile) * tile
    two_rows, gu_far, ed_far, shared_out, shared_back, grad_sgu, grad_sd = remote_call(
        share_kernel, 1,
        [
            jax.ShapeDtypeStruct((2, groups, tok, D + LANES), bf16), gu_all, ed_all,
            jax.ShapeDtypeStruct((length, D), bf16),
            jax.ShapeDtypeStruct((length, D), bf16),
            jax.ShapeDtypeStruct((copies // 2, 2, own_rows, 2 * own_ff), bf16),
            jax.ShapeDtypeStruct((copies, down_rows, D), bf16),
        ],
        [
            payload, ((length, D), bf16),
            ((length, own_ff), bf16), ((length, 2 * own_ff), bf16),
        ],
        [pairs((2 * groups - 1,))] * 2 + [pairs((2 * mate_sems(planes_half),))] * 2 + [pairs((4,))],
        two_own, gu_came, ed_came, cot_two, sgu, sd,
    )
    scale_words = two_rows[0, :, :, D:].reshape(length, LANES)
    two_rows = two_rows.reshape(2 * length, D + LANES)

    blocks = 2 * groups
    expert_at = (place * own_experts + half * held).reshape(1)
    slot_rows = blocks * capacity

    def by_block(*shape):
        return pl.BlockSpec(shape, lambda b: (b,) + (0,) * (len(shape) - 1))

    def fixed(*shape):
        return pl.BlockSpec(shape, lambda b: (0,) * len(shape))

    slot_spec = pl.BlockSpec((held, capacity, D), lambda b: (0, b, 0))
    in_smem = pl.BlockSpec(memory_space=pltpu.SMEM)
    slot_shape = jax.ShapeDtypeStruct((held, slot_rows, D), bf16)
    slot_in, slot_top, slot_grad, weights, pick = grid_call(
        functools.partial(route_kernel, top_count=top, heads=heads), blocks,
        [by_block(tok, D + LANES), by_block(tok, D), by_block(tok, LANES), fixed(D, LANES), in_smem],
        [slot_spec] * 3 + [by_block(tok, LANES), by_block(1, tok, held * capacity)],
        [slot_shape] * 3
        + [
            jax.ShapeDtypeStruct((2 * length, LANES), f32),
            jax.ShapeDtypeStruct((blocks, tok, held * capacity), bf16),
        ],
        [],
        two_rows, cot_two, routes_two, router, expert_at,
    )
    packed_rows = 2 * rows_egu + rows_ed * D // EXPERT_FF

    def by_expert(*shape):
        return pl.BlockSpec((1,) + shape, lambda e: (e,) + (0,) * len(shape))

    def weight_spec(rows, columns):
        return pl.BlockSpec((mates, 1, rows, columns), lambda e: (0, e, 0, 0))

    slot_out, slot_back, slot_q, expert_grads = grid_call(
        expert_kernel, held,
        [by_expert(slot_rows, D)] * 3
        + [in_smem]
        + [weight_spec(rows_egu, 2 * EXPERT_FF)] * 2
        + [weight_spec(rows_ed, D)] * 2,
        [by_expert(slot_rows, D)] * 2
        + [
            by_expert(slot_rows, LANES),
            pl.BlockSpec((mates, 1, 2, packed_rows, EXPERT_FF), lambda e: (0, e, 0, 0, 0)),
        ],
        [slot_shape] * 2
        + [
            jax.ShapeDtypeStruct((held, slot_rows, LANES), f32),
            jax.ShapeDtypeStruct((mates, held, 2, packed_rows, EXPERT_FF), bf16),
        ],
        [((slot_rows, EXPERT_FF), bf16), ((slot_rows, 2 * EXPERT_FF), bf16)],
        slot_in, slot_top, slot_grad, half.reshape(1), gu_near, gu_far, ed_near, ed_far,
    )
    own_spec = pl.BlockSpec((tok, D), lambda b: (jnp.minimum(b, groups - 1), 0))
    out_parts, back_parts = grid_call(
        combine_kernel, blocks,
        [
            by_block(1, tok, held * capacity), by_block(tok, LANES), in_smem, slot_spec, slot_spec,
            pl.BlockSpec((held, capacity, LANES), lambda b: (0, b, 0)), own_spec, own_spec,
        ],
        [by_block(tok, D), by_block(tok, D + LANES)],
        [
            jax.ShapeDtypeStruct((2 * length, D), bf16),
            jax.ShapeDtypeStruct((2 * length, D + LANES), bf16),
        ],
        [],
        pick, weights, expert_at, slot_out, slot_back, slot_q, shared_out, shared_back,
    )

    weights_tok = lax.dynamic_slice_in_dim(weights, place * tok, tok, axis=0)
    gathered_shape = jax.ShapeDtypeStruct((groups, tok, D + LANES), bf16)
    hidden_all, grad_hidden, grad_logits, gain_two, expert_sums, came_one = remote_call(
        functools.partial(back_kernel, own_experts=own_experts, heads=heads), 2,
        [
            gathered_shape,
            jax.ShapeDtypeStruct((tok, D), f32),
            jax.ShapeDtypeStruct((tok, LANES), bf16),
            jax.ShapeDtypeStruct((8, D), f32),
            jax.ShapeDtypeStruct((held, 2, packed_rows, EXPERT_FF), bf16),
            jax.ShapeDtypeStruct((packed_rows, EXPERT_FF), bf16),
        ],
        [((groups - 1, tok, D + LANES), bf16)] * 2
        + [payload] * 3
        + [
            ((planes_half - 1, held, 2, packed_rows, EXPERT_FF), bf16),
            ((planes_half, held, 2, packed_rows, EXPERT_FF), bf16),
            ((planes_half, held, 2, packed_rows, EXPERT_FF), bf16),
        ],
        [
            pairs((3 * groups - 2,)), pairs((3 * groups - 2,)),
            pairs((held * (planes_half - 1) + 1,)), pairs((held * (planes_half - 1) + 1,)),
            pairs((held * planes_half,)), pairs((held * planes_half,)),
            pairs((planes_half,)), pairs(()),
        ],
        back_parts, hidden, mixer_res, cotangent, weights_tok, router, norm_gains,
        expert_grads.reshape((planes_half, 2) + expert_grads.shape[1:]), outside=(7,),
    )
    hidden_all = hidden_all.reshape(length, -1)
    grad_gain_two = gain_two[0]

    out_rows = -(-rows_out // tile) * tile
    (
        grad_proj, conv_grads, col_grads, head_grads, expert_sum, grad_wout, out_other,
        got_sgu,
    ) = remote_call(
        backward_kernel, 5,
        [
            jax.ShapeDtypeStruct((length, body + LANES), bf16),
            jax.ShapeDtypeStruct((8, conv_cols), f32),
            jax.ShapeDtypeStruct((8, inner), f32),
            jax.ShapeDtypeStruct((8, LANES), f32),
            jax.ShapeDtypeStruct((own_experts, packed_rows, EXPERT_FF), bf16),
            jax.ShapeDtypeStruct((copies, out_rows, D), bf16),
            jax.ShapeDtypeStruct((tok, D), bf16),
            jax.ShapeDtypeStruct((groups, rows_in, 2 * own_ff), bf16),
        ],
        [square, square, lane_rows, lane_cols, square, lane_rows, lane_cols, lane_rows, lane_rows,
         ((length, LANES), bf16), ((inner, D), bf16), ((packed_rows, EXPERT_FF), bf16),
         ((groups - 1, tok, D), bf16), ((tok, D), bf16),
         ((copies // 2, own_rows, 2 * own_ff), bf16), ((copies // 2, own_rows, 2 * own_ff), bf16),
         ((planes_half - 1, 2, own_rows, 2 * own_ff), bf16), ((2, own_rows, 2 * own_ff), bf16),
         ((own_rows, 2 * own_ff), bf16), ((groups, rows_in, 2 * own_ff), bf16)],
        [pairs(()), pairs(()), pairs((groups - 1,)), pairs((groups - 1,)), pairs(())]
        + [pairs((2 * planes_half + groups - 1,))] * 2
        + [pairs((2,))],
        hidden_all, scale_words, wout, conv_pad, masks, head_rows, col_rows, doc_col, doc_row,
        packed, dt_raw, full_y, expert_sums, came_one, out_parts, grad_sgu,
        outside=(14, 15),
    )
    wide_out = D * out_rows // own_rows
    wide_down = D * down_rows // own_rows
    chunks_one = (body + LANES) // CHUNK
    chunks_two = -(-(wide_out + wide_down) // CHUNK)
    chunks = chunks_one + chunks_two
    shared_chunks = list(range(chunks_one))
    shared_wide = len(shared_chunks) * CHUNK
    small_wide = conv_cols + inner + LANES + CHUNK
    folds = own_rows // out_rows + own_rows // down_rows
    dense_sems = [pairs((chunks,))] * 2 + [pairs((2 * chunks * (planes_half - 1),))] * 2
    dense_sems += [pairs((chunks,))] * 2 + [pairs((chunks * (groups - 1),))] * 2
    dense_sems += [pairs((groups - 1,))] * 2 + [pairs((groups,))] * 2
    dense_sems += [pairs((planes_half + groups,))] * 2
    dense_sems += [pairs((per_pair * folds * (groups - 1),))] * 2
    dense_sems += [pairs((chunks,)), pairs((per_pair * folds,)), pairs((3,))]
    got_rows, sum_out, sum_sd, grad_tokens, output, small = remote_call(
        functools.partial(dense_kernel, shared_chunks=shared_chunks, heads=heads), 6,
        [
            jax.ShapeDtypeStruct((groups, rows_in, shared_wide), bf16),
            jax.ShapeDtypeStruct((out_rows, D), f32),
            jax.ShapeDtypeStruct((down_rows, D), f32),
            jax.ShapeDtypeStruct((tok, D), bf16),
            jax.ShapeDtypeStruct((tok, D), bf16),
            jax.ShapeDtypeStruct((groups, 8, small_wide), f32),
        ],
        [
            ((length, D), bf16),
            ((chunks_one, copies // 2, 2, own_rows, CHUNK), bf16),
            ((copies // 2, 2, own_rows, chunks_two * CHUNK), bf16),
            ((chunks, copies // 2, own_rows, CHUNK), bf16),
            ((chunks, planes_half - 1, 2, own_rows, CHUNK), bf16),
            ((chunks, 2, own_rows, CHUNK), bf16),
            ((chunks, own_rows, CHUNK), bf16),
            ((len(shared_chunks), groups, rows_in, CHUNK), bf16),
            ((length, D), bf16),
            ((groups - 1, tok, D), bf16),
            ((tok, D), bf16),
            ((groups - 1, tok, D), bf16),
            ((tok, D), bf16),
            ((length, 1), f32),
            ((4, 8, small_wide), f32),
            ((planes_half + 1, 8, small_wide), f32),
        ],
        dense_sems,
        x_all, tokens, win, norm_gains, grad_proj, two_own, grad_logits, grad_wout,
        grad_sd, grad_hidden, out_parts, out_other, hidden, conv_grads, col_grads, head_grads, gain_two,
        outside=(7, 8, 10),
    )
    sum_egu = jnp.concatenate(
        [expert_sum[:, :rows_egu], expert_sum[:, rows_egu : 2 * rows_egu]], axis=2
    ).astype(f32)
    sum_ed = jnp.concatenate(
        [
            expert_sum[:, 2 * rows_egu + k * rows_ed : 2 * rows_egu + (k + 1) * rows_ed]
            for k in range(D // EXPERT_FF)
        ],
        axis=2,
    ).astype(f32)

    sum_conv = jnp.concatenate(
        [
            small[:, : CONV + 1, :inner].transpose(1, 0, 2).reshape(CONV + 1, INNER),
            jnp.sum(small[:, : CONV + 1, inner:conv_cols], axis=0),
        ],
        axis=1,
    )
    start = conv_cols
    sum_mixer = small[:, 0, start : start + inner].reshape(INNER)
    sum_skip = jnp.sum(
        small[:, 1, start : start + inner].reshape(groups, heads, HEAD_DIM), axis=2
    ).reshape(HEADS)
    start = start + inner
    sum_head = jnp.stack(
        [small[:, k, start : start + heads].reshape(HEADS) for k in range(2)] + [sum_skip]
    )
    start = start + LANES
    gain_sums = jnp.sum(small[:, :, start:], axis=0)
    sum_gains = jnp.stack(
        [gain_sums[D // CHUNK :].reshape(D), gain_sums[: D // CHUNK].reshape(D)]
    )

    given = (
        (w_in, w_in_first, w_in_second),
        (w_out, w_out_first, w_out_second),
        (w_shared_gu, w_shared_gu_first, w_shared_gu_second),
        (w_shared_down, w_shared_down_first, w_shared_down_second),
    )
    updated = vmem_call(
        functools.partial(
            update_kernel, inner=inner, own_ff=own_ff, heads=heads
        ),
        [jax.ShapeDtypeStruct(one[0].shape, f32) for one in given for _ in range(4)]
        + [jax.ShapeDtypeStruct((rows_in, LANES), f32)],
        [],
        got_rows, got_sgu, sum_out, sum_sd, *[part for one in given for part in one],
    )
    up_in, up_out, up_sgu, up_sd = (updated[4 * k : 4 * k + 4] for k in range(4))
    up_router = tuple(
        part.T
        for part in adam_step(
            w_router.T, w_router_first.T, w_router_second.T, updated[16].T[:experts]
        )
    )
    up_egu = adam_step(w_expert_gu, w_expert_gu_first, w_expert_gu_second, sum_egu)
    up_ed = adam_step(w_expert_down, w_expert_down_first, w_expert_down_second, sum_ed)
    up_gains = adam_step(norm_gains, norm_gains_first, norm_gains_second, sum_gains)
    up_conv = adam_step(conv_params, conv_params_first, conv_params_second, sum_conv)
    up_head = adam_step(head_params, head_params_first, head_params_second, sum_head)
    up_mixer = adam_step(mixer_gain, mixer_gain_first, mixer_gain_second, sum_mixer)

    large = (up_in, up_out, up_router, up_sgu, up_sd, up_egu, up_ed)
    little = (up_gains, up_conv, up_head, up_mixer)
    return (
        (output, grad_tokens)
        + tuple(part for one in large for part in tuple(one)[:4])
        + tuple(part for one in little for part in (one[0], one[4], one[2], one[3]))
    )


def solution(mesh):
    copies, groups = mesh.devices.shape
    split = Mesh(mesh.devices.reshape(2, copies // 4, 2, groups), ALL)
    rows = P(ALL, None)
    expert_rows = P("expert", DP, None)
    whole = P()
    return jax.shard_map(
        on_device,
        mesh=split,
        in_specs=(rows, rows, P(DP, None), rows)
        + (rows,) * 15
        + (expert_rows,) * 6
        + (whole,) * 12,
        out_specs=(rows, rows) + (rows,) * 20 + (expert_rows,) * 8 + (whole,) * 16,
        check_vma=False,
    )
```
